32 devices in a mesh: rows: 8 (over y, x, core), seq: 4 (over z).
Axes of the slice: x: 2, y: 2, z: 4, core: 2. Of those that a mesh axis runs over, the one named last changes fastest.
Arguments:
- tokens: bfloat16 [96, 512, 384], P('rows', 'seq'), may hold values from -6 to 6
- lengths: int32 [96, 8], P('rows'), may hold values from 1 to 505, as said below
- w_query: bfloat16 [384, 384], replicated, may hold values from -0.3125 to 0.3125
- b_query: float32 [384], replicated, may hold values from -3 to 3
- w_key: bfloat16 [384, 384], replicated, may hold values from -0.3125 to 0.3125
- w_value: bfloat16 [384, 384], replicated, may hold values from -0.3125 to 0.3125
- b_value: float32 [384], replicated, may hold values from -3 to 3
- w_out: bfloat16 [384, 384], replicated, may hold values from -3.5 to 3.5
- b_out: float32 [384], replicated, may hold values from -3 to 3
- gain_attn: float32 [384], replicated, may hold values from 0.5 to 1.5
- shift_attn: float32 [384], replicated, may hold values from -3 to 3
- w_up: bfloat16 [384, 1536], replicated, may hold values from -0.3125 to 0.3125
- b_up: float32 [1536], replicated, may hold values from -3 to 3
- w_down: bfloat16 [1536, 384], replicated, may hold values from -0.15625 to 0.15625
- b_down: float32 [384], replicated, may hold values from -3 to 3
- gain_ffn: float32 [384], replicated, may hold values from 0.5 to 1.5
- shift_ffn: float32 [384], replicated, may hold values from -3 to 3
- cotangent: bfloat16 [96, 512, 384], P('rows', 'seq'), may hold values from -6 to 6
Outputs:
- layer_out: bfloat16 [96, 512, 384], P('rows', 'seq')
- grad_tokens: float32 [96, 512, 384], P('rows', 'seq')
- grad_query: float32 [384, 384], replicated
- grad_qbias: float32 [384], replicated
- grad_key: float32 [384, 384], replicated
- grad_value: float32 [384, 384], replicated
- grad_vbias: float32 [384], replicated
- grad_output: float32 [384, 384], replicated
- grad_obias: float32 [384], replicated
- grad_gain1: float32 [384], replicated
- grad_shift1: float32 [384], replicated
- grad_up: float32 [384, 1536], replicated
- grad_upbias: float32 [1536], replicated
- grad_down: float32 [1536, 384], replicated
- grad_dnbias: float32 [384], replicated
- grad_gain2: float32 [384], replicated
- grad_shift2: float32 [384], replicated
The draws below stay inside these ranges and needn't reach their ends.
Inputs may be any that keep to these rules, and one draw needn't show every extreme that they name: Each row's 8 lengths sum to 512; in every row one pair starts within the first 128 positions and ends within the last 128.
All inputs are finite; a program needn't handle non-finite values.
Results may differ from the reference program's by a relative error of at most 0.014.
Values may be sent and summed in bfloat16 or wider, within the bound.
No kernel may reach another device: no remote copies, remote signals or barrier semaphores. Data moves between devices by JAX's collectives and lax.ppermute only.
A program may use at most 192 MiB of HBM per device.

```python
import math
import jax
import jax.numpy as jnp
from jax import lax

HEADS = 12
HD = 32
FF = 1536
LENGTH = 512
SEGS = 8
D = 384
SEQ_DEV = 128
ROWS = 96


def draw_lengths(key, part):
    key = jax.random.fold_in(key, 11)
    short_key, place_key, pick_key = jax.random.split(key, 3)
    shorts = jax.random.randint(short_key, (ROWS, SEGS - 1), 1, SEQ_DEV // 8 + 1).astype(jnp.int32)
    chosen = jax.random.randint(pick_key, (), 0, ROWS).astype(jnp.int32)
    row_ids = jnp.arange(ROWS, dtype=jnp.int32)[:, None]
    shorts = jnp.where(row_ids == chosen, jnp.ones_like(shorts), shorts)
    longest = LENGTH - jnp.sum(shorts, axis=1)
    placed = jax.random.randint(place_key, (ROWS, 1), 0, SEGS).astype(jnp.int32)
    slots = jnp.arange(SEGS, dtype=jnp.int32)[None, :]
    source = jnp.clip(jnp.where(slots < placed, slots, slots - 1), 0, SEGS - 2)
    picked = jnp.take_along_axis(shorts, source, axis=1)
    return jnp.where(slots == placed, longest[:, None], picked).astype(jnp.int32)


def block_scale(key, shape, cuts, smallest, largest):
    gain = 1.0
    for position, shards_of in cuts:
        draws = jax.random.uniform(jax.random.fold_in(jax.random.fold_in(key, 6), position), (shards_of,), jnp.float32, smallest / len(cuts), largest / len(cuts))
        gain = gain * jnp.repeat(jnp.exp(draws), shape[position] // shards_of).reshape((-1,) + (1,) * (len(shape) - 1 - position))
    return gain


def bell_draw(rng, shape, spread, bound, shards=(), kind=jnp.bfloat16):
    entries = jax.random.normal(rng, shape, jnp.float32) * spread
    if len(shards) > 0:
        entries = block_scale(rng, shape, shards, -0.22, 0.18) * entries
    return jnp.clip(entries, min=-bound, max=bound).astype(kind)


def setup_inputs(seed: int = 0) -> dict:
    arg_keys = jax.random.split(jax.random.key(seed), 19)
    tokens = bell_draw(arg_keys[0], (ROWS, LENGTH, D), 1.0, 6.0, ((0, 8), (1, 4)))
    lengths = draw_lengths(jax.random.fold_in(arg_keys[18], 71), 0)
    w_query = bell_draw(arg_keys[2], (D, D), D ** -0.5, 0.3125)
    b_query = bell_draw(arg_keys[3], (D,), 0.5, 3.0, (), jnp.float32)
    w_key = bell_draw(arg_keys[4], (D, D), D ** -0.5, 0.3125)
    w_value = bell_draw(arg_keys[5], (D, D), D ** -0.5, 0.3125)
    b_value = bell_draw(arg_keys[6], (D,), 0.5, 3.0, (), jnp.float32)
    w_out = bell_draw(arg_keys[7], (D, D), (max(1, D // 128)) ** -0.5, 3.5)
    b_out = bell_draw(arg_keys[8], (D,), 0.5, 3.0, (), jnp.float32)
    gain_attn = jnp.clip(1.0 + 0.1 * jax.random.normal(arg_keys[9], (D,), jnp.float32), 0.5, 1.5)
    shift_attn = bell_draw(arg_keys[10], (D,), 0.5, 3.0, (), jnp.float32)
    w_up = bell_draw(arg_keys[11], (D, FF), D ** -0.5, 0.3125)
    b_up = bell_draw(arg_keys[12], (FF,), 0.5, 3.0, (), jnp.float32)
    w_down = bell_draw(arg_keys[13], (FF, D), FF ** -0.5, 0.15625)
    b_down = bell_draw(arg_keys[14], (D,), 0.5, 3.0, (), jnp.float32)
    gain_ffn = jnp.clip(1.0 + 0.1 * jax.random.normal(arg_keys[15], (D,), jnp.float32), 0.5, 1.5)
    shift_ffn = bell_draw(arg_keys[16], (D,), 0.5, 3.0, (), jnp.float32)
    cotangent = bell_draw(arg_keys[17], (ROWS, LENGTH, D), 1.0, 6.0, ((0, 8), (1, 4)))
    return {"tokens": tokens, "lengths": lengths, "w_query": w_query, "b_query": b_query, "w_key": w_key, "w_value": w_value, "b_value": b_value, "w_out": w_out, "b_out": b_out, "gain_attn": gain_attn, "shift_attn": shift_attn, "w_up": w_up, "b_up": b_up, "w_down": w_down, "b_down": b_down, "gain_ffn": gain_ffn, "shift_ffn": shift_ffn, "cotangent": cotangent}


@jax.custom_vjp
def low(v):
    return lax.optimization_barrier(v.astype(jnp.bfloat16)).astype(jnp.float32)

@jax.custom_vjp
def low_back(v):
    return v

def low_keep(v):
    return (low(v), None)

def low_pass(kept, grad):
    return (grad,)

def back_keep(v):
    return (v, None)

def back_low(kept, grad):
    return (low(grad),)
low.defvjp(low_keep, low_pass)
low_back.defvjp(back_keep, back_low)
MASKED = -1e+30
EPSILON = 1e-05
HIGHEST = lax.Precision.HIGHEST

def both_ways(value):
    return low(low_back(value))

def matmul(operand, weight):
    return jnp.einsum('gld,de->gle', operand, weight, precision=HIGHEST)

def normalize(hidden):
    centre = hidden - lax.optimization_barrier(jnp.mean(hidden, axis=-1, keepdims=True))
    return centre * lax.rsqrt(lax.optimization_barrier(jnp.mean(centre * centre, axis=-1, keepdims=True)) + EPSILON)

def forward(tokens, segment, params):
    w_query, b_query, w_key, w_value, b_value, w_out, b_out, gain_attn, shift_attn, w_up, b_up, w_down, b_down, gain_ffn, shift_ffn = params
    groups = tokens.shape[0]
    length = tokens.shape[1]
    width = tokens.shape[2]
    query = both_ways(matmul(tokens, w_query) + b_query).reshape(groups, length, HEADS, HD)
    keys = both_ways(matmul(tokens, w_key)).reshape(groups, length, HEADS, HD)
    values = both_ways(matmul(tokens, w_value) + b_value).reshape(groups, length, HEADS, HD)
    logits = jnp.einsum('gqhd,gkhd->ghqk', query, keys, precision=HIGHEST) * HD ** (-0.5)
    matching = segment[:, None, :, None] == segment[:, None, None, :]
    logits = low_back(jnp.where(matching, logits, MASKED))
    shifted = jnp.exp(logits - lax.optimization_barrier(jnp.max(logits, axis=-1, keepdims=True)))
    weights = low(shifted / lax.optimization_barrier(jnp.sum(shifted, axis=-1, keepdims=True)))
    mixed = jnp.einsum('ghqk,gkhd->gqhd', weights, values, precision=HIGHEST)
    attended = both_ways(mixed.reshape(groups, length, width))
    residual = tokens + low_back(matmul(attended, w_out) + b_out)
    normed = normalize(residual) * gain_attn + shift_attn
    upward = low_back(matmul(low(normed), w_up) + b_up)
    activated = low(jax.nn.gelu(upward, approximate=False))
    second = normed + low_back(matmul(activated, w_down) + b_down)
    return normalize(second) * gain_ffn + shift_ffn

def reference(tokens, lengths, w_query, b_query, w_key, w_value, b_value, w_out, b_out, gain_attn, shift_attn, w_up, b_up, w_down, b_down, gain_ffn, shift_ffn, cotangent):
    bounds = jnp.cumsum(lengths, axis=1)
    places = jnp.arange(LENGTH, dtype=jnp.int32)
    segment = lax.optimization_barrier(jnp.sum((places[None, :, None] >= bounds[:, None, :]).astype(jnp.int32), axis=-1))
    params = tuple((member.astype(jnp.float32) for member in (w_query, b_query, w_key, w_value, b_value, w_out, b_out, gain_attn, shift_attn, w_up, b_up, w_down, b_down, gain_ffn, shift_ffn)))
    per_step = math.gcd(ROWS, 8)
    steps_count = ROWS // per_step
    inputs = tokens.astype(jnp.float32).reshape(steps_count, per_step, LENGTH, D)
    segments = segment.reshape(steps_count, per_step, LENGTH)
    upstream = cotangent.astype(jnp.float32).reshape(steps_count, per_step, LENGTH, D)

    def advance(summed, packed):
        block_tokens, block_segment, block_upstream = packed
        result, pull = jax.vjp(lambda left, right: forward(left, block_segment, right), block_tokens, params)
        grad_block, grad_params = pull(block_upstream)
        summed = jax.tree.map(jnp.add, summed, grad_params)
        return (summed, (result.astype(jnp.bfloat16), grad_block))
    zeroed = jax.tree.map(jnp.zeros_like, params)
    summed, (outputs, grad_inputs) = lax.scan(advance, zeroed, (inputs, segments, upstream))
    return (outputs.reshape(ROWS, LENGTH, D), grad_inputs.reshape(ROWS, LENGTH, D), summed[0], summed[1], summed[2], summed[3], summed[4], summed[5], summed[6], summed[7], summed[8], summed[9], summed[10], summed[11], summed[12], summed[13], summed[14])
```

```python
import functools
import math

import jax
import jax.numpy as jnp
from jax import lax
from jax.experimental import pallas as pl
from jax.experimental.pallas import tpu as pltpu
from jax.sharding import PartitionSpec as P

HEADS = 12
HD = 32
GROUPS = 3
PER_GROUP = HEADS // GROUPS
AUG = 16
BIG = 2.0**100
EPSILON = 1e-05
SCALE = HD ** (-0.5)
LOG2E = math.log2(math.e)
Q_FACTOR = SCALE * LOG2E
LN2 = math.log(2.0)
VMEM_LIMIT = 60 * 2**20

f32 = jnp.float32
bf16 = jnp.bfloat16
NN = (((1,), (0,)), ((), ()))
NT = (((1,), (1,)), ((), ()))
TN = (((0,), (0,)), ((), ()))


def dot(left, right, dims=NN):
    return lax.dot_general(left, right, dims, preferred_element_type=f32)


def fold_lanes(values):
    total = values[:, :128]
    for start in range(128, values.shape[1], 128):
        total = total + values[:, start : start + 128]
    return total


def row_sum(partial):
    return jnp.sum(partial.T, axis=0, keepdims=True)


def normalize(hidden):
    scale = 1.0 / hidden.shape[0]
    centre = hidden - jnp.sum(hidden, axis=0, keepdims=True) * scale
    variance = jnp.sum(centre * centre, axis=0, keepdims=True) * scale
    inverse = lax.rsqrt(variance + EPSILON)
    return centre * inverse, inverse


def normalize_back(upstream, scaled, inverse):
    scale = 1.0 / upstream.shape[0]
    mean = jnp.sum(upstream, axis=0, keepdims=True) * scale
    spread = jnp.sum(upstream * scaled, axis=0, keepdims=True) * scale
    return inverse * (upstream - mean - scaled * spread)


def gelu_parts(v):
    size = jnp.abs(v)
    t = 1.0 / (1.0 + (0.3275911 * 0.5**0.5) * size)
    bell = jnp.exp2((v * v) * (-0.5 * LOG2E))
    poly = 0.5 * 1.061405429
    for coefficient in (-1.453152027, 1.421413741, -0.284496736, 0.254829592):
        poly = poly * t + 0.5 * coefficient
    tail = poly * t * bell
    cdf = jnp.where(v < 0, tail, 1.0 - tail)
    slope = cdf + v * bell * (2.0 * math.pi) ** (-0.5)
    return v * cdf, slope


def attend_kernel(
    *refs, pieces, row_base
):
    x_refs = refs[:pieces]
    qaug_ref, kaug_ref, wq_ref, wk_ref, wv_ref, bq_ref, bv_ref = refs[pieces : pieces + 7]
    xt_ref, qt_ref, kt_ref, vt_ref, att_ref, inv_ref, p_ref = refs[pieces + 7 :]
    group = pl.program_id(1)

    @pl.when(group == 0)
    def _():
        xt = jnp.concatenate([ref[0].T for ref in x_refs], axis=1)
        xt_ref[0] = xt
        qt_ref[0] = ((dot(wq_ref[...], xt) + bq_ref[...]) * Q_FACTOR).astype(bf16)
        kt_ref[0] = dot(wk_ref[...], xt).astype(bf16)
        vt_ref[0] = (dot(wv_ref[...], xt) + bv_ref[...]).astype(bf16)

    length = xt_ref.shape[2]
    half = min(256, length)
    ones = jnp.ones((AUG, length), bf16)
    units = [(h, start) for h in range(PER_GROUP) for start in range(0, length, half)]
    keys, values = {}, {}

    def rows(ref, h):
        return ref[0, pl.ds(pl.multiple_of((group * PER_GROUP + h) * HD, HD), HD), :]

    def score(unit):
        h, start = unit
        if h not in keys:
            keys[h] = jnp.concatenate([rows(kt_ref, h), kaug_ref[0]], axis=0)
        query = jnp.concatenate([rows(qt_ref, h), qaug_ref[0]], axis=0)
        return dot(keys[h], query[:, start : start + half], TN)

    scores = score(units[0])
    for index, (h, start) in enumerate(units):
        following = score(units[index + 1]) if index + 1 < len(units) else None
        peak = jnp.max(scores, axis=0, keepdims=True)
        probs = jnp.exp2(scores - peak).astype(bf16)
        p_ref[0, h, :, start : start + half] = probs
        if h not in values:
            values[h] = jnp.concatenate([rows(vt_ref, h), ones], axis=0)
        mixed = dot(values[h], probs)
        inverse = 1.0 / mixed[HD : HD + 1]
        att_ref[0, pl.ds(pl.multiple_of((group * PER_GROUP + h) * HD, HD), HD), start : start + half] = (
            mixed[:HD] * inverse
        )
        inv_ref[0, 0, h : h + 1, start : start + half] = inverse
        scores = following


def attend(pieces, qaug, kaug, weights):
    rows, span, width = pieces[0].shape
    count = len(pieces)
    length = span * count
    wq, wk, wv, bq, bv = weights
    piece_spec = pl.BlockSpec((1, span, width), lambda r, g: (r, 0, 0))
    aug_spec = pl.BlockSpec((1, AUG, length), lambda r, g: (r, 0, 0))
    full = lambda a: pl.BlockSpec(a.shape, lambda r, g: (0, 0))
    wide = pl.BlockSpec((1, width, length), lambda r, g: (r, 0, 0))
    return pl.pallas_call(
        functools.partial(attend_kernel, pieces=count, row_base=0),
        grid=(rows, GROUPS),
        in_specs=[piece_spec] * count + [aug_spec] * 2 + [full(w) for w in weights],
        out_specs=[wide] * 5
        + [
            pl.BlockSpec((1, 1, 8, length), lambda r, g: (r, g, 0, 0)),
            pl.BlockSpec((1, PER_GROUP, length, length), lambda r, g: (r, g, 0, 0)),
        ],
        out_shape=[jax.ShapeDtypeStruct((rows, width, length), bf16)] * 4
        + [
            jax.ShapeDtypeStruct((rows, width, length), f32),
            jax.ShapeDtypeStruct((rows, GROUPS, 8, length), f32),
            jax.ShapeDtypeStruct((rows, HEADS, length, length), bf16),
        ],
        compiler_params=pltpu.CompilerParams(vmem_limit_bytes=VMEM_LIMIT),
        name="attend",
    )(*pieces, qaug, kaug, *weights)


def dense_kernel(*refs, pieces, rows):
    cot_refs = refs[:pieces]
    (
        xt_ref, att_ref, inv_ref, wo_t, wo, wup_t, wup, wdn_t, wdn, bo, gain1, shift1, bup, bdn, gain2, shift2,
    ) = refs[pieces : pieces + 16]
    lo_refs = refs[pieces + 16 : 2 * pieces + 16]
    gres_ref, og_ref, delta_ref, packed_ref = refs[2 * pieces + 16 : 2 * pieces + 20]
    acc_dn, acc_up, acc_out, acc_bias, acc_upb = refs[2 * pieces + 20 :]
    step = pl.program_id(0)
    span = cot_refs[0].shape[1]
    width = xt_ref.shape[1]

    @pl.when(step == 0)
    def _():
        for ref in (acc_dn, acc_up, acc_out, acc_bias, acc_upb):
            ref[...] = jnp.zeros_like(ref)

    att = att_ref[0]
    att_b = att.astype(bf16)
    res1 = xt_ref[0].astype(f32) + dot(wo_t[...], att_b) + bo[...]
    scaled1, inverse1 = normalize(res1)
    normed = scaled1 * gain1[...] + shift1[...]
    normed_b = normed.astype(bf16)
    upward = dot(wup_t[...], normed_b) + bup[...]
    act, slope = gelu_parts(upward)
    act_b = act.astype(bf16)
    res2 = normed + dot(wdn_t[...], act_b) + bdn[...]
    scaled2, inverse2 = normalize(res2)
    out = (scaled2 * gain2[...] + shift2[...]).astype(bf16)
    for index, ref in enumerate(lo_refs):
        ref[0] = out[:, index * span : (index + 1) * span].T
    cot = jnp.concatenate([ref[0].T for ref in cot_refs], axis=1).astype(f32)
    acc_bias[0] += fold_lanes(cot * scaled2)
    acc_bias[1] += fold_lanes(cot)
    gres2 = normalize_back(cot * gain2[...], scaled2, inverse2)
    down_b = gres2.astype(bf16)
    acc_bias[2] += fold_lanes(down_b.astype(f32))
    acc_dn[...] += dot(act_b, down_b, NT)
    up_b = (dot(wdn[...], down_b) * slope).astype(bf16)
    acc_upb[...] += fold_lanes(up_b.astype(f32))
    acc_up[...] += dot(normed_b, up_b, NT)
    gnormed = gres2 + dot(wup[...], up_b)
    acc_bias[3] += fold_lanes(gnormed * scaled1)
    acc_bias[4] += fold_lanes(gnormed)
    gres1 = normalize_back(gnormed * gain1[...], scaled1, inverse1)
    gres_ref[0] = gres1
    branch_b = gres1.astype(bf16)
    acc_bias[5] += fold_lanes(branch_b.astype(f32))
    acc_out[...] += dot(att_b, branch_b, NT)
    og = dot(wo[...], branch_b)
    for h in range(HEADS):
        part = slice(h * HD, (h + 1) * HD)
        scaled_og = (og[part] * inv_ref[0, h // PER_GROUP, h % PER_GROUP : h % PER_GROUP + 1, :]).astype(bf16)
        og_ref[0, part, :] = scaled_og
        delta_ref[0, h : h + 1, :] = jnp.sum(scaled_og.astype(f32) * att[part], axis=0, keepdims=True)

    @pl.when(step == rows - 1)
    def _():
        ff = acc_up.shape[1]
        packed_ref[:ff] = acc_dn[...].astype(bf16)
        for index in range(ff // width):
            packed_ref[ff + index * width : ff + (index + 1) * width] = acc_up[
                :, index * width : (index + 1) * width
            ].astype(bf16)
        packed_ref[2 * ff : 2 * ff + width] = acc_out[...].astype(bf16)
        bias_rows = [row_sum(acc_bias[i]) for i in range(6)]
        bias_rows += [row_sum(acc_upb[i * width : (i + 1) * width]) for i in range(ff // width)]
        tail = packed_ref.shape[0] - 2 * ff - width
        bias_rows.append(jnp.zeros((tail - len(bias_rows), width), f32))
        packed_ref[2 * ff + width :] = jnp.concatenate(bias_rows, axis=0).astype(bf16)


def dense(pieces, xt, att, inv, weights, packed_rows):
    rows, span, width = pieces[0].shape
    count = len(pieces)
    length = span * count
    ff = weights[2].shape[0]
    piece_spec = pl.BlockSpec((1, span, width), lambda r: (r, 0, 0))
    wide = pl.BlockSpec((1, width, length), lambda r: (r, 0, 0))
    full = lambda a: pl.BlockSpec(a.shape, lambda r: (0, 0))
    return pl.pallas_call(
        functools.partial(dense_kernel, pieces=count, rows=rows),
        grid=(rows,),
        in_specs=[piece_spec] * count
        + [wide, wide, pl.BlockSpec((1, GROUPS, 8, length), lambda r: (r, 0, 0, 0))]
        + [full(w) for w in weights],
        out_specs=[piece_spec] * count
        + [
            wide,
            wide,
            pl.BlockSpec((1, 16, length), lambda r: (r, 0, 0)),
            pl.BlockSpec((packed_rows, width), lambda r: (0, 0)),
        ],
        out_shape=[jax.ShapeDtypeStruct((rows, span, width), bf16)] * count
        + [
            jax.ShapeDtypeStruct((rows, width, length), f32),
            jax.ShapeDtypeStruct((rows, width, length), bf16),
            jax.ShapeDtypeStruct((rows, 16, length), f32),
            jax.ShapeDtypeStruct((packed_rows, width), bf16),
        ],
        scratch_shapes=[
            pltpu.VMEM((ff, width), f32),
            pltpu.VMEM((width, ff), f32),
            pltpu.VMEM((width, width), f32),
            pltpu.VMEM((6, width, 128), f32),
            pltpu.VMEM((ff, 128), f32),
        ],
        compiler_params=pltpu.CompilerParams(vmem_limit_bytes=VMEM_LIMIT),
        name="dense",
    )(*pieces, xt, att, inv, *weights)


def back_kernel(*refs, pieces, rows):
    xt_ref, qt_ref, kt_ref, vt_ref, og_ref, delta_ref, p_ref, gres_ref, w_ref = refs[:9]
    out_refs = refs[9 : 9 + pieces]
    packed_ref = refs[9 + pieces]
    grads, acc_w, acc_bias = refs[10 + pieces :]
    row = pl.program_id(0)
    group = pl.program_id(1)
    length = xt_ref.shape[2]
    width = xt_ref.shape[1]
    span = out_refs[0].shape[1]

    @pl.when((row == 0) & (group == 0))
    def _():
        acc_w[...] = jnp.zeros_like(acc_w)
        acc_bias[...] = jnp.zeros_like(acc_bias)

    def start_of(h):
        return pl.multiple_of((group * PER_GROUP + h) * HD, HD)

    def rows_of(ref, h):
        return ref[0, pl.ds(start_of(h), HD), :]

    sign = jnp.where(lax.broadcasted_iota(jnp.int32, (AUG, length), 0) < 3, 1.0, 0.0).astype(bf16)

    def grad_probs(h):
        delta = delta_ref[0, pl.ds(group * PER_GROUP + h, 1), :]
        first = delta.astype(bf16)
        rest = delta - first.astype(f32)
        second = rest.astype(bf16)
        third = (rest - second.astype(f32)).astype(bf16)
        aug = jnp.concatenate(
            [-first.astype(f32), -second.astype(f32), -third.astype(f32), jnp.zeros((AUG - 3, length), f32)], axis=0
        ).astype(bf16)
        left = jnp.concatenate([rows_of(vt_ref, h), sign], axis=0)
        right = jnp.concatenate([rows_of(og_ref, h), aug], axis=0)
        return dot(left, right, TN)

    upstream = grad_probs(0)
    for h in range(PER_GROUP):
        following = grad_probs(h + 1) if h + 1 < PER_GROUP else None
        probs = p_ref[0, h]
        grad_logits = (probs.astype(f32) * upstream).astype(bf16)
        start = start_of(h)
        grads[pl.ds(start, HD), :] = (dot(rows_of(kt_ref, h), grad_logits) * SCALE).astype(bf16)
        grads[pl.ds(width + start, HD), :] = (dot(rows_of(qt_ref, h), grad_logits, NT) * LN2).astype(bf16)
        grads[pl.ds(2 * width + start, HD), :] = dot(rows_of(og_ref, h), probs, NT).astype(bf16)
        upstream = following

    @pl.when(group == GROUPS - 1)
    def _():
        total = grads[...]
        acc_w[...] += dot(xt_ref[0], total, NT)
        acc_bias[0] += fold_lanes(total[:width].astype(f32))
        acc_bias[1] += fold_lanes(total[2 * width :].astype(f32))
        result = (gres_ref[0] + dot(w_ref[...], total)).astype(bf16)
        for index, ref in enumerate(out_refs):
            ref[0] = result[:, index * span : (index + 1) * span].T

    @pl.when((row == rows - 1) & (group == GROUPS - 1))
    def _():
        for index in range(3):
            packed_ref[index * width : (index + 1) * width] = acc_w[
                :, index * width : (index + 1) * width
            ].astype(bf16)
        bias_rows = [row_sum(acc_bias[i]) for i in range(2)]
        tail = packed_ref.shape[0] - 3 * width
        bias_rows.append(jnp.zeros((tail - len(bias_rows), width), f32))
        packed_ref[3 * width :] = jnp.concatenate(bias_rows, axis=0).astype(bf16)


def back(count, xt, qt, kt, vt, og, delta, probs, gres, w_all, packed_rows):
    rows, width, length = xt.shape
    span = length // count
    wide = pl.BlockSpec((1, width, length), lambda r, g: (r, 0, 0))
    return pl.pallas_call(
        functools.partial(back_kernel, pieces=count, rows=rows),
        grid=(rows, GROUPS),
        in_specs=[wide] * 5
        + [
            pl.BlockSpec((1, 16, length), lambda r, g: (r, 0, 0)),
            pl.BlockSpec((1, PER_GROUP, length, length), lambda r, g: (r, g, 0, 0)),
            wide,
            pl.BlockSpec(w_all.shape, lambda r, g: (0, 0)),
        ],
        out_specs=[pl.BlockSpec((1, span, width), lambda r, g: (r, 0, 0))] * count
        + [pl.BlockSpec((packed_rows, width), lambda r, g: (0, 0))],
        out_shape=[jax.ShapeDtypeStruct((rows, span, width), bf16)] * count
        + [jax.ShapeDtypeStruct((packed_rows, width), bf16)],
        scratch_shapes=[
            pltpu.VMEM((3 * width, length), bf16),
            pltpu.VMEM((width, 3 * width), f32),
            pltpu.VMEM((2, width, 128), f32),
        ],
        compiler_params=pltpu.CompilerParams(vmem_limit_bytes=VMEM_LIMIT),
        name="back",
    )(xt, qt, kt, vt, og, delta, probs, gres, w_all)


def exchange(pieces, axis):
    count = len(pieces)
    moved = [pieces[0]]
    for shift in range(1, count):
        moved.append(lax.ppermute(pieces[shift], axis, [(i, i ^ shift) for i in range(count)]))
    return moved


def halve(block, axis, bit, size):
    rows = block.shape[0] // 2
    side = (lax.axis_index(axis) // bit) % 2
    kept = lax.dynamic_slice_in_dim(block, side * rows, rows, 0)
    given = lax.dynamic_slice_in_dim(block, (1 - side) * rows, rows, 0)
    taken = lax.ppermute(given, axis, [(i, i ^ bit) for i in range(size)])
    return (kept.astype(f32) + taken.astype(f32)).astype(bf16)


def double(block, axis, bit, size):
    side = (lax.axis_index(axis) // bit) % 2
    taken = lax.ppermute(block, axis, [(i, i ^ bit) for i in range(size)])
    first = jnp.where(side == 0, block, taken)
    second = jnp.where(side == 0, taken, block)
    return jnp.concatenate([first, second], axis=0)


def sum_all(packed, axes):
    steps = []
    for axis, size in axes:
        bit = 1
        while bit < size:
            steps.append((axis, bit, size))
            bit *= 2
    for step in steps:
        packed = halve(packed, *step)
    for step in reversed(steps):
        packed = double(packed, *step)
    return packed


def round_up(value, unit):
    return -(-value // unit) * unit


def body(
    tokens, lengths, w_query, b_query, w_key, w_value, b_value, w_out, b_out, gain_attn, shift_attn,
    w_up, b_up, w_down, b_down, gain_ffn, shift_ffn, cotangent, *, sizes,
):
    count = sizes["seq"]
    devices = count * sizes["rows"]
    row_count, span, width = tokens.shape
    ff = w_up.shape[1]
    length = span * count
    rows = row_count // count
    me = lax.axis_index("seq")
    order = me ^ jnp.arange(count, dtype=jnp.int32)

    def column(vector):
        return vector.reshape(-1, 1)

    def spread(array):
        return jnp.take(array.reshape(count, rows, span, width), order, axis=0)

    token_parts = spread(tokens)
    cot_parts = spread(cotangent)
    token_rows = [exchange([token_parts[s, j : j + 1] for s in range(count)], "seq") for j in range(rows)]
    cot_moved = exchange([cot_parts[s] for s in range(count)], "seq")

    bounds = lax.dynamic_slice_in_dim(jnp.cumsum(lengths, axis=1), me * rows, rows, 0)
    places = (order[:, None] * span + jnp.arange(span, dtype=jnp.int32)[None, :]).reshape(length)
    segment = jnp.sum((places[None, None, :] >= bounds[:, :, None]).astype(jnp.int32), axis=1)
    ids = jnp.arange(AUG, dtype=jnp.int32)[None, :, None]
    same = segment[:, None, :] == ids
    qaug = same.astype(bf16)
    kaug = jnp.where(same | (ids >= lengths.shape[1]), 0.0, -BIG).astype(bf16)

    attend_weights = (w_query.T, w_key.T, w_value.T, column(b_query), column(b_value))
    dense_weights = (
        w_out.T, w_out, w_up.T, w_up, w_down.T, w_down, column(b_out), column(gain_attn), column(shift_attn),
        column(b_up), column(b_down), column(gain_ffn), column(shift_ffn),
    )
    first = [attend(token_rows[j], qaug[j : j + 1], kaug[j : j + 1], attend_weights) for j in range(rows)]
    xt, att, inv = [jnp.concatenate([f[i] for f in first], axis=0) for i in (0, 4, 5)]
    later_rows = round_up(2 * ff + width + 16, 16 * devices)
    dense_out = dense(cot_moved, xt, att, inv, dense_weights, later_rows)
    lo_moved = exchange(dense_out[:count], "seq")
    gres, og, delta, later = dense_out[count:]
    axes = [("rows", sizes["rows"]), ("seq", count)]
    later = sum_all(later, axes)
    w_all = jnp.concatenate([w_query, w_key, w_value], axis=1)
    first_rows = round_up(3 * width + 16, 16 * devices)
    qt, kt, vt, probs = [jnp.concatenate([f[i] for f in first], axis=0) for i in (1, 2, 3, 6)]
    back_out = back(count, xt, qt, kt, vt, og, delta, probs, gres, w_all, first_rows)
    grad_moved = exchange(back_out[:count], "seq")
    early = sum_all(back_out[count], axes)

    def place(moved, dtype):
        whole = jnp.zeros((count, rows, span, width), dtype)
        for shift in range(count):
            whole = lax.dynamic_update_slice(whole, moved[shift][None].astype(dtype), (me ^ shift, 0, 0, 0))
        return whole.reshape(row_count, span, width)

    layer_out = place(lo_moved, bf16)
    grad_tokens = place(grad_moved, f32)
    early = early.astype(f32)
    grad_query, grad_key, grad_value = [early[i * width : (i + 1) * width] for i in range(3)]
    grad_qbias, grad_vbias = early[3 * width], early[3 * width + 1]
    later = later.astype(f32)
    grad_down = later[:ff]
    grad_up = jnp.concatenate([later[ff + i * width : ff + (i + 1) * width] for i in range(ff // width)], axis=1)
    grad_output = later[2 * ff : 2 * ff + width]
    biases = later[2 * ff + width : 2 * ff + width + 6 + ff // width]
    grad_gain2, grad_shift2, grad_dnbias, grad_gain1, grad_shift1, grad_obias = [biases[i] for i in range(6)]
    grad_upbias = biases[6:].reshape(ff)
    return (
        layer_out, grad_tokens, grad_query, grad_qbias, grad_key, grad_value, grad_vbias, grad_output, grad_obias,
        grad_gain1, grad_shift1, grad_up, grad_upbias, grad_down, grad_dnbias, grad_gain2, grad_shift2,
    )


def solution(mesh):
    split = P("rows", "seq", None)
    in_specs = (split, P("rows", None)) + (P(),) * 15 + (split,)
    out_specs = (split, split) + (P(),) * 15
    sizes = dict(mesh.shape)
    return jax.shard_map(
        functools.partial(body, sizes=sizes), mesh=mesh, in_specs=in_specs, out_specs=out_specs, check_vma=False
    )
```

```python
import functools
import math

import jax
import jax.numpy as jnp
from jax import lax
from jax.experimental import pallas as pl
from jax.experimental.pallas import tpu as pltpu
from jax.sharding import PartitionSpec as P

HEADS = 12
HD = 32
GROUPS = 3
PER_GROUP = HEADS // GROUPS
AUG = 16
BIG = 2.0**100
SMALL_SCORE = 60.0
EPSILON = 1e-05
SCALE = HD ** (-0.5)
LOG2E = math.log2(math.e)
Q_FACTOR = SCALE * LOG2E
LN2 = math.log(2.0)
VMEM_LIMIT = 60 * 2**20

f32 = jnp.float32
bf16 = jnp.bfloat16
NN = (((1,), (0,)), ((), ()))
NT = (((1,), (1,)), ((), ()))
TN = (((0,), (0,)), ((), ()))


def dot(left, right, dims=NN):
    return lax.dot_general(left, right, dims, preferred_element_type=f32)


def fold_lanes(values):
    total = values[:, :128]
    for start in range(128, values.shape[1], 128):
        total = total + values[:, start : start + 128]
    return total


def row_sum(partial):
    return jnp.sum(partial.T, axis=0, keepdims=True)


def normalize(hidden):
    scale = 1.0 / hidden.shape[0]
    centre = hidden - jnp.sum(hidden, axis=0, keepdims=True) * scale
    variance = jnp.sum(centre * centre, axis=0, keepdims=True) * scale
    inverse = lax.rsqrt(variance + EPSILON)
    return centre * inverse, inverse


def normalize_back(upstream, scaled, inverse):
    scale = 1.0 / upstream.shape[0]
    mean = jnp.sum(upstream, axis=0, keepdims=True) * scale
    spread = jnp.sum(upstream * scaled, axis=0, keepdims=True) * scale
    return inverse * (upstream - mean - scaled * spread)


def gelu_parts(v):
    cdf = 0.5 + 0.5 * lax.erf(v * 0.5**0.5)
    bell = jnp.exp2((v * v) * (-0.5 * LOG2E))
    return v * cdf, cdf + v * bell * (2.0 * math.pi) ** (-0.5)


def prepare_kernel(wq, wk, wv, wo, wup, wdn, rows, wq_t, wk_t, wv_t, wo_t, wup_t, wdn_t, columns):
    for source, target in ((wq, wq_t), (wk, wk_t), (wv, wv_t), (wo, wo_t), (wup, wup_t), (wdn, wdn_t)):
        target[...] = source[...].T
    width = rows.shape[1]
    columns[...] = jnp.concatenate([rows[...], jnp.zeros((128 - rows.shape[0], width), f32)], axis=0).T


def prepare(weights, rows):
    shapes = [jax.ShapeDtypeStruct(w.shape[::-1], w.dtype) for w in weights]
    shapes.append(jax.ShapeDtypeStruct((rows.shape[1], 128), f32))
    return pl.pallas_call(
        prepare_kernel,
        out_shape=shapes,
        compiler_params=pltpu.CompilerParams(vmem_limit_bytes=VMEM_LIMIT),
        cost_estimate=cost(5),
        name="prepare",
    )(*weights, rows)


def cost(micros):
    return pl.CostEstimate(flops=int(micros * 5e8), transcendentals=0, bytes_accessed=int(micros * 2e6))


B_QUERY, B_VALUE, B_OUT, GAIN1, SHIFT1, B_DOWN, GAIN2, SHIFT2, B_UP = range(9)


def forward_kernel(*refs, pieces, carried):
    x_refs = refs[:pieces]
    aug_ref, cols, wq, wk, wv, wo, wup, wdn = refs[pieces : pieces + 8]
    outs = refs[pieces + 8 + carried :]
    lo_refs = outs[:pieces]
    (
        xt_ref, qt_ref, kt_ref, vt_ref, p_ref, att_ref, s1_ref, s2_ref, stat_ref, act_ref, slope_ref, small_ref,
    ) = outs[pieces:]
    group = pl.program_id(1)
    span = x_refs[0].shape[1]

    def column(index):
        return cols[:, index : index + 1]

    @pl.when(group == 0)
    def _():
        xt = jnp.concatenate([ref[0].T for ref in x_refs], axis=1)
        xt_ref[0] = xt
        query = (dot(wq[...], xt) + column(B_QUERY)) * Q_FACTOR
        key = dot(wk[...], xt)
        qt_ref[0] = query.astype(bf16)
        kt_ref[0] = key.astype(bf16)
        bounds = [
            jnp.max(head_sums(query * query), axis=1, keepdims=True),
            jnp.max(head_sums(key * key), axis=1, keepdims=True),
        ]
        small_ref[0] = (jnp.max(bounds[0] * bounds[1]) < SMALL_SCORE**2).astype(jnp.int32)
        vt_ref[0] = (dot(wv[...], xt) + column(B_VALUE)).astype(bf16)

    length = xt_ref.shape[2]
    ones = jnp.ones((AUG, length), bf16)

    def rows(ref, h):
        return ref[0, pl.ds(pl.multiple_of((group * PER_GROUP + h) * HD, HD), HD), :]

    def score(h):
        keys = jnp.concatenate([rows(kt_ref, h), aug_ref[0, AUG:]], axis=0)
        query = jnp.concatenate([rows(qt_ref, h), aug_ref[0, :AUG]], axis=0)
        return dot(keys, query, TN)

    def mix(h):
        values = jnp.concatenate([rows(vt_ref, h), ones], axis=0)
        mixed = dot(values, p_ref[0, h])
        inverse = 1.0 / mixed[HD : HD + 1]
        att_ref[0, pl.ds(pl.multiple_of((group * PER_GROUP + h) * HD, HD), HD), :] = mixed[:HD] * inverse
        stat_ref[0, pl.ds(group * PER_GROUP + h, 1), :] = inverse

    def heads(shifted):
        scores = score(0)
        for h in range(PER_GROUP):
            following = score(h + 1) if h + 1 < PER_GROUP else None
            if h >= 1:
                mix(h - 1)
            if shifted:
                scores = scores - jnp.max(scores, axis=0, keepdims=True)
            p_ref[0, h] = jnp.exp2(scores).astype(bf16)
            scores = following
        mix(PER_GROUP - 1)

    @pl.when(small_ref[0] == 1)
    def _():
        heads(False)

    @pl.when(small_ref[0] == 0)
    def _():
        heads(True)

    @pl.when(group == GROUPS - 1)
    def _():
        res1 = xt_ref[0].astype(f32) + dot(wo[...], att_ref[0].astype(bf16)) + column(B_OUT)
        scaled1, inverse1 = normalize(res1)
        s1_ref[0] = scaled1
        stat_ref[0, HEADS : HEADS + 1] = inverse1
        normed = scaled1 * column(GAIN1) + shift_of(cols, SHIFT1)
        ff = wup.shape[0]
        width = wup.shape[1]
        b_up = jnp.concatenate([column(B_UP + i) for i in range(ff // width)], axis=0)
        upward = dot(wup[...], normed.astype(bf16)) + b_up
        act, slope = gelu_parts(upward)
        act_b = act.astype(bf16)
        act_ref[0] = act_b
        slope_ref[0] = slope.astype(bf16)
        res2 = normed + dot(wdn[...], act_b) + column(B_DOWN)
        scaled2, inverse2 = normalize(res2)
        s2_ref[0] = scaled2
        stat_ref[0, HEADS + 1 : HEADS + 2] = inverse2
        out = (scaled2 * column(GAIN2) + column(SHIFT2)).astype(bf16)
        for index, ref in enumerate(lo_refs):
            ref[0] = out[:, index * span : (index + 1) * span].T


def head_sums(values):
    return jnp.sum(values.reshape(HEADS, HD, values.shape[1]), axis=1)


def shift_of(cols, index):
    return cols[:, index : index + 1]


def forward(pieces, base, total, aug, weights, carried):
    rows, span, width = pieces[0].shape
    count = len(pieces)
    length = span * count
    ff = weights[5].shape[0]
    piece_spec = pl.BlockSpec((1, span, width), lambda r, g: (r, 0, 0))
    full = lambda a: pl.BlockSpec(a.shape, lambda r, g: (0, 0))

    def tall(height):
        return pl.BlockSpec((1, height, length), lambda r, g: (r + base, 0, 0))

    saved_specs = [tall(width)] * 4 + [
        pl.BlockSpec((1, PER_GROUP, length, length), lambda r, g: (r + base, g, 0, 0)),
        tall(width), tall(width), tall(width), tall(16), tall(ff), tall(ff),
    ]
    saved_shapes = [jax.ShapeDtypeStruct((total, width, length), bf16)] * 4 + [
        jax.ShapeDtypeStruct((total, HEADS, length, length), bf16),
        jax.ShapeDtypeStruct((total, width, length), f32),
        jax.ShapeDtypeStruct((total, width, length), f32),
        jax.ShapeDtypeStruct((total, width, length), f32),
        jax.ShapeDtypeStruct((total, 16, length), f32),
        jax.ShapeDtypeStruct((total, ff, length), bf16),
        jax.ShapeDtypeStruct((total, ff, length), bf16),
    ]
    first = count + 1 + len(weights)
    out = pl.pallas_call(
        functools.partial(forward_kernel, pieces=count, carried=len(carried)),
        grid=(rows, GROUPS),
        in_specs=[piece_spec] * count
        + [pl.BlockSpec((1, 2 * AUG, length), lambda r, g: (r + base, 0, 0))]
        + [full(w) for w in weights]
        + [pl.BlockSpec(memory_space=pl.ANY)] * len(carried),
        out_specs=[pl.BlockSpec((1, span, width), lambda r, g: (r + base, 0, 0))] * count + saved_specs,
        out_shape=[jax.ShapeDtypeStruct((total, span, width), bf16)] * count + saved_shapes,
        scratch_shapes=[pltpu.SMEM((1,), jnp.int32)],
        input_output_aliases={first + i: i for i in range(len(carried))},
        compiler_params=pltpu.CompilerParams(vmem_limit_bytes=VMEM_LIMIT),
        cost_estimate=cost(14 * rows),
        name="forward",
    )(*pieces, aug, *weights, *carried)
    return out


def emit(packed, index, outs, inner):
    size = outs[0].shape[0] // inner
    for shift, ref in enumerate(outs):
        for block in range(inner):
            start = pl.multiple_of((block * len(outs) + (index ^ shift)) * size, 16)
            ref[block * size : (block + 1) * size] = packed[pl.ds(start, size), :]


def dense_kernel(*refs, pieces, rows, parts, inner):
    index_ref = refs[0]
    cot_refs = refs[1 : 1 + pieces]
    (
        att_ref, s1_ref, s2_ref, stat_ref, act_ref, slope_ref, cols, wo, wup, wdn,
    ) = refs[1 + pieces : 11 + pieces]
    gres_ref, og_ref, delta_ref = refs[11 + pieces : 14 + pieces]
    part_refs = refs[14 + pieces : 14 + pieces + parts]
    acc_dn, acc_up, acc_out, acc_bias, acc_upb, packed = refs[14 + pieces + parts :]
    step = pl.program_id(0)
    width = s1_ref.shape[1]
    ff = acc_up.shape[1]

    def column(index):
        return cols[:, index : index + 1]

    @pl.when(step == 0)
    def _():
        for ref in (acc_dn, acc_up, acc_out, acc_bias, acc_upb):
            ref[...] = jnp.zeros_like(ref)

    att = att_ref[0]
    att_b = att.astype(bf16)
    scaled1 = s1_ref[0]
    scaled2 = s2_ref[0]
    inverse1 = stat_ref[0, HEADS : HEADS + 1]
    inverse2 = stat_ref[0, HEADS + 1 : HEADS + 2]
    normed_b = (scaled1 * column(GAIN1) + column(SHIFT1)).astype(bf16)
    act_b = act_ref[0]
    cot = jnp.concatenate([ref[0].T for ref in cot_refs], axis=1).astype(f32)
    acc_bias[0] += fold_lanes(cot * scaled2)
    acc_bias[1] += fold_lanes(cot)
    gres2 = normalize_back(cot * column(GAIN2), scaled2, inverse2)
    down_b = gres2.astype(bf16)
    acc_bias[2] += fold_lanes(down_b.astype(f32))
    up_b = (dot(wdn[...], down_b) * slope_ref[0].astype(f32)).astype(bf16)
    acc_dn[...] += dot(act_b, down_b, NT)
    acc_upb[...] += fold_lanes(up_b.astype(f32))
    gnormed = gres2 + dot(wup[...], up_b)
    acc_up[...] += dot(normed_b, up_b, NT)
    acc_bias[3] += fold_lanes(gnormed * scaled1)
    acc_bias[4] += fold_lanes(gnormed)
    gres1 = normalize_back(gnormed * column(GAIN1), scaled1, inverse1)
    gres_ref[0] = gres1
    branch_b = gres1.astype(bf16)
    acc_bias[5] += fold_lanes(branch_b.astype(f32))
    og = dot(wo[...], branch_b)
    acc_out[...] += dot(att_b, branch_b, NT)
    for h in range(HEADS):
        part = slice(h * HD, (h + 1) * HD)
        scaled_og = (og[part] * stat_ref[0, h : h + 1, :]).astype(bf16)
        og_ref[0, part, :] = scaled_og
        delta_ref[0, h : h + 1, :] = jnp.sum(scaled_og.astype(f32) * att[part], axis=0, keepdims=True)

    @pl.when(step == rows - 1)
    def _():
        packed[:ff] = acc_dn[...].astype(bf16)
        for index in range(ff // width):
            packed[ff + index * width : ff + (index + 1) * width] = acc_up[
                :, index * width : (index + 1) * width
            ].astype(bf16)
        packed[2 * ff : 2 * ff + width] = acc_out[...].astype(bf16)
        bias_rows = [row_sum(acc_bias[i]) for i in range(6)]
        bias_rows += [row_sum(acc_upb[i * width : (i + 1) * width]) for i in range(ff // width)]
        tail = packed.shape[0] - 2 * ff - width
        bias_rows.append(jnp.zeros((tail - len(bias_rows), width), f32))
        packed[2 * ff + width :] = jnp.concatenate(bias_rows, axis=0).astype(bf16)
        emit(packed, index_ref[0], part_refs, inner)


def dense(pieces, saved, cols, weights, packed_rows, parts, inner, index):
    rows, span, width = pieces[0].shape
    count = len(pieces)
    length = span * count
    ff = weights[2].shape[0]
    piece_spec = pl.BlockSpec((1, span, width), lambda r, i: (r, 0, 0))
    full = lambda a: pl.BlockSpec(a.shape, lambda r, i: (0, 0))

    def tall(height):
        return pl.BlockSpec((1, height, length), lambda r, i: (r, 0, 0))

    part = (packed_rows // parts, width)
    out = pl.pallas_call(
        functools.partial(dense_kernel, pieces=count, rows=rows, parts=parts, inner=inner),
        grid_spec=pltpu.PrefetchScalarGridSpec(
            num_scalar_prefetch=1,
            grid=(rows,),
            in_specs=[piece_spec] * count
            + [tall(a.shape[1]) for a in saved]
            + [full(cols)]
            + [full(w) for w in weights],
            out_specs=[tall(width), tall(width), tall(16)] + [pl.BlockSpec(part, lambda r, i: (0, 0))] * parts,
            scratch_shapes=[
                pltpu.VMEM((ff, width), f32),
                pltpu.VMEM((width, ff), f32),
                pltpu.VMEM((width, width), f32),
                pltpu.VMEM((6, width, 128), f32),
                pltpu.VMEM((ff, 128), f32),
                pltpu.VMEM((packed_rows, width), bf16),
            ],
        ),
        out_shape=[
            jax.ShapeDtypeStruct((rows, width, length), f32),
            jax.ShapeDtypeStruct((rows, width, length), bf16),
            jax.ShapeDtypeStruct((rows, 16, length), f32),
        ]
        + [jax.ShapeDtypeStruct(part, bf16)] * parts,
        compiler_params=pltpu.CompilerParams(vmem_limit_bytes=VMEM_LIMIT),
        cost_estimate=cost(20),
        name="dense",
    )(index, *pieces, *saved, cols, *weights)
    return out[0], out[1], out[2], out[3:]


def back_kernel(*refs, pieces, parts, inner, carried, after):
    index_ref, xt_ref, qt_ref, kt_ref, vt_ref, og_ref, delta_ref, p_ref, gres_ref, w_ref = refs[:10]
    if carried:
        acc_in, bias_in = refs[10:12]
    out_refs = refs[10 + carried + after : 10 + carried + after + pieces]
    rest = refs[10 + carried + after + pieces :]
    if parts:
        part_refs, (grads, held, packed) = rest[:parts], rest[parts:]
    else:
        acc_ref, bias_ref, grads, held = rest
    group = pl.program_id(1)
    length = xt_ref.shape[2]
    width = xt_ref.shape[1]
    span = out_refs[0].shape[1]

    def start_of(h):
        return pl.multiple_of((group * PER_GROUP + h) * HD, HD)

    def rows_of(ref, h):
        return ref[0, pl.ds(start_of(h), HD), :]

    sign = jnp.where(lax.broadcasted_iota(jnp.int32, (AUG, length), 0) < 3, 1.0, 0.0).astype(bf16)

    def grad_probs(h):
        delta = delta_ref[0, pl.ds(group * PER_GROUP + h, 1), :]
        first = delta.astype(bf16)
        rest = delta - first.astype(f32)
        second = rest.astype(bf16)
        third = (rest - second.astype(f32)).astype(bf16)
        aug = jnp.concatenate(
            [-first.astype(f32), -second.astype(f32), -third.astype(f32), jnp.zeros((AUG - 3, length), f32)], axis=0
        ).astype(bf16)
        left = jnp.concatenate([rows_of(vt_ref, h), sign], axis=0)
        right = jnp.concatenate([rows_of(og_ref, h), aug], axis=0)
        return dot(left, right, TN)

    for h in range(PER_GROUP):
        probs = p_ref[0, h]
        held[h] = (probs.astype(f32) * grad_probs(h)).astype(bf16)
        grads[pl.ds(2 * width + start_of(h), HD), :] = dot(rows_of(og_ref, h), probs, NT).astype(bf16)
    for h in range(PER_GROUP):
        start = start_of(h)
        grads[pl.ds(start, HD), :] = (dot(rows_of(kt_ref, h), held[h]) * SCALE).astype(bf16)
        grads[pl.ds(width + start, HD), :] = (dot(rows_of(qt_ref, h), held[h], NT) * LN2).astype(bf16)

    @pl.when(group == GROUPS - 1)
    def _():
        total = grads[...]
        acc = dot(xt_ref[0], total, NT)
        bias_q = fold_lanes(total[:width].astype(f32))
        bias_v = fold_lanes(total[2 * width :].astype(f32))
        if carried:
            acc = acc + acc_in[...]
            bias_q = bias_q + bias_in[0]
            bias_v = bias_v + bias_in[1]
        if parts:
            for index in range(3 * width // 128):
                packed[index * width : (index + 1) * width] = acc[:, index * 128 : (index + 1) * 128].astype(bf16)
            bias_rows = []
            for bias in (bias_q, bias_v):
                flat = row_sum(bias)
                bias_rows += [flat[:, i * 128 : (i + 1) * 128] for i in range(width // 128)]
            tail = packed.shape[0] - 9 * width
            bias_rows.append(jnp.zeros((tail - len(bias_rows), 128), f32))
            packed[9 * width :] = jnp.concatenate(bias_rows, axis=0).astype(bf16)
            emit(packed, index_ref[0], part_refs, inner)
        else:
            acc_ref[...] = acc
            bias_ref[0] = bias_q
            bias_ref[1] = bias_v
        result = (gres_ref[0] + dot(w_ref[...], total)).astype(bf16)
        for index, ref in enumerate(out_refs):
            ref[0] = result[:, index * span : (index + 1) * span].T


def back(
    shared, at, row, saved, gres, og, delta, probs, w_all, packed_rows, parts, inner, index, sums, after
):
    count = len(shared) if isinstance(shared, (list, tuple)) else shared
    fresh = not isinstance(shared, (list, tuple))
    height = -at if fresh else shared[0].shape[0]
    target = 0 if fresh else at
    carried = list(sums)
    xt, qt, kt, vt = saved
    rows, width, length = xt.shape
    span = length // count
    wide = pl.BlockSpec((1, width, length), lambda r, g, i: (row, 0, 0))
    sums = [((width, 3 * width), lambda r, g, i: (0, 0)), ((2, width, 128), lambda r, g, i: (0, 0, 0))]
    sum_specs = [pl.BlockSpec(*s) for s in sums]
    part = (packed_rows // max(parts, 1), 128)
    if parts:
        last_specs = [pl.BlockSpec(part, lambda r, g, i: (0, 0))] * parts
        last_shapes = [jax.ShapeDtypeStruct(part, bf16)] * parts
    else:
        last_specs = sum_specs
        last_shapes = [jax.ShapeDtypeStruct(s[0], f32) for s in sums]
    scratch = [pltpu.VMEM((3 * width, length), bf16), pltpu.VMEM((PER_GROUP, length, length), bf16)]
    if parts:
        scratch.append(pltpu.VMEM((packed_rows, 128), bf16))
    out = pl.pallas_call(
        functools.partial(
            back_kernel, pieces=count, parts=parts, inner=inner, carried=len(carried), after=len(after) + (0 if fresh else count)
        ),
        grid_spec=pltpu.PrefetchScalarGridSpec(
            num_scalar_prefetch=1,
            grid=(1, GROUPS),
            in_specs=[wide] * 5
            + [
                pl.BlockSpec((1, 16, length), lambda r, g, i: (row, 0, 0)),
                pl.BlockSpec((1, PER_GROUP, length, length), lambda r, g, i: (row, g, 0, 0)),
                wide,
                pl.BlockSpec(w_all.shape, lambda r, g, i: (0, 0)),
            ]
            + (sum_specs if carried else [])
            + ([] if fresh else [pl.BlockSpec(memory_space=pl.ANY)] * count)
            + [pl.BlockSpec(memory_space=pl.ANY)] * len(after),
            out_specs=[pl.BlockSpec((1, span, width), lambda r, g, i: (target, 0, 0))] * count + last_specs,
            scratch_shapes=scratch,
        ),
        out_shape=[jax.ShapeDtypeStruct((height, span, width), bf16)] * count + last_shapes,
        input_output_aliases={} if fresh else {10 + len(carried) + i: i for i in range(count)},
        compiler_params=pltpu.CompilerParams(vmem_limit_bytes=VMEM_LIMIT),
        cost_estimate=cost(10),
        name="back",
    )(index, xt, qt, kt, vt, og, delta, probs, gres, w_all, *carried, *([] if fresh else shared), *after)
    return out[:count], out[count:]


def exchange(pieces, axis, devices, unit=1):
    moved = [pieces[0]]
    for shift in range(1, len(pieces)):
        moved.append(lax.ppermute(pieces[shift], axis, [(i, i ^ (shift * unit)) for i in range(devices)]))
    return moved


def tree_sum(blocks):
    while len(blocks) > 1:
        blocks = [left + right for left, right in zip(blocks[::2], blocks[1::2])]
    return blocks[0]


def combine_kernel(index_ref, *refs, inputs, after, inner):
    total = tree_sum([ref[...].astype(f32) for ref in refs[:inputs]]).astype(bf16)
    outs = refs[inputs + after :]
    if len(outs) == 1:
        outs[0][...] = total
    else:
        packed = outs[-1]
        packed[...] = total
        emit(packed, index_ref[0], outs[:-1], inner)


def combine(blocks, parts, inner, index, after=()):
    rows, width = blocks[0].shape
    part = (rows // parts, width)
    full = lambda s: pl.BlockSpec(s, lambda i, j: (0, 0))
    return pl.pallas_call(
        functools.partial(combine_kernel, inputs=len(blocks), after=len(after), inner=inner),
        grid_spec=pltpu.PrefetchScalarGridSpec(
            num_scalar_prefetch=1,
            grid=(1,),
            in_specs=[full((rows, width))] * len(blocks) + [pl.BlockSpec(memory_space=pl.ANY)] * len(after),
            out_specs=[full(part)] * parts,
            scratch_shapes=[pltpu.VMEM((rows, width), bf16)] if parts > 1 else [],
        ),
        out_shape=[jax.ShapeDtypeStruct(part, bf16)] * parts,
        compiler_params=pltpu.CompilerParams(vmem_limit_bytes=VMEM_LIMIT),
        cost_estimate=cost(1),
        name="combine",
    )(index, *blocks, *after)


def assemble_kernel(index_ref, *refs, inputs):
    out = refs[-1]
    size = refs[0].shape[0]
    for shift, ref in enumerate(refs[:inputs]):
        out[pl.ds(pl.multiple_of((index_ref[0] ^ shift) * size, 16), size), :] = ref[...]


def assemble(blocks, index, after=()):
    rows, width = blocks[0].shape
    full = lambda s: pl.BlockSpec(s, lambda i, j: (0, 0))
    shape = (rows * len(blocks), width)
    return pl.pallas_call(
        functools.partial(assemble_kernel, inputs=len(blocks)),
        grid_spec=pltpu.PrefetchScalarGridSpec(
            num_scalar_prefetch=1,
            grid=(1,),
            in_specs=[full((rows, width))] * len(blocks) + [pl.BlockSpec(memory_space=pl.ANY)] * len(after),
            out_specs=full(shape),
        ),
        out_shape=jax.ShapeDtypeStruct(shape, bf16),
        compiler_params=pltpu.CompilerParams(vmem_limit_bytes=VMEM_LIMIT),
        cost_estimate=cost(1),
        name="assemble",
    )(index, *blocks, *after)


def place_kernel(index_ref, *refs, sets, count):
    out = refs[-1]
    row = pl.program_id(0)
    start = 0
    for number, size in enumerate(sets):

        @pl.when((row >= start) & (row < start + size))
        def _(number=number):
            for shift in range(count):
                out[index_ref[0] ^ shift] = refs[number * count + shift][...].astype(out.dtype)

        start += size


def place(sets, dtype, index, after=()):
    sizes = [pieces[0].shape[0] for pieces in sets]
    count = len(sets[0])
    rows = sum(sizes)
    _, span, width = sets[0][0].shape
    shape = (count, rows, span, width)
    in_specs = []
    start = 0
    for size in sizes:
        block = lambda r, i, start=start, size=size: (jnp.clip(r - start, 0, size - 1), 0, 0)
        in_specs += [pl.BlockSpec((1, span, width), block)] * count
        start += size
    out = pl.pallas_call(
        functools.partial(place_kernel, sets=sizes, count=count),
        grid_spec=pltpu.PrefetchScalarGridSpec(
            num_scalar_prefetch=1,
            grid=(rows,),
            in_specs=in_specs + [pl.BlockSpec(memory_space=pl.ANY)] * len(after),
            out_specs=pl.BlockSpec((count, 1, span, width), lambda r, i: (0, r, 0, 0)),
        ),
        out_shape=jax.ShapeDtypeStruct(shape, dtype),
        compiler_params=pltpu.CompilerParams(vmem_limit_bytes=VMEM_LIMIT),
        cost_estimate=cost(3),
        name="place",
    )(index, *[piece for pieces in sets for piece in pieces], *after)
    return out.reshape(count * rows, span, width)


def sum_stages(sizes):
    stages = []
    for axis in ("rows", "seq"):
        devices = sizes[axis]
        unit = 1
        while unit < devices:
            size = 2 if unit == 1 and devices.bit_length() % 2 == 0 else 4
            stages.append((axis, devices, unit, size, devices // (unit * size)))
            unit *= size
    return stages


def place_of(stage):
    axis, _, unit, size, _ = stage
    return ((lax.axis_index(axis) // unit) % size).astype(jnp.int32).reshape(1)


def send_parts(parts, stage):
    axis, devices, unit, _, _ = stage
    return exchange(parts, axis, devices, unit)


def cut_for(taken, stage, after=()):
    return combine(taken, stage[3], stage[4], place_of(stage), after)


def add(taken, after=()):
    return combine(taken, 1, 1, jnp.zeros((1,), jnp.int32), after)[0]


def unpack_later_kernel(block, down, up, out, *biases):
    ff, width = down.shape
    down[...] = block[:ff].astype(f32)
    for index in range(ff // width):
        up[:, index * width : (index + 1) * width] = block[ff + index * width : ff + (index + 1) * width].astype(f32)
    out[...] = block[2 * ff : 2 * ff + width].astype(f32)
    rows = block[2 * ff + width : 2 * ff + width + 16].astype(f32)
    for index, ref in enumerate(biases[:-1]):
        ref[...] = rows[index]
    per = ff // width
    biases[-1][...] = jnp.concatenate([rows[len(biases) - 1 + i] for i in range(per)], axis=0)


def unpack_later(block, width, ff):
    shapes = [(ff, width), (width, ff), (width, width)] + [(width,)] * 6 + [(ff,)]
    return pl.pallas_call(
        unpack_later_kernel,
        out_shape=[jax.ShapeDtypeStruct(s, f32) for s in shapes],
        compiler_params=pltpu.CompilerParams(vmem_limit_bytes=VMEM_LIMIT),
        cost_estimate=cost(4),
        name="unpack_later",
    )(block)


def unpack_early_kernel(block, query, key, value, bias_q, bias_v):
    width = query.shape[0]
    per = width // 128
    for number, ref in enumerate((query, key, value)):
        for index in range(per):
            start = (number * per + index) * width
            ref[:, index * 128 : (index + 1) * 128] = block[start : start + width].astype(f32)
    rows = block[3 * per * width : 3 * per * width + 16].astype(f32)
    for number, ref in enumerate((bias_q, bias_v)):
        ref[...] = jnp.concatenate([rows[number * per + i] for i in range(per)], axis=0)


def unpack_early(block, width):
    shapes = [(width, width)] * 3 + [(width,)] * 2
    return pl.pallas_call(
        unpack_early_kernel,
        out_shape=[jax.ShapeDtypeStruct(s, f32) for s in shapes],
        compiler_params=pltpu.CompilerParams(vmem_limit_bytes=VMEM_LIMIT),
        cost_estimate=cost(2),
        name="unpack_early",
    )(block)


def round_up(value, unit):
    return -(-value // unit) * unit


def body(
    tokens, lengths, w_query, b_query, w_key, w_value, b_value, w_out, b_out, gain_attn, shift_attn,
    w_up, b_up, w_down, b_down, gain_ffn, shift_ffn, cotangent, *, sizes,
):
    count = sizes["seq"]
    devices = count * sizes["rows"]
    row_count, span, width = tokens.shape
    ff = w_up.shape[1]
    length = span * count
    rows = row_count // count
    me = lax.axis_index("seq")
    order = me ^ jnp.arange(count, dtype=jnp.int32)

    def send(array, start, stop):
        parts = jnp.take(array.reshape(count, rows, span, width)[:, start:stop], order, axis=0)
        return exchange([parts[s] for s in range(count)], "seq", count)

    chunks = [(0, 1), (1, rows)] if rows > 1 else [(0, rows)]
    token_rows = [send(tokens, *chunk) for chunk in chunks]
    cot_moved = send(cotangent, 0, rows)

    bounds = lax.dynamic_slice_in_dim(jnp.cumsum(lengths, axis=1), me * rows, rows, 0)
    places = (order[:, None] * span + jnp.arange(span, dtype=jnp.int32)[None, :]).reshape(length)
    segment = jnp.sum((places[None, None, :] >= bounds[:, :, None]).astype(jnp.int32), axis=1)
    ids = jnp.arange(2 * AUG, dtype=jnp.int32)[None, :, None]
    same = segment[:, None, :] == ids % AUG
    aug = jnp.where(ids < AUG, jnp.where(same, 1.0, 0.0), jnp.where(same | (ids % AUG >= lengths.shape[1]), 0.0, -BIG))
    aug = aug.astype(bf16)

    vectors = [b_query, b_value, b_out, gain_attn, shift_attn, b_down, gain_ffn, shift_ffn]
    vectors = jnp.concatenate([jnp.stack(vectors), b_up.reshape(-1, width)], axis=0)
    *turned, cols = prepare((w_query, w_key, w_value, w_out, w_up, w_down), vectors)
    carried = []
    for (start, _), pieces in zip(chunks, token_rows):
        carried = forward(pieces, start, rows, aug, [cols] + turned, carried)
    lo_moved = exchange(carried[:count], "seq", count)
    carried = carried[count:]
    stages = sum_stages(sizes)
    row_stages, seq_stages = [[stage for stage in stages if stage[0] == axis] for axis in ("rows", "seq")]
    first = stages[0]
    index = place_of(first)
    later_rows = round_up(2 * ff + width + 16, 16 * devices)
    gres, og, delta, later = dense(
        cot_moved, carried[5:], cols, (w_out, w_up, w_down), later_rows, first[3], first[4], index
    )
    w_all = jnp.concatenate([w_query, w_key, w_value], axis=1)
    first_rows = round_up(9 * width + 16, 16 * devices)

    def back_row(shared, at, row, sums, after):
        parts = first[3] if row == rows - 1 else 0
        return back(
            shared, at, row, carried[:4], gres, og, delta, carried[4], w_all, first_rows, parts, first[4], index, sums,
            after,
        )

    number = 0
    taken = send_parts(later, stages[0])
    sums = []
    done = []
    sets = []
    shared = None
    waits = []
    for row in range(rows):
        if number + 1 < len(stages):
            number += 1
            later = cut_for(taken, stages[number], done)
            waits += list(later)
            taken = send_parts(later, stages[number])
        elif taken is not None:
            later = add(taken, done)
            waits.append(later)
            taken = None
        if row == 0:
            waits += lo_moved[2:3]
        elif row == 1:
            waits += lo_moved[1:2] + lo_moved[3:]
        if row >= 2:
            waits += sets[row - 2][1:]
        shared, sums = back_row(count, -1, row, sums, waits)
        done = sums[:1]
        waits = []
        if row < rows - 1:
            sets.append(exchange(shared, "seq", count))
    while number + 1 < len(stages):
        number += 1
        later = cut_for(taken, stages[number], done)
        taken = send_parts(later, stages[number])
    if taken is not None:
        later = add(taken, done)
    waits = list(sets[-1][1:]) if sets else []
    early = sums
    for number, stage in enumerate(row_stages):
        taken = send_parts(early, stage)
        if number + 1 < len(row_stages):
            early = cut_for(taken, row_stages[number + 1])
    early = add(taken)
    for stage in reversed(seq_stages):
        later = assemble(send_parts([later] * stage[3], stage), place_of(stage), list(done) + waits)
        waits = []
    later = lax.all_gather(later, "rows", axis=0, tiled=True)
    for stage in seq_stages:
        early = add(send_parts([early] * stage[3], stage))
    here = me.astype(jnp.int32).reshape(1)
    layer_out = place([lo_moved], bf16, here, done)
    sets.append(exchange(shared, "seq", count))
    grad_tokens = place(sets, f32, here, [early])
    early = lax.all_gather(early, "rows", axis=0, tiled=True)
    (
        grad_down, grad_up, grad_output, grad_gain2, grad_shift2, grad_dnbias, grad_gain1, grad_shift1, grad_obias,
        grad_upbias,
    ) = unpack_later(later, width, ff)
    grad_query, grad_key, grad_value, grad_qbias, grad_vbias = unpack_early(early, width)
    return (
        layer_out, grad_tokens, grad_query, grad_qbias, grad_key, grad_value, grad_vbias, grad_output, grad_obias,
        grad_gain1, grad_shift1, grad_up, grad_upbias, grad_down, grad_dnbias, grad_gain2, grad_shift2,
    )


def solution(mesh):
    split = P("rows", "seq", None)
    in_specs = (split, P("rows", None)) + (P(),) * 15 + (split,)
    out_specs = (split, split) + (P(),) * 15
    sizes = dict(mesh.shape)
    return jax.shard_map(
        functools.partial(body, sizes=sizes), mesh=mesh, in_specs=in_specs, out_specs=out_specs, check_vma=False
    )
```

```python
import functools
import math

import jax
import jax.numpy as jnp
from jax import lax
from jax.experimental import pallas as pl
from jax.experimental.pallas import tpu as pltpu
from jax.sharding import PartitionSpec as P

HEADS = 12
HD = 32
GROUPS = 3
PER_GROUP = HEADS // GROUPS
AUG = 16
BIG = 2.0**100
SMALL_SCORE = 60.0
EPSILON = 1e-05
SCALE = HD ** (-0.5)
LOG2E = math.log2(math.e)
Q_FACTOR = SCALE * LOG2E
LN2 = math.log(2.0)
VMEM_LIMIT = 60 * 2**20

f32 = jnp.float32
bf16 = jnp.bfloat16
NN = (((1,), (0,)), ((), ()))
NT = (((1,), (1,)), ((), ()))
TN = (((0,), (0,)), ((), ()))


def dot(left, right, dims=NN):
    return lax.dot_general(left, right, dims, preferred_element_type=f32)


def fold_lanes(values):
    total = values[:, :128]
    for start in range(128, values.shape[1], 128):
        total = total + values[:, start : start + 128]
    return total


def row_sum(partial):
    return jnp.sum(partial.T, axis=0, keepdims=True)


def normalize(hidden):
    scale = 1.0 / hidden.shape[0]
    centre = hidden - jnp.sum(hidden, axis=0, keepdims=True) * scale
    variance = jnp.sum(centre * centre, axis=0, keepdims=True) * scale
    inverse = lax.rsqrt(variance + EPSILON)
    return centre * inverse, inverse


def normalize_back(upstream, scaled, inverse):
    scale = 1.0 / upstream.shape[0]
    mean = jnp.sum(upstream, axis=0, keepdims=True) * scale
    spread = jnp.sum(upstream * scaled, axis=0, keepdims=True) * scale
    return inverse * (upstream - mean - scaled * spread)


def gelu_parts(v):
    cdf = 0.5 + 0.5 * lax.erf(v * 0.5**0.5)
    bell = jnp.exp2((v * v) * (-0.5 * LOG2E))
    return v * cdf, cdf + v * bell * (2.0 * math.pi) ** (-0.5)


def prepare_kernel(wq, wk, wv, wo, wup, wdn, rows, wq_t, wk_t, wv_t, wo_t, wup_t, wdn_t, columns):
    for source, target in ((wq, wq_t), (wk, wk_t), (wv, wv_t), (wo, wo_t), (wup, wup_t), (wdn, wdn_t)):
        target[...] = source[...].T
    width = rows.shape[1]
    columns[...] = jnp.concatenate([rows[...], jnp.zeros((128 - rows.shape[0], width), f32)], axis=0).T


def prepare(weights, rows):
    shapes = [jax.ShapeDtypeStruct(w.shape[::-1], w.dtype) for w in weights]
    shapes.append(jax.ShapeDtypeStruct((rows.shape[1], 128), f32))
    return pl.pallas_call(
        prepare_kernel,
        out_shape=shapes,
        compiler_params=pltpu.CompilerParams(vmem_limit_bytes=VMEM_LIMIT),
        cost_estimate=cost(5),
        name="prepare",
    )(*weights, rows)


def cost(micros):
    return pl.CostEstimate(flops=int(micros * 1e5), transcendentals=0, bytes_accessed=int(micros * 1e3))


B_QUERY, B_VALUE, B_OUT, GAIN1, SHIFT1, B_DOWN, GAIN2, SHIFT2, B_UP = range(9)


ANY = pl.BlockSpec(memory_space=pl.ANY)


def head_sums(values):
    return jnp.sum(values.reshape(HEADS, HD, values.shape[1]), axis=1)


def pick_kernel(index_ref, *refs, count):
    for shift in range(count):
        out = refs[len(refs) - count + shift]
        out[0] = refs[shift][0]
        out[1] = refs[count + shift][0]


def pick(tokens, cotangent, count, rows, row, index, after):
    _, span, width = tokens.shape
    specs = [
        pl.BlockSpec((1, span, width), lambda i, place, shift=shift: ((place[0] ^ shift) * rows + row, 0, 0))
        for shift in range(count)
    ]
    return pl.pallas_call(
        functools.partial(pick_kernel, count=count),
        grid_spec=pltpu.PrefetchScalarGridSpec(
            num_scalar_prefetch=1,
            grid=(1,),
            in_specs=specs * 2 + [ANY] * len(after),
            out_specs=[pl.BlockSpec((2, span, width), lambda i, place: (0, 0, 0))] * count,
        ),
        out_shape=[jax.ShapeDtypeStruct((2, span, width), bf16)] * count,
        compiler_params=pltpu.CompilerParams(vmem_limit_bytes=VMEM_LIMIT),
        cost_estimate=cost(1),
        name="pick",
    )(index, *[tokens] * count, *[cotangent] * count, *after)


def emit(packed, index, outs, inner):
    size = outs[0].shape[0] // inner
    for shift, ref in enumerate(outs):
        for block in range(inner):
            start = pl.multiple_of((block * len(outs) + (index ^ shift)) * size, 16)
            ref[block * size : (block + 1) * size] = packed[pl.ds(start, size), :]


class Taker:
    def __init__(self, refs):
        self.refs = list(refs)

    def __call__(self, number):
        taken = self.refs[:number]
        del self.refs[:number]
        return taken


def column_of(cols, index):
    return cols[:, index : index + 1]


def project_row(piece_refs, cols, wq, wk, wv, saved, small_ref):
    xt = jnp.concatenate([ref[0].T for ref in piece_refs], axis=1)
    query = (dot(wq[...], xt) + column_of(cols, B_QUERY)) * Q_FACTOR
    key = dot(wk[...], xt)
    saved[0] = query.astype(bf16)
    saved[1] = key.astype(bf16)
    saved[2] = (dot(wv[...], xt) + column_of(cols, B_VALUE)).astype(bf16)
    saved[3] = xt
    bounds = [
        jnp.max(head_sums(query * query), axis=1, keepdims=True),
        jnp.max(head_sums(key * key), axis=1, keepdims=True),
    ]
    small_ref[0] = (jnp.max(bounds[0] * bounds[1]) < SMALL_SCORE**2).astype(jnp.int32)


def head_rows(group, h):
    return pl.ds(pl.multiple_of((group * PER_GROUP + h) * HD, HD), HD)


def attend_heads(group, saved, aug_ref, probs, att_ref, stat_ref, small_ref):
    length = saved.shape[2]
    ones = jnp.ones((AUG, length), bf16)

    def score(h):
        keys = jnp.concatenate([saved[1, head_rows(group, h), :], aug_ref[0, AUG:]], axis=0)
        query = jnp.concatenate([saved[0, head_rows(group, h), :], aug_ref[0, :AUG]], axis=0)
        return dot(keys, query, TN)

    def mix(h):
        values = jnp.concatenate([saved[2, head_rows(group, h), :], ones], axis=0)
        mixed = dot(values, probs(h)[...])
        inverse = 1.0 / mixed[HD : HD + 1]
        att_ref[head_rows(group, h), :] = mixed[:HD] * inverse
        stat_ref[pl.ds(group * PER_GROUP + h, 1), :] = inverse

    def heads(shifted):
        scores = score(0)
        for h in range(PER_GROUP):
            following = score(h + 1) if h + 1 < PER_GROUP else None
            if h >= 1:
                mix(h - 1)
            if shifted:
                scores = scores - jnp.max(scores, axis=0, keepdims=True)
            probs(h)[...] = jnp.exp2(scores).astype(bf16)
            scores = following
        mix(PER_GROUP - 1)

    @pl.when(small_ref[0] == 1)
    def _():
        heads(False)

    @pl.when(small_ref[0] == 0)
    def _():
        heads(True)


def dense_row(piece_refs, cols, saved, att_ref, stat_ref, weights, sums, carried, write_out, summed, og_ref, delta_ref, gres_ref):
    wo_t, wo, wup_t, wup, wdn_t, wdn = weights
    acc_dn, acc_up, acc_out = sums
    ff = acc_dn.shape[0]
    width = att_ref.shape[0]

    def column(index):
        return column_of(cols, index)

    def add(number, value):
        ref = sums[number]
        ref[...] = ref[...] + value if carried else value
        summed(number)

    att = att_ref[...]
    att_b = att.astype(bf16)
    res1 = saved[3].astype(f32) + dot(wo_t[...], att_b) + column(B_OUT)
    scaled1, inverse1 = normalize(res1)
    normed = scaled1 * column(GAIN1) + column(SHIFT1)
    normed_b = normed.astype(bf16)
    b_up = jnp.concatenate([column(B_UP + i) for i in range(ff // width)], axis=0)
    act, slope = gelu_parts(dot(wup_t[...], normed_b) + b_up)
    act_b = act.astype(bf16)
    res2 = normed + dot(wdn_t[...], act_b) + column(B_DOWN)
    scaled2, inverse2 = normalize(res2)
    write_out((scaled2 * column(GAIN2) + column(SHIFT2)).astype(bf16))
    cot = jnp.concatenate([ref[1].T for ref in piece_refs], axis=1).astype(f32)
    gres2 = normalize_back(cot * column(GAIN2), scaled2, inverse2)
    down_b = gres2.astype(bf16)
    up_b = (dot(wdn[...], down_b) * slope).astype(bf16)
    add(0, dot(act_b, down_b, NT))
    gnormed = gres2 + dot(wup[...], up_b)
    add(1, dot(normed_b, up_b, NT))
    gres1 = normalize_back(gnormed * column(GAIN1), scaled1, inverse1)
    gres_ref[...] = gres1
    branch_b = gres1.astype(bf16)
    og = dot(wo[...], branch_b)
    add(2, dot(att_b, branch_b, NT))
    for h in range(HEADS):
        part = slice(h * HD, (h + 1) * HD)
        scaled_og = (og[part] * stat_ref[h : h + 1, :]).astype(bf16)
        og_ref[part, :] = scaled_og
        delta_ref[h : h + 1, :] = jnp.sum(scaled_og.astype(f32) * att[part], axis=0, keepdims=True)
    biases = [cot * scaled2, cot, down_b.astype(f32), gnormed * scaled1, gnormed, branch_b.astype(f32)]
    bias_rows = [row_sum(fold_lanes(value)) for value in biases]
    up_sum = fold_lanes(up_b.astype(f32))
    bias_rows += [row_sum(up_sum[i * width : (i + 1) * width]) for i in range(ff // width)]
    bias_rows.append(jnp.zeros((16 - len(bias_rows), width), f32))
    return jnp.concatenate(bias_rows, axis=0)


def back_heads(group, saved, og_ref, delta_ref, probs, grads, held):
    length = og_ref.shape[1]
    width = og_ref.shape[0]
    sign = jnp.where(lax.broadcasted_iota(jnp.int32, (AUG, length), 0) < 3, 1.0, 0.0).astype(bf16)

    def grad_probs(h):
        delta = delta_ref[pl.ds(group * PER_GROUP + h, 1), :]
        first = delta.astype(bf16)
        rest = delta - first.astype(f32)
        second = rest.astype(bf16)
        third = (rest - second.astype(f32)).astype(bf16)
        aug = jnp.concatenate(
            [-first.astype(f32), -second.astype(f32), -third.astype(f32), jnp.zeros((AUG - 3, length), f32)], axis=0
        ).astype(bf16)
        left = jnp.concatenate([saved[2, head_rows(group, h), :], sign], axis=0)
        right = jnp.concatenate([og_ref[head_rows(group, h), :], aug], axis=0)
        return dot(left, right, TN)

    def target(which, h):
        return pl.ds(pl.multiple_of(which * width + (group * PER_GROUP + h) * HD, HD), HD)

    for h in range(PER_GROUP):
        held[h] = (probs(h)[...].astype(f32) * grad_probs(h)).astype(bf16)
        grads[target(2, h), :] = dot(og_ref[head_rows(group, h), :], probs(h)[...], NT).astype(bf16)
    for h in range(PER_GROUP):
        grads[target(0, h), :] = (dot(saved[1, head_rows(group, h), :], held[h]) * SCALE).astype(bf16)
        grads[target(1, h), :] = (dot(saved[0, head_rows(group, h), :], held[h], NT) * LN2).astype(bf16)


def back_biases(total, width):
    rows = [row_sum(fold_lanes(part.astype(f32))) for part in (total[:width], total[2 * width :])]
    return jnp.concatenate(rows + [jnp.zeros((6, width), f32)], axis=0)


def write_pieces(values, ref, here, at=0):
    span = ref.shape[2]
    for shift in range(ref.shape[0]):
        ref[here ^ shift, at] = values[:, shift * span : (shift + 1) * span].T


def copies_of(sources, targets, sem):
    return [pltpu.make_async_copy(a, b, sem.at[i]) for i, (a, b) in enumerate(zip(sources, targets))]


def whole_kernel(here_ref, *refs, pieces, carried, after):
    take = Taker(refs)
    piece_refs = take(pieces)
    aug_ref, cols, wq, wk, wv = take(5)
    weights_hbm = take(7)
    sums_hbm = take(4 if carried else 0)
    bias_in = take(2 if carried else 0)
    take(1 if carried else 0)
    take(after)
    (out_ref,) = take(1)
    sums_out = take(4)
    bias_out = take(2)
    saved, p_all, att_ref, stat_ref, og_ref, delta_ref, gres_ref, grads, held = take(9)
    weights = take(7)
    sums = take(4)
    small_ref, weight_sem, sum_sem, out_sem = take(4)
    step = pl.program_id(0)
    width = att_ref.shape[0]
    weight_copies = copies_of(weights_hbm, weights, weight_sem)
    sum_copies = copies_of(sums_hbm, sums, sum_sem)
    out_copies = copies_of(sums, sums_out, out_sem)

    @pl.when(step == 0)
    def _():
        for copy in weight_copies + sum_copies:
            copy.start()
        project_row(piece_refs, cols, wq, wk, wv, saved, small_ref)

    @pl.when(step < GROUPS)
    def _():
        attend_heads(step, saved, aug_ref, lambda h: p_all.at[step * PER_GROUP + h], att_ref, stat_ref, small_ref)

    @pl.when(step == GROUPS - 1)
    def _():
        for copy in weight_copies[:6] + sum_copies[:3]:
            copy.wait()
        total = dense_row(
            piece_refs, cols, saved, att_ref, stat_ref, weights[:6], sums[:3], carried,
            lambda values: write_pieces(values, out_ref, here_ref[0], 0), lambda number: out_copies[number].start(),
            og_ref, delta_ref, gres_ref,
        )
        bias_out[0][...] = total + bias_in[0][...] if carried else total

    @pl.when(step >= GROUPS)
    def _():
        group = step - GROUPS
        back_heads(group, saved, og_ref, delta_ref, lambda h: p_all.at[group * PER_GROUP + h], grads, held)

    @pl.when(step == 2 * GROUPS - 1)
    def _():
        for copy in weight_copies[6:] + sum_copies[3:]:
            copy.wait()
        total = grads[...]
        acc = dot(saved[3], total, NT)
        sums[3][...] = sums[3][...] + acc if carried else acc
        out_copies[3].start()
        bias = back_biases(total, width)
        bias_out[1][...] = bias + bias_in[1][...] if carried else bias
        result = (gres_ref[...] + dot(weights[6][...], total)).astype(bf16)
        write_pieces(result, out_ref, here_ref[0], 1)
        for copy in out_copies:
            copy.wait()


def whole(here, pieces, row, height, aug, cols, wqkv, weights, carried, after):
    _, span, width = pieces[0].shape
    count = len(pieces)
    length = span * count
    ff = weights[3].shape[1]
    full = lambda shape: pl.BlockSpec(shape, lambda g, i: (0,) * len(shape))
    sum_shapes = [(ff, width), (width, ff), (width, width), (width, 3 * width)]
    bias_shapes = [(16, width), (8, width)]
    first = 1 + count + 5 + 7
    out = pl.pallas_call(
        functools.partial(whole_kernel, pieces=count, carried=bool(carried), after=len(after)),
        grid_spec=pltpu.PrefetchScalarGridSpec(
            num_scalar_prefetch=1,
            grid=(2 * GROUPS,),
            in_specs=[full((2, span, width))] * count
            + [pl.BlockSpec((1, 2 * AUG, length), lambda g, i: (row, 0, 0)), full(cols.shape)]
            + [full(w.shape) for w in wqkv]
            + [ANY] * 7
            + ([ANY] * 4 + [full(s) for s in bias_shapes] + [ANY] if carried else [])
            + [ANY] * len(after),
            out_specs=[pl.BlockSpec((count, 2, span, width), lambda g, i: (0, row, 0, 0))]
            + [ANY] * 4
            + [full(s) for s in bias_shapes],
            scratch_shapes=[
                pltpu.VMEM((4, width, length), bf16),
                pltpu.VMEM((HEADS, length, length), bf16),
                pltpu.VMEM((width, length), f32),
                pltpu.VMEM((16, length), f32),
                pltpu.VMEM((width, length), bf16),
                pltpu.VMEM((16, length), f32),
                pltpu.VMEM((width, length), f32),
                pltpu.VMEM((3 * width, length), bf16),
                pltpu.VMEM((PER_GROUP, length, length), bf16),
            ]
            + [pltpu.VMEM(w.shape, bf16) for w in weights]
            + [pltpu.VMEM(s, f32) for s in sum_shapes]
            + [
                pltpu.SMEM((1,), jnp.int32),
                pltpu.SemaphoreType.DMA((7,)),
                pltpu.SemaphoreType.DMA((4,)),
                pltpu.SemaphoreType.DMA((4,)),
            ],
        ),
        out_shape=[jax.ShapeDtypeStruct((count, height, span, width), bf16)]
        + [jax.ShapeDtypeStruct(s, f32) for s in sum_shapes + bias_shapes],
        input_output_aliases={first + 6: 0} if carried else {},
        compiler_params=pltpu.CompilerParams(vmem_limit_bytes=VMEM_LIMIT),
        cost_estimate=cost(20),
        name="whole",
    )(here, *pieces, aug, cols, *wqkv, *weights, *carried, *after)
    return out[1:], out[0]


def layer_kernel(index_ref, *refs, pieces, carried, after, parts, inner):
    take = Taker(refs)
    piece_refs = take(pieces)
    aug_ref, cols, wq, wk, wv = take(5)
    weights_hbm = take(6)
    sums_hbm = take(3 if carried else 0)
    bias_in = take(1 if carried else 0)
    take((1 if carried else 0) + after)
    (out_ref,) = take(1)
    saved_hbm, p_hbm, og_ref, delta_ref, gres_ref = take(5)
    part_refs = take(parts)
    saved, p_buf, att_ref, stat_ref = take(4)
    weights = take(6)
    sums = take(3)
    packed, small_ref, weight_sem, sum_sem, p_sem, saved_sem = take(6)
    group = pl.program_id(0)
    width = att_ref.shape[0]
    weight_copies = copies_of(weights_hbm, weights, weight_sem)
    sum_copies = copies_of(sums_hbm, sums, sum_sem)
    saved_copy = pltpu.make_async_copy(saved, saved_hbm, saved_sem)
    slot = lax.rem(group, 2)

    def p_copy(number):
        start = number * PER_GROUP
        return pltpu.make_async_copy(
            p_buf.at[lax.rem(number, 2)], p_hbm.at[pl.ds(start, PER_GROUP)], p_sem.at[lax.rem(number, 2)]
        )

    @pl.when(group == 0)
    def _():
        for copy in weight_copies + sum_copies:
            copy.start()
        project_row(piece_refs, cols, wq, wk, wv, saved, small_ref)
        saved_copy.start()

    @pl.when(group >= 2)
    def _():
        p_copy(group - 2).wait()

    attend_heads(group, saved, aug_ref, lambda h: p_buf.at[slot, h], att_ref, stat_ref, small_ref)
    p_copy(group).start()

    @pl.when(group == GROUPS - 1)
    def _():
        for copy in weight_copies + sum_copies:
            copy.wait()
        total = dense_row(
            piece_refs, cols, saved, att_ref, stat_ref, weights, sums, carried,
            lambda values: write_pieces(values, out_ref, index_ref[1]), lambda number: None, og_ref, delta_ref, gres_ref,
        )
        if carried:
            total = total + bias_in[0][...]
        acc_dn, acc_up, acc_out = sums
        ff = acc_dn.shape[0]
        packed[:ff] = acc_dn[...].astype(bf16)
        for index in range(ff // width):
            packed[ff + index * width : ff + (index + 1) * width] = acc_up[
                :, index * width : (index + 1) * width
            ].astype(bf16)
        packed[2 * ff : 2 * ff + width] = acc_out[...].astype(bf16)
        packed[2 * ff + width : 2 * ff + width + 16] = total.astype(bf16)
        rest = packed.shape[0] - 2 * ff - width - 16
        if rest:
            packed[2 * ff + width + 16 :] = jnp.zeros((rest, width), bf16)
        emit(packed, index_ref[0], part_refs, inner)
        saved_copy.wait()
        for number in range(max(GROUPS - 2, 0), GROUPS):
            p_copy(number).wait()


def layer(pieces, row, height, aug, cols, wqkv, weights, sums, packed_rows, parts, inner, index, after):
    _, span, width = pieces[0].shape
    count = len(pieces)
    length = span * count
    ff = weights[3].shape[1]
    full = lambda shape: pl.BlockSpec(shape, lambda g, i: (0,) * len(shape))
    sum_shapes = [(ff, width), (width, ff), (width, width)]
    part = (packed_rows // parts, width)
    out = pl.pallas_call(
        functools.partial(
            layer_kernel, pieces=count, carried=bool(sums), after=len(after), parts=parts, inner=inner
        ),
        grid_spec=pltpu.PrefetchScalarGridSpec(
            num_scalar_prefetch=1,
            grid=(GROUPS,),
            in_specs=[full((2, span, width))] * count
            + [pl.BlockSpec((1, 2 * AUG, length), lambda g, i: (row, 0, 0)), full(cols.shape)]
            + [full(w.shape) for w in wqkv]
            + [ANY] * 6
            + ([ANY] * 3 + [full((16, width)), ANY] if sums else [])
            + [ANY] * len(after),
            out_specs=[pl.BlockSpec((count, 1, span, width), lambda g, i: (0, height - 1, 0, 0))]
            + [ANY, ANY, full((width, length)), full((16, length)), full((width, length))]
            + [full(part)] * parts,
            scratch_shapes=[
                pltpu.VMEM((4, width, length), bf16),
                pltpu.VMEM((2, PER_GROUP, length, length), bf16),
                pltpu.VMEM((width, length), f32),
                pltpu.VMEM((16, length), f32),
            ]
            + [pltpu.VMEM(w.shape, bf16) for w in weights]
            + [pltpu.VMEM(shape, f32) for shape in sum_shapes]
            + [
                pltpu.VMEM((packed_rows, width), bf16),
                pltpu.SMEM((1,), jnp.int32),
                pltpu.SemaphoreType.DMA((6,)),
                pltpu.SemaphoreType.DMA((3,)),
                pltpu.SemaphoreType.DMA((2,)),
                pltpu.SemaphoreType.DMA,
            ],
        ),
        out_shape=[jax.ShapeDtypeStruct((count, height, span, width), bf16)]
        + [
            jax.ShapeDtypeStruct((4, width, length), bf16),
            jax.ShapeDtypeStruct((HEADS, length, length), bf16),
            jax.ShapeDtypeStruct((width, length), bf16),
            jax.ShapeDtypeStruct((16, length), f32),
            jax.ShapeDtypeStruct((width, length), f32),
        ]
        + [jax.ShapeDtypeStruct(part, bf16)] * parts,
        input_output_aliases={1 + count + 5 + 6 + 4: 0} if sums else {},
        compiler_params=pltpu.CompilerParams(vmem_limit_bytes=VMEM_LIMIT),
        cost_estimate=cost(14),
        name="layer",
    )(index, *pieces, aug, cols, *wqkv, *weights, *sums, *after)
    return out[0], out[1:6], out[6:]


def back_kernel(index_ref, *refs, carried, after, parts, inner):
    take = Taker(refs)
    saved, og_ref, delta_ref, p_ref, saved_hbm, gres_hbm, w_hbm = take(7)
    sum_hbm = take(1 if carried else 0)
    bias_in = take(1 if carried else 0)
    take(after)
    (out_ref,) = take(1)
    part_refs = take(parts)
    grads, held, xt, gres, w_all = take(5)
    sum_in = take(1 if carried else 0)
    packed, sem = take(2)
    group = pl.program_id(0)
    width = og_ref.shape[0]
    copies = copies_of([saved_hbm.at[3], gres_hbm, w_hbm] + sum_hbm, [xt, gres, w_all] + sum_in, sem)

    @pl.when(group == 0)
    def _():
        for copy in copies:
            copy.start()

    back_heads(group, saved, og_ref, delta_ref, lambda h: p_ref.at[h], grads, held)

    @pl.when(group == GROUPS - 1)
    def _():
        for copy in copies:
            copy.wait()
        total = grads[...]
        acc = dot(xt[...], total, NT)
        bias = back_biases(total, width)
        if carried:
            acc = acc + sum_in[0][...]
            bias = bias + bias_in[0][...]
        per = width // 128
        for index in range(3 * per):
            packed[index * width : (index + 1) * width] = acc[:, index * 128 : (index + 1) * 128].astype(bf16)
        bias_rows = [bias[n : n + 1, i * 128 : (i + 1) * 128] for n in range(2) for i in range(per)]
        tail = packed.shape[0] - 3 * per * width
        bias_rows.append(jnp.zeros((tail - len(bias_rows), 128), f32))
        packed[3 * per * width :] = jnp.concatenate(bias_rows, axis=0).astype(bf16)
        emit(packed, index_ref[0], part_refs, inner)
        write_pieces((gres[...] + dot(w_all[...], total)).astype(bf16), out_ref, index_ref[1])


def back(count, saved, probs, og, delta, gres, w_all, sums, packed_rows, parts, inner, index, after):
    _, width, length = saved.shape
    span = length // count
    full = lambda shape: pl.BlockSpec(shape, lambda g, i: (0,) * len(shape))
    part = (packed_rows // parts, 128)
    out = pl.pallas_call(
        functools.partial(back_kernel, carried=bool(sums), after=len(after), parts=parts, inner=inner),
        grid_spec=pltpu.PrefetchScalarGridSpec(
            num_scalar_prefetch=1,
            grid=(GROUPS,),
            in_specs=[
                full((3, width, length)),
                full((width, length)),
                full((16, length)),
                pl.BlockSpec((PER_GROUP, length, length), lambda g, i: (g, 0, 0)),
            ]
            + [ANY] * 3
            + ([ANY, full((8, width))] if sums else [])
            + [ANY] * len(after),
            out_specs=[full((count, 1, span, width))] + [full(part)] * parts,
            scratch_shapes=[
                pltpu.VMEM((3 * width, length), bf16),
                pltpu.VMEM((PER_GROUP, length, length), bf16),
                pltpu.VMEM((width, length), bf16),
                pltpu.VMEM((width, length), f32),
                pltpu.VMEM(w_all.shape, bf16),
            ]
            + ([pltpu.VMEM((width, 3 * width), f32)] if sums else [])
            + [pltpu.VMEM((packed_rows, 128), bf16), pltpu.SemaphoreType.DMA((4,))],
        ),
        out_shape=[jax.ShapeDtypeStruct((count, 1, span, width), bf16)] + [jax.ShapeDtypeStruct(part, bf16)] * parts,
        compiler_params=pltpu.CompilerParams(vmem_limit_bytes=VMEM_LIMIT),
        cost_estimate=cost(9),
        name="back",
    )(index, saved, og, delta, probs, saved, gres, w_all, *sums, *after)
    return out[0], out[1:]


def exchange(pieces, axis, devices, unit=1):
    moved = [pieces[0]]
    for shift in range(1, len(pieces)):
        moved.append(lax.ppermute(pieces[shift], axis, [(i, i ^ (shift * unit)) for i in range(devices)]))
    return moved


def tree_sum(blocks):
    while len(blocks) > 1:
        blocks = [left + right for left, right in zip(blocks[::2], blocks[1::2])]
    return blocks[0]


def combine_kernel(index_ref, *refs, inputs, after, inner):
    total = tree_sum([ref[...].astype(f32) for ref in refs[:inputs]]).astype(bf16)
    outs = refs[inputs + after :]
    if len(outs) == 1:
        outs[0][...] = total
    else:
        packed = outs[-1]
        packed[...] = total
        emit(packed, index_ref[0], outs[:-1], inner)


def combine(blocks, parts, inner, index, after=()):
    rows, width = blocks[0].shape
    part = (rows // parts, width)
    full = lambda s: pl.BlockSpec(s, lambda i, j: (0, 0))
    return pl.pallas_call(
        functools.partial(combine_kernel, inputs=len(blocks), after=len(after), inner=inner),
        grid_spec=pltpu.PrefetchScalarGridSpec(
            num_scalar_prefetch=1,
            grid=(1,),
            in_specs=[full((rows, width))] * len(blocks) + [pl.BlockSpec(memory_space=pl.ANY)] * len(after),
            out_specs=[full(part)] * parts,
            scratch_shapes=[pltpu.VMEM((rows, width), bf16)] if parts > 1 else [],
        ),
        out_shape=[jax.ShapeDtypeStruct(part, bf16)] * parts,
        compiler_params=pltpu.CompilerParams(vmem_limit_bytes=VMEM_LIMIT),
        cost_estimate=cost(1),
        name="combine",
    )(index, *blocks, *after)


def merge_kernel(index_ref, *refs, count, after, parts, inner):
    left = tree_sum([ref[...].astype(f32) for ref in refs[:count]])
    right = tree_sum([ref[...].astype(f32) for ref in refs[count : 2 * count]])
    packed = refs[-1]
    packed[...] = jnp.concatenate([left, right], axis=1).astype(bf16)
    emit(packed, index_ref[0], refs[2 * count + after : -1], inner)


def merge(lefts, rights, stage, after=()):
    rows, left = lefts[0].shape
    width = left + rights[0].shape[1]
    parts = stage[3]
    full = lambda s: pl.BlockSpec(s, lambda i, j: (0, 0))
    return pl.pallas_call(
        functools.partial(merge_kernel, count=len(lefts), after=len(after), parts=parts, inner=stage[4]),
        grid_spec=pltpu.PrefetchScalarGridSpec(
            num_scalar_prefetch=1,
            grid=(1,),
            in_specs=[full(b.shape) for b in list(lefts) + list(rights)] + [ANY] * len(after),
            out_specs=[full((rows // parts, width))] * parts,
            scratch_shapes=[pltpu.VMEM((rows, width), bf16)],
        ),
        out_shape=[jax.ShapeDtypeStruct((rows // parts, width), bf16)] * parts,
        compiler_params=pltpu.CompilerParams(vmem_limit_bytes=VMEM_LIMIT),
        cost_estimate=cost(2),
        name="merge",
    )(place_of(stage), *lefts, *rights, *after)


def put_together(refs, out, index, inner):
    size = refs[0].shape[0] // inner
    for shift, ref in enumerate(refs):
        for block in range(inner):
            start = pl.multiple_of((block * len(refs) + (index ^ shift)) * size, 16)
            out[pl.ds(start, size), :] = ref[block * size : (block + 1) * size]


def assemble_kernel(index_ref, *refs, inputs, after, inner):
    put_together(refs[:inputs], refs[inputs + after], index_ref[0], inner)


def assemble(blocks, stage, after=(), through=()):
    rows, width = blocks[0].shape
    full = lambda s: pl.BlockSpec(s, lambda i, j: (0, 0))
    shape = (rows * len(blocks), width)
    first = 1 + len(blocks) + len(after)
    after = list(after) + list(through)
    out = pl.pallas_call(
        functools.partial(assemble_kernel, inputs=len(blocks), after=len(after), inner=stage[4]),
        grid_spec=pltpu.PrefetchScalarGridSpec(
            num_scalar_prefetch=1,
            grid=(1,),
            in_specs=[full((rows, width))] * len(blocks) + [ANY] * len(after),
            out_specs=[full(shape)] + [ANY] * len(through),
        ),
        out_shape=[jax.ShapeDtypeStruct(shape, bf16)] + [jax.ShapeDtypeStruct(a.shape, a.dtype) for a in through],
        input_output_aliases={first + i: 1 + i for i in range(len(through))},
        compiler_params=pltpu.CompilerParams(vmem_limit_bytes=VMEM_LIMIT),
        cost_estimate=cost(1),
        name="assemble",
    )(place_of(stage), *blocks, *after)
    return out[0], out[1:]


def place_kernel(*refs, rows):
    outs = refs[-2:]
    row = pl.program_id(0)
    for number in range(rows):

        @pl.when(row == number)
        def _(number=number):
            for which in range(2):
                outs[which][...] = refs[2 * number + which][...].astype(outs[which].dtype)


def place(sources):
    rows = len(sources)
    count, _, span, width = sources[0][0][0].shape
    shape = (count, rows, span, width)
    in_specs = []
    arrays = []
    for row in sources:
        for sent, at in row:
            in_specs.append(pl.BlockSpec((count, 1, span, width), lambda r, at=at: (0, at, 0, 0)))
            arrays.append(sent)
    out_spec = pl.BlockSpec((count, 1, span, width), lambda r: (0, r, 0, 0))
    layer_out, grad = pl.pallas_call(
        functools.partial(place_kernel, rows=rows),
        grid=(rows,),
        in_specs=in_specs,
        out_specs=[out_spec, out_spec],
        out_shape=[jax.ShapeDtypeStruct(shape, bf16), jax.ShapeDtypeStruct(shape, f32)],
        compiler_params=pltpu.CompilerParams(vmem_limit_bytes=VMEM_LIMIT),
        cost_estimate=cost(5),
        name="place",
    )(*arrays)
    return layer_out.reshape(count * rows, span, width), grad.reshape(count * rows, span, width)


def sum_stages(sizes):
    stages = []
    for axis in ("rows", "seq"):
        devices = sizes[axis]
        unit = 1
        while unit < devices:
            size = 2 if unit == 1 and devices.bit_length() % 2 == 0 else 4
            stages.append((axis, devices, unit, size, devices // (unit * size)))
            unit *= size
    return stages


def place_of(stage):
    axis, _, unit, size, _ = stage
    return ((lax.axis_index(axis) // unit) % size).astype(jnp.int32).reshape(1)


def send_parts(parts, stage):
    axis, devices, unit, _, _ = stage
    return exchange(parts, axis, devices, unit)


def cut_for(taken, stage, after=()):
    return combine(taken, stage[3], stage[4], place_of(stage), after)


def add(taken, after=()):
    return combine(taken, 1, 1, jnp.zeros((1,), jnp.int32), after)[0]


def unpack_kernel(index_ref, *refs, inputs, after, inner):
    down, up, out, *biases = refs[inputs + after : inputs + after + 10]
    query, key, value, bias_q, bias_v = refs[inputs + after + 10 : -1]
    block = refs[-1]
    put_together(refs[:inputs], block, index_ref[0], inner)
    ff, width = down.shape
    per = ff // width
    down[...] = block[:ff, :width].astype(f32)
    for index in range(per):
        rows = slice(ff + index * width, ff + (index + 1) * width)
        up[:, index * width : (index + 1) * width] = block[rows, :width].astype(f32)
    out[...] = block[2 * ff : 2 * ff + width, :width].astype(f32)
    rows = block[2 * ff + width : 2 * ff + width + 16, :width].astype(f32)
    for index, ref in enumerate(biases[:-1]):
        ref[...] = rows[index]
    biases[-1][...] = jnp.concatenate([rows[len(biases) - 1 + i] for i in range(per)], axis=0)
    per = width // 128
    for number, ref in enumerate((query, key, value)):
        for index in range(per):
            start = (number * per + index) * width
            ref[:, index * 128 : (index + 1) * 128] = block[start : start + width, width:].astype(f32)
    rows = block[3 * per * width : 3 * per * width + 16, width:].astype(f32)
    for number, ref in enumerate((bias_q, bias_v)):
        ref[...] = jnp.concatenate([rows[number * per + i] for i in range(per)], axis=0)


def unpack(blocks, stage, shapes, after=()):
    rows, width = blocks[0].shape
    full = lambda s: pl.BlockSpec(s, lambda i, j: (0,) * len(s))
    return pl.pallas_call(
        functools.partial(unpack_kernel, inputs=len(blocks), after=len(after), inner=stage[4]),
        grid_spec=pltpu.PrefetchScalarGridSpec(
            num_scalar_prefetch=1,
            grid=(1,),
            in_specs=[full((rows, width))] * len(blocks) + [ANY] * len(after),
            out_specs=[full(s) for s in shapes],
            scratch_shapes=[pltpu.VMEM((rows * len(blocks), width), bf16)],
        ),
        out_shape=[jax.ShapeDtypeStruct(s, f32) for s in shapes],
        compiler_params=pltpu.CompilerParams(vmem_limit_bytes=VMEM_LIMIT),
        cost_estimate=cost(4),
        name="unpack",
    )(place_of(stage), *blocks, *after)


def round_up(value, unit):
    return -(-value // unit) * unit


def body(
    tokens, lengths, w_query, b_query, w_key, w_value, b_value, w_out, b_out, gain_attn, shift_attn,
    w_up, b_up, w_down, b_down, gain_ffn, shift_ffn, cotangent, *, sizes,
):
    count = sizes["seq"]
    devices = count * sizes["rows"]
    row_count, span, width = tokens.shape
    ff = w_up.shape[1]
    length = span * count
    rows = row_count // count
    me = lax.axis_index("seq")
    here = me.astype(jnp.int32).reshape(1)
    order = me ^ jnp.arange(count, dtype=jnp.int32)
    stages = sum_stages(sizes)
    row_stages, seq_stages = [[stage for stage in stages if stage[0] == axis] for axis in ("rows", "seq")]
    first = stages[0]
    index = place_of(first)
    later_rows = round_up(2 * ff + width + 16, 16 * devices)
    first_rows = later_rows

    picked = {0: pick(tokens, cotangent, count, rows, 0, here, [])}
    given = {0: exchange(picked[0], "seq", count)}

    bounds = lax.dynamic_slice_in_dim(jnp.cumsum(lengths, axis=1), me * rows, rows, 0)
    places = (order[:, None] * span + jnp.arange(span, dtype=jnp.int32)[None, :]).reshape(length)
    segment = jnp.sum((places[None, None, :] >= bounds[:, :, None]).astype(jnp.int32), axis=1)
    ids = jnp.arange(2 * AUG, dtype=jnp.int32)[None, :, None]
    same = segment[:, None, :] == ids % AUG
    aug = jnp.where(ids < AUG, jnp.where(same, 1.0, 0.0), jnp.where(same | (ids % AUG >= lengths.shape[1]), 0.0, -BIG))
    aug = aug.astype(bf16)

    vectors = [b_query, b_value, b_out, gain_attn, shift_attn, b_down, gain_ffn, shift_ffn]
    vectors = jnp.concatenate([jnp.stack(vectors), b_up.reshape(-1, width)], axis=0)
    wq_t, wk_t, wv_t, wo_t, wup_t, wdn_t, cols = prepare((w_query, w_key, w_value, w_out, w_up, w_down), vectors)
    dense_weights = (wo_t, w_out, wup_t, w_up, wdn_t, w_down)
    w_all = jnp.concatenate([w_query, w_key, w_value], axis=1)

    wqkv = (wq_t, wk_t, wv_t)
    last = rows - 1

    def send_row(row, after):
        if row > last:
            return []
        picked[row] = pick(tokens, cotangent, count, rows, row, here, list(given[row - 1][1:]) + after)
        given[row] = exchange(picked[row], "seq", count)
        return picked[row][:1]

    both = jnp.concatenate([index, here])
    carried, shared = [], None
    for row in range(last):
        after = send_row(row + 1, [] if shared is None else [shared])
        sums, shared = whole(here, given[row], row, 2 * last + 1, aug, cols, wqkv, dense_weights + (w_all,), carried, after)
        carried = list(sums) + [shared]

    def return_pieces(array):
        return lax.all_to_all(array, "seq", 0, 0, tiled=True)

    shared, saved, later = layer(
        given[last], last, 2 * last + 1, aug, cols, wqkv, dense_weights,
        (carried[:3] + carried[4:5] + carried[6:]) if carried else [], later_rows,
        first[3], first[4], both, [],
    )
    keys, probs, og, delta, gres = saved
    taken = send_parts(later, first)
    moved = return_pieces(shared)
    ends, early = back(
        count, keys, probs, og, delta, gres, w_all, (carried[3:4] + carried[5:6]) if carried else [], first_rows,
        first[3], first[4], both, [],
    )
    parts = early
    after = list(early[:1])
    for stage in row_stages[1:]:
        cut = cut_for(taken, stage, after)
        taken = send_parts(cut, stage)
        after = list(cut[:1])
    given_early = send_parts(early, first)
    for number, stage in enumerate(row_stages[1:]):
        parts = cut_for(given_early, stage, after)
        given_early = send_parts(parts, stage)
    parts = merge(taken, given_early, seq_stages[0], [moved])
    for number, stage in enumerate(seq_stages):
        taken = send_parts(parts, stage)
        if number + 1 < len(seq_stages):
            parts = cut_for(taken, seq_stages[number + 1])
    block = add(taken)
    for number, stage in enumerate(reversed(stages[1:])):
        taken = send_parts([block] * stage[3], stage)
        at_end = number == len(stages) - 2
        if at_end:
            ends = return_pieces(ends)
        block, passed = assemble(taken, stage, [ends] if at_end else [], [] if at_end else [ends])
        ends = passed[0] if passed else ends
    shapes = [(ff, width), (width, ff), (width, width)] + [(width,)] * 6 + [(ff,)] + [(width, width)] * 3 + [(width,)] * 2
    (
        grad_down, grad_up, grad_output, grad_gain2, grad_shift2, grad_dnbias, grad_gain1, grad_shift1, grad_obias,
        grad_upbias, grad_query, grad_key, grad_value, grad_qbias, grad_vbias,
    ) = unpack(send_parts([block] * first[3], first), first, shapes)
    layer_out, grad_tokens = place([((moved, 2 * row), (moved, 2 * row + 1)) for row in range(last)] + [((moved, 2 * last), (ends, 0))])
    return (
        layer_out, grad_tokens, grad_query, grad_qbias, grad_key, grad_value, grad_vbias, grad_output, grad_obias,
        grad_gain1, grad_shift1, grad_up, grad_upbias, grad_down, grad_dnbias, grad_gain2, grad_shift2,
    )


def solution(mesh):
    split = P("rows", "seq", None)
    in_specs = (split, P("rows", None)) + (P(),) * 15 + (split,)
    out_specs = (split, split) + (P(),) * 15
    sizes = dict(mesh.shape)
    return jax.shard_map(
        functools.partial(body, sizes=sizes), mesh=mesh, in_specs=in_specs, out_specs=out_specs, check_vma=False
    )
```

```python
import functools
import math

import jax
import jax.numpy as jnp
from jax import lax
from jax.experimental import pallas as pl
from jax.experimental.pallas import tpu as pltpu
from jax.sharding import PartitionSpec as P

HEADS = 12
HD = 32
GROUPS = 3
PER_GROUP = HEADS // GROUPS
AUG = 16
BIG = 2.0**100
SMALL_SCORE = 60.0
EPSILON = 1e-05
SCALE = HD ** (-0.5)
LOG2E = math.log2(math.e)
Q_FACTOR = SCALE * LOG2E
LN2 = math.log(2.0)
VMEM_LIMIT = 60 * 2**20

f32 = jnp.float32
bf16 = jnp.bfloat16
NN = (((1,), (0,)), ((), ()))
NT = (((1,), (1,)), ((), ()))
TN = (((0,), (0,)), ((), ()))


def dot(left, right, dims=NN):
    return lax.dot_general(left, right, dims, preferred_element_type=f32)


def fold_lanes(values):
    total = values[:, :128]
    for start in range(128, values.shape[1], 128):
        total = total + values[:, start : start + 128]
    return total


def row_sum(partial):
    return jnp.sum(partial.T, axis=0, keepdims=True)


def normalize(hidden):
    scale = 1.0 / hidden.shape[0]
    centre = hidden - jnp.sum(hidden, axis=0, keepdims=True) * scale
    variance = jnp.sum(centre * centre, axis=0, keepdims=True) * scale
    inverse = lax.rsqrt(variance + EPSILON)
    return centre * inverse, inverse


def normalize_back(upstream, scaled, inverse):
    scale = 1.0 / upstream.shape[0]
    mean = jnp.sum(upstream, axis=0, keepdims=True) * scale
    spread = jnp.sum(upstream * scaled, axis=0, keepdims=True) * scale
    return inverse * (upstream - mean - scaled * spread)


def gelu_parts(v):
    cdf = 0.5 + 0.5 * lax.erf(v * 0.5**0.5)
    bell = jnp.exp2((v * v) * (-0.5 * LOG2E))
    return v * cdf, cdf + v * bell * (2.0 * math.pi) ** (-0.5)


def prepare_kernel(*refs, through):
    sources, rows = refs[:6], refs[6]
    targets, columns = refs[8 + through : 14 + through], refs[14 + through]
    for source, target in zip(sources, targets):
        target[...] = source[...].T
    width = rows.shape[1]
    columns[...] = jnp.concatenate([rows[...], jnp.zeros((128 - rows.shape[0], width), f32)], axis=0).T


def prepare(weights, rows, aug, through):
    full = lambda shape: pl.BlockSpec(shape, lambda i: (0, 0))
    shapes = [w.shape[::-1] for w in weights]
    out = pl.pallas_call(
        functools.partial(prepare_kernel, through=len(through)),
        grid=(1,),
        in_specs=[full(w.shape) for w in weights] + [full(rows.shape)] + [ANY] * (1 + len(through)),
        out_specs=[full(s) for s in shapes] + [full((rows.shape[1], 128))] + [ANY] * len(through),
        out_shape=[jax.ShapeDtypeStruct(s, bf16) for s in shapes]
        + [jax.ShapeDtypeStruct((rows.shape[1], 128), f32)]
        + [jax.ShapeDtypeStruct(a.shape, a.dtype) for a in through],
        input_output_aliases={8 + i: 7 + i for i in range(len(through))},
        compiler_params=pltpu.CompilerParams(vmem_limit_bytes=VMEM_LIMIT),
        cost_estimate=cost(5),
        name="prepare",
    )(*weights, rows, aug, *through)
    return out[:7], out[7:]


def cost(micros):
    return pl.CostEstimate(flops=int(micros * 1e5), transcendentals=0, bytes_accessed=int(micros * 1e3))


B_QUERY, B_VALUE, B_OUT, GAIN1, SHIFT1, B_DOWN, GAIN2, SHIFT2, B_UP = range(9)


ANY = pl.BlockSpec(memory_space=pl.ANY)


def head_sums(values):
    return jnp.sum(values.reshape(HEADS, HD, values.shape[1]), axis=1)


def emit(packed, index, outs, inner):
    size = outs[0].shape[0] // inner
    for shift, ref in enumerate(outs):
        for block in range(inner):
            start = pl.multiple_of((block * len(outs) + (index ^ shift)) * size, 16)
            ref[block * size : (block + 1) * size] = packed[pl.ds(start, size), :]


class Taker:
    def __init__(self, refs):
        self.refs = list(refs)

    def __call__(self, number):
        taken = self.refs[:number]
        del self.refs[:number]
        return taken


def column_of(cols, index):
    return cols[:, index : index + 1]


def project_row(piece_ref, cols, wq, wk, wv, saved, small_ref):
    xt = jnp.concatenate([piece_ref[i, 0].T for i in range(piece_ref.shape[0])], axis=1)
    query = (dot(wq[...], xt) + column_of(cols, B_QUERY)) * Q_FACTOR
    key = dot(wk[...], xt)
    saved[0] = query.astype(bf16)
    saved[1] = key.astype(bf16)
    saved[2] = (dot(wv[...], xt) + column_of(cols, B_VALUE)).astype(bf16)
    saved[3] = xt
    bounds = [
        jnp.max(head_sums(query * query), axis=1, keepdims=True),
        jnp.max(head_sums(key * key), axis=1, keepdims=True),
    ]
    small_ref[0] = (jnp.max(bounds[0] * bounds[1]) < SMALL_SCORE**2).astype(jnp.int32)


def head_rows(group, h):
    return pl.ds(pl.multiple_of((group * PER_GROUP + h) * HD, HD), HD)


def attend_heads(group, saved, aug_ref, probs, att_ref, stat_ref, small_ref):
    length = saved.shape[2]
    ones = jnp.ones((AUG, length), bf16)

    def score(h):
        keys = jnp.concatenate([saved[1, head_rows(group, h), :], aug_ref[0, AUG:]], axis=0)
        query = jnp.concatenate([saved[0, head_rows(group, h), :], aug_ref[0, :AUG]], axis=0)
        return dot(keys, query, TN)

    def mix(h):
        values = jnp.concatenate([saved[2, head_rows(group, h), :], ones], axis=0)
        mixed = dot(values, probs(h)[...])
        inverse = 1.0 / mixed[HD : HD + 1]
        att_ref[head_rows(group, h), :] = mixed[:HD] * inverse
        stat_ref[pl.ds(group * PER_GROUP + h, 1), :] = inverse

    def heads(shifted):
        scores = score(0)
        for h in range(PER_GROUP):
            following = score(h + 1) if h + 1 < PER_GROUP else None
            if h >= 1:
                mix(h - 1)
            if shifted:
                scores = scores - jnp.max(scores, axis=0, keepdims=True)
            probs(h)[...] = jnp.exp2(scores).astype(bf16)
            scores = following
        mix(PER_GROUP - 1)

    @pl.when(small_ref[0] == 1)
    def _():
        heads(False)

    @pl.when(small_ref[0] == 0)
    def _():
        heads(True)


def dense_row(piece_ref, cols, saved, att_ref, stat_ref, weights, sums, carried, write_out, summed, og_ref, delta_ref, gres_ref):
    wo_t, wo, wup_t, wup, wdn_t, wdn = weights
    acc_dn, acc_up, acc_out = sums
    ff = acc_dn.shape[0]
    width = att_ref.shape[0]

    def column(index):
        return column_of(cols, index)

    def add(number, value):
        ref = sums[number]
        ref[...] = ref[...] + value if carried else value
        summed(number)

    att = att_ref[...]
    att_b = att.astype(bf16)
    res1 = saved[3].astype(f32) + dot(wo_t[...], att_b) + column(B_OUT)
    scaled1, inverse1 = normalize(res1)
    normed = scaled1 * column(GAIN1) + column(SHIFT1)
    normed_b = normed.astype(bf16)
    b_up = jnp.concatenate([column(B_UP + i) for i in range(ff // width)], axis=0)
    act, slope = gelu_parts(dot(wup_t[...], normed_b) + b_up)
    act_b = act.astype(bf16)
    res2 = normed + dot(wdn_t[...], act_b) + column(B_DOWN)
    scaled2, inverse2 = normalize(res2)
    write_out((scaled2 * column(GAIN2) + column(SHIFT2)).astype(bf16))
    cot = jnp.concatenate([piece_ref[i, 1].T for i in range(piece_ref.shape[0])], axis=1).astype(f32)
    gres2 = normalize_back(cot * column(GAIN2), scaled2, inverse2)
    down_b = gres2.astype(bf16)
    up_b = (dot(wdn[...], down_b) * slope).astype(bf16)
    add(0, dot(act_b, down_b, NT))
    gnormed = gres2 + dot(wup[...], up_b)
    add(1, dot(normed_b, up_b, NT))
    gres1 = normalize_back(gnormed * column(GAIN1), scaled1, inverse1)
    gres_ref[...] = gres1
    branch_b = gres1.astype(bf16)
    og = dot(wo[...], branch_b)
    add(2, dot(att_b, branch_b, NT))
    for h in range(HEADS):
        part = slice(h * HD, (h + 1) * HD)
        scaled_og = (og[part] * stat_ref[h : h + 1, :]).astype(bf16)
        og_ref[part, :] = scaled_og
        delta_ref[h : h + 1, :] = jnp.sum(scaled_og.astype(f32) * att[part], axis=0, keepdims=True)
    biases = [cot * scaled2, cot, down_b.astype(f32), gnormed * scaled1, gnormed, branch_b.astype(f32)]
    bias_rows = [row_sum(fold_lanes(value)) for value in biases]
    up_sum = fold_lanes(up_b.astype(f32))
    bias_rows += [row_sum(up_sum[i * width : (i + 1) * width]) for i in range(ff // width)]
    bias_rows.append(jnp.zeros((16 - len(bias_rows), width), f32))
    return jnp.concatenate(bias_rows, axis=0)


def back_heads(group, saved, og_ref, delta_ref, probs, grads, held):
    length = og_ref.shape[1]
    width = og_ref.shape[0]
    sign = jnp.where(lax.broadcasted_iota(jnp.int32, (AUG, length), 0) < 3, 1.0, 0.0).astype(bf16)

    def grad_probs(h):
        delta = delta_ref[pl.ds(group * PER_GROUP + h, 1), :]
        first = delta.astype(bf16)
        rest = delta - first.astype(f32)
        second = rest.astype(bf16)
        third = (rest - second.astype(f32)).astype(bf16)
        aug = jnp.concatenate(
            [-first.astype(f32), -second.astype(f32), -third.astype(f32), jnp.zeros((AUG - 3, length), f32)], axis=0
        ).astype(bf16)
        left = jnp.concatenate([saved[2, head_rows(group, h), :], sign], axis=0)
        right = jnp.concatenate([og_ref[head_rows(group, h), :], aug], axis=0)
        return dot(left, right, TN)

    def target(which, h):
        return pl.ds(pl.multiple_of(which * width + (group * PER_GROUP + h) * HD, HD), HD)

    for h in range(PER_GROUP):
        held[h] = (probs(h)[...].astype(f32) * grad_probs(h)).astype(bf16)
        grads[target(2, h), :] = dot(og_ref[head_rows(group, h), :], probs(h)[...], NT).astype(bf16)
    for h in range(PER_GROUP):
        grads[target(0, h), :] = (dot(saved[1, head_rows(group, h), :], held[h]) * SCALE).astype(bf16)
        grads[target(1, h), :] = (dot(saved[0, head_rows(group, h), :], held[h], NT) * LN2).astype(bf16)


def back_biases(total, width):
    rows = [row_sum(fold_lanes(part.astype(f32))) for part in (total[:width], total[2 * width :])]
    return jnp.concatenate(rows + [jnp.zeros((6, width), f32)], axis=0)


def write_pieces(values, ref, at=0):
    span = ref.shape[2]
    for piece in range(ref.shape[0]):
        ref[piece, at] = values[:, piece * span : (piece + 1) * span].T


def copies_of(sources, targets, sem):
    return [pltpu.make_async_copy(a, b, sem.at[i]) for i, (a, b) in enumerate(zip(sources, targets))]


def whole_kernel(*refs, carried, through):
    take = Taker(refs)
    (piece_ref,) = take(1)
    aug_ref, cols, wq, wk, wv = take(5)
    weights_hbm = take(7)
    sums_hbm = take(4 if carried else 0)
    bias_in = take(2 if carried else 0)
    take((1 if carried else 0) + through)
    (out_ref,) = take(1)
    sums_out = take(4)
    bias_out = take(2)
    take(through)
    saved, p_all, att_ref, stat_ref, og_ref, delta_ref, gres_ref, grads, held = take(9)
    weights = take(7)
    sums = take(4)
    small_ref, weight_sem, sum_sem, out_sem = take(4)
    step = pl.program_id(0)
    width = att_ref.shape[0]
    weight_copies = copies_of(weights_hbm, weights, weight_sem)
    sum_copies = copies_of(sums_hbm, sums, sum_sem)
    out_copies = copies_of(sums, sums_out, out_sem)

    @pl.when(step == 0)
    def _():
        for copy in weight_copies + sum_copies:
            copy.start()
        project_row(piece_ref, cols, wq, wk, wv, saved, small_ref)

    @pl.when(step < GROUPS)
    def _():
        attend_heads(step, saved, aug_ref, lambda h: p_all.at[step * PER_GROUP + h], att_ref, stat_ref, small_ref)

    @pl.when(step == GROUPS - 1)
    def _():
        for copy in weight_copies[:6] + sum_copies[:3]:
            copy.wait()
        total = dense_row(
            piece_ref, cols, saved, att_ref, stat_ref, weights[:6], sums[:3], carried,
            lambda values: write_pieces(values, out_ref, 0), lambda number: out_copies[number].start(),
            og_ref, delta_ref, gres_ref,
        )
        bias_out[0][...] = total + bias_in[0][...] if carried else total

    @pl.when(step >= GROUPS)
    def _():
        group = step - GROUPS
        back_heads(group, saved, og_ref, delta_ref, lambda h: p_all.at[group * PER_GROUP + h], grads, held)

    @pl.when(step == 2 * GROUPS - 1)
    def _():
        for copy in weight_copies[6:] + sum_copies[3:]:
            copy.wait()
        total = grads[...]
        acc = dot(saved[3], total, NT)
        sums[3][...] = sums[3][...] + acc if carried else acc
        out_copies[3].start()
        bias = back_biases(total, width)
        bias_out[1][...] = bias + bias_in[1][...] if carried else bias
        result = (gres_ref[...] + dot(weights[6][...], total)).astype(bf16)
        write_pieces(result, out_ref, 1)
        for copy in out_copies:
            copy.wait()


def whole(pieces, row, height, aug, cols, wqkv, weights, carried, through):
    count, _, span, width = pieces.shape
    length = span * count
    ff = weights[3].shape[1]
    full = lambda shape: pl.BlockSpec(shape, lambda g: (0,) * len(shape))
    sum_shapes = [(ff, width), (width, ff), (width, width), (width, 3 * width)]
    bias_shapes = [(16, width), (8, width)]
    first = 1 + 5 + 7 + len(carried)
    aliases = {first + i: 7 + i for i in range(len(through))}
    out = pl.pallas_call(
        functools.partial(whole_kernel, carried=bool(carried), through=len(through)),
        grid=(2 * GROUPS,),
        in_specs=[full(pieces.shape)]
        + [pl.BlockSpec((1, 2 * AUG, length), lambda g: (row, 0, 0)), full(cols.shape)]
        + [full(w.shape) for w in wqkv]
        + [ANY] * 7
        + ([ANY] * 4 + [full(s) for s in bias_shapes] + [ANY] if carried else [])
        + [ANY] * len(through),
        out_specs=[pl.BlockSpec((count, 2, span, width), lambda g: (0, row, 0, 0))]
        + [ANY] * 4
        + [full(s) for s in bias_shapes]
        + [ANY] * len(through),
        scratch_shapes=[
            pltpu.VMEM((4, width, length), bf16),
            pltpu.VMEM((HEADS, length, length), bf16),
            pltpu.VMEM((width, length), f32),
            pltpu.VMEM((16, length), f32),
            pltpu.VMEM((width, length), bf16),
            pltpu.VMEM((16, length), f32),
            pltpu.VMEM((width, length), f32),
            pltpu.VMEM((3 * width, length), bf16),
            pltpu.VMEM((PER_GROUP, length, length), bf16),
        ]
        + [pltpu.VMEM(w.shape, bf16) for w in weights]
        + [pltpu.VMEM(s, f32) for s in sum_shapes]
        + [
            pltpu.SMEM((1,), jnp.int32),
            pltpu.SemaphoreType.DMA((7,)),
            pltpu.SemaphoreType.DMA((4,)),
            pltpu.SemaphoreType.DMA((4,)),
        ],
        out_shape=[jax.ShapeDtypeStruct((count, height, span, width), bf16)]
        + [jax.ShapeDtypeStruct(s, f32) for s in sum_shapes + bias_shapes]
        + [jax.ShapeDtypeStruct(a.shape, a.dtype) for a in through],
        input_output_aliases={first - 1: 0, **aliases} if carried else aliases,
        compiler_params=pltpu.CompilerParams(vmem_limit_bytes=VMEM_LIMIT),
        cost_estimate=cost(20),
        name="whole",
    )(pieces, aug, cols, *wqkv, *weights, *carried, *through)
    return out[1:7], out[0], out[7:]


def layer_kernel(index_ref, *refs, carried, after, parts, inner):
    take = Taker(refs)
    (piece_ref,) = take(1)
    aug_ref, cols, wq, wk, wv = take(5)
    weights_hbm = take(6)
    sums_hbm = take(3 if carried else 0)
    bias_in = take(1 if carried else 0)
    take(after)
    (out_ref,) = take(1)
    saved_hbm, p_hbm, og_ref, delta_ref, gres_ref = take(5)
    part_refs = take(parts)
    saved, p_buf, att_ref, stat_ref = take(4)
    weights = take(6)
    sums = take(3)
    packed, small_ref, weight_sem, sum_sem, p_sem, saved_sem = take(6)
    group = pl.program_id(0)
    width = att_ref.shape[0]
    weight_copies = copies_of(weights_hbm, weights, weight_sem)
    sum_copies = copies_of(sums_hbm, sums, sum_sem)
    saved_copy = pltpu.make_async_copy(saved, saved_hbm, saved_sem)
    slot = lax.rem(group, 2)

    def p_copy(number):
        start = number * PER_GROUP
        return pltpu.make_async_copy(
            p_buf.at[lax.rem(number, 2)], p_hbm.at[pl.ds(start, PER_GROUP)], p_sem.at[lax.rem(number, 2)]
        )

    @pl.when(group == 0)
    def _():
        for copy in weight_copies + sum_copies:
            copy.start()
        project_row(piece_ref, cols, wq, wk, wv, saved, small_ref)
        saved_copy.start()

    @pl.when(group >= 2)
    def _():
        p_copy(group - 2).wait()

    attend_heads(group, saved, aug_ref, lambda h: p_buf.at[slot, h], att_ref, stat_ref, small_ref)
    p_copy(group).start()

    @pl.when(group == GROUPS - 1)
    def _():
        for copy in weight_copies + sum_copies:
            copy.wait()
        total = dense_row(
            piece_ref, cols, saved, att_ref, stat_ref, weights, sums, carried,
            lambda values: write_pieces(values, out_ref), lambda number: None, og_ref, delta_ref, gres_ref,
        )
        if carried:
            total = total + bias_in[0][...]
        acc_dn, acc_up, acc_out = sums
        ff = acc_dn.shape[0]
        packed[:ff] = acc_dn[...].astype(bf16)
        for index in range(ff // width):
            packed[ff + index * width : ff + (index + 1) * width] = acc_up[
                :, index * width : (index + 1) * width
            ].astype(bf16)
        packed[2 * ff : 2 * ff + width] = acc_out[...].astype(bf16)
        packed[2 * ff + width : 2 * ff + width + 16] = total.astype(bf16)
        rest = packed.shape[0] - 2 * ff - width - 16
        if rest:
            packed[2 * ff + width + 16 :] = jnp.zeros((rest, width), bf16)
        emit(packed, index_ref[0], part_refs, inner)
        saved_copy.wait()
        for number in range(max(GROUPS - 2, 0), GROUPS):
            p_copy(number).wait()


def layer(pieces, row, aug, cols, wqkv, weights, sums, packed_rows, parts, inner, index, after):
    count, _, span, width = pieces.shape
    length = span * count
    ff = weights[3].shape[1]
    full = lambda shape: pl.BlockSpec(shape, lambda g, i: (0,) * len(shape))
    sum_shapes = [(ff, width), (width, ff), (width, width)]
    part = (packed_rows // parts, width)
    out = pl.pallas_call(
        functools.partial(
            layer_kernel, carried=bool(sums), after=len(after), parts=parts, inner=inner
        ),
        grid_spec=pltpu.PrefetchScalarGridSpec(
            num_scalar_prefetch=1,
            grid=(GROUPS,),
            in_specs=[full(pieces.shape)]
            + [pl.BlockSpec((1, 2 * AUG, length), lambda g, i: (row, 0, 0)), full(cols.shape)]
            + [full(w.shape) for w in wqkv]
            + [ANY] * 6
            + ([ANY] * 3 + [full((16, width))] if sums else [])
            + [ANY] * len(after),
            out_specs=[pl.BlockSpec((count, 1, span, width), lambda g, i: (0, 0, 0, 0))]
            + [ANY, ANY, full((width, length)), full((16, length)), full((width, length))]
            + [full(part)] * parts,
            scratch_shapes=[
                pltpu.VMEM((4, width, length), bf16),
                pltpu.VMEM((2, PER_GROUP, length, length), bf16),
                pltpu.VMEM((width, length), f32),
                pltpu.VMEM((16, length), f32),
            ]
            + [pltpu.VMEM(w.shape, bf16) for w in weights]
            + [pltpu.VMEM(shape, f32) for shape in sum_shapes]
            + [
                pltpu.VMEM((packed_rows, width), bf16),
                pltpu.SMEM((1,), jnp.int32),
                pltpu.SemaphoreType.DMA((6,)),
                pltpu.SemaphoreType.DMA((3,)),
                pltpu.SemaphoreType.DMA((2,)),
                pltpu.SemaphoreType.DMA,
            ],
        ),
        out_shape=[jax.ShapeDtypeStruct((count, 2, span, width), bf16)]
        + [
            jax.ShapeDtypeStruct((4, width, length), bf16),
            jax.ShapeDtypeStruct((HEADS, length, length), bf16),
            jax.ShapeDtypeStruct((width, length), bf16),
            jax.ShapeDtypeStruct((16, length), f32),
            jax.ShapeDtypeStruct((width, length), f32),
        ]
        + [jax.ShapeDtypeStruct(part, bf16)] * parts,
        compiler_params=pltpu.CompilerParams(vmem_limit_bytes=VMEM_LIMIT),
        cost_estimate=cost(14),
        name="layer",
    )(index, pieces, aug, cols, *wqkv, *weights, *sums, *after)
    return out[0], out[1:6], out[6:]


def back_kernel(index_ref, *refs, carried, after, parts, inner):
    take = Taker(refs)
    saved, og_ref, delta_ref, p_ref, saved_hbm, gres_hbm, w_hbm = take(7)
    sum_hbm = take(1 if carried else 0)
    bias_in = take(1 if carried else 0)
    take(after)
    (out_ref,) = take(1)
    part_refs = take(parts)
    grads, held, xt, gres, w_all = take(5)
    sum_in = take(1 if carried else 0)
    packed, sem = take(2)
    group = pl.program_id(0)
    width = og_ref.shape[0]
    copies = copies_of([saved_hbm.at[3], gres_hbm, w_hbm] + sum_hbm, [xt, gres, w_all] + sum_in, sem)

    @pl.when(group == 0)
    def _():
        for copy in copies:
            copy.start()

    back_heads(group, saved, og_ref, delta_ref, lambda h: p_ref.at[h], grads, held)

    @pl.when(group == GROUPS - 1)
    def _():
        for copy in copies:
            copy.wait()
        total = grads[...]
        acc = dot(xt[...], total, NT)
        bias = back_biases(total, width)
        if carried:
            acc = acc + sum_in[0][...]
            bias = bias + bias_in[0][...]
        per = width // 128
        for index in range(3 * per):
            packed[index * width : (index + 1) * width] = acc[:, index * 128 : (index + 1) * 128].astype(bf16)
        bias_rows = [bias[n : n + 1, i * 128 : (i + 1) * 128] for n in range(2) for i in range(per)]
        tail = packed.shape[0] - 3 * per * width
        bias_rows.append(jnp.zeros((tail - len(bias_rows), 128), f32))
        packed[3 * per * width :] = jnp.concatenate(bias_rows, axis=0).astype(bf16)
        emit(packed, index_ref[0], part_refs, inner)
        write_pieces((gres[...] + dot(w_all[...], total)).astype(bf16), out_ref)


def back(shared, saved, probs, og, delta, gres, w_all, sums, packed_rows, parts, inner, index, after):
    _, width, length = saved.shape
    count, _, span, _ = shared.shape
    first = 1 + 7 + len(sums)
    after = [shared] + list(after)
    full = lambda shape: pl.BlockSpec(shape, lambda g, i: (0,) * len(shape))
    part = (packed_rows // parts, 128)
    out = pl.pallas_call(
        functools.partial(back_kernel, carried=bool(sums), after=len(after), parts=parts, inner=inner),
        grid_spec=pltpu.PrefetchScalarGridSpec(
            num_scalar_prefetch=1,
            grid=(GROUPS,),
            in_specs=[
                full((3, width, length)),
                full((width, length)),
                full((16, length)),
                pl.BlockSpec((PER_GROUP, length, length), lambda g, i: (g, 0, 0)),
            ]
            + [ANY] * 3
            + ([ANY, full((8, width))] if sums else [])
            + [ANY] * len(after),
            out_specs=[pl.BlockSpec((count, 1, span, width), lambda g, i: (0, 1, 0, 0))] + [full(part)] * parts,
            scratch_shapes=[
                pltpu.VMEM((3 * width, length), bf16),
                pltpu.VMEM((PER_GROUP, length, length), bf16),
                pltpu.VMEM((width, length), bf16),
                pltpu.VMEM((width, length), f32),
                pltpu.VMEM(w_all.shape, bf16),
            ]
            + ([pltpu.VMEM((width, 3 * width), f32)] if sums else [])
            + [pltpu.VMEM((packed_rows, 128), bf16), pltpu.SemaphoreType.DMA((4,))],
        ),
        out_shape=[jax.ShapeDtypeStruct((count, 2, span, width), bf16)] + [jax.ShapeDtypeStruct(part, bf16)] * parts,
        input_output_aliases={first: 0},
        compiler_params=pltpu.CompilerParams(vmem_limit_bytes=VMEM_LIMIT),
        cost_estimate=cost(9),
        name="back",
    )(index, saved, og, delta, probs, saved, gres, w_all, *sums, *after)
    return out[0], out[1:]


def exchange(pieces, axis, devices, unit=1):
    moved = [pieces[0]]
    for shift in range(1, len(pieces)):
        moved.append(lax.ppermute(pieces[shift], axis, [(i, i ^ (shift * unit)) for i in range(devices)]))
    return moved


def tree_sum(blocks):
    while len(blocks) > 1:
        blocks = [left + right for left, right in zip(blocks[::2], blocks[1::2])]
    return blocks[0]


def combine_kernel(index_ref, *refs, inputs, after, through, parts, inner):
    total = tree_sum([ref[...].astype(f32) for ref in refs[:inputs]]).astype(bf16)
    refs = refs[inputs + after + through :]
    outs = refs[:parts]
    if parts == 1:
        outs[0][...] = total
    else:
        packed = refs[-1]
        packed[...] = total
        emit(packed, index_ref[0], outs, inner)


def combine(blocks, parts, inner, index, after=(), through=()):
    rows, width = blocks[0].shape
    part = (rows // parts, width)
    first = 1 + len(blocks) + len(after)
    full = lambda s: pl.BlockSpec(s, lambda i, j: (0, 0))
    out = pl.pallas_call(
        functools.partial(
            combine_kernel, inputs=len(blocks), after=len(after), through=len(through), parts=parts, inner=inner
        ),
        grid_spec=pltpu.PrefetchScalarGridSpec(
            num_scalar_prefetch=1,
            grid=(1,),
            in_specs=[full((rows, width))] * len(blocks) + [ANY] * (len(after) + len(through)),
            out_specs=[full(part)] * parts + [ANY] * len(through),
            scratch_shapes=[pltpu.VMEM((rows, width), bf16)] if parts > 1 else [],
        ),
        out_shape=[jax.ShapeDtypeStruct(part, bf16)] * parts
        + [jax.ShapeDtypeStruct(a.shape, a.dtype) for a in through],
        input_output_aliases={first + i: parts + i for i in range(len(through))},
        compiler_params=pltpu.CompilerParams(vmem_limit_bytes=12 * 2**20),
        cost_estimate=cost(1),
        name="combine",
    )(index, *blocks, *after, *through)
    return out[:parts], out[parts:]


def merge_kernel(index_ref, *refs, count, after, parts, inner):
    left = tree_sum([ref[...].astype(f32) for ref in refs[:count]])
    right = tree_sum([ref[...].astype(f32) for ref in refs[count : 2 * count]])
    packed = refs[-1]
    packed[...] = jnp.concatenate([left, right], axis=1).astype(bf16)
    emit(packed, index_ref[0], refs[2 * count + after : -1], inner)


def merge(lefts, rights, stage, after=()):
    rows, left = lefts[0].shape
    width = left + rights[0].shape[1]
    parts = stage[3]
    full = lambda s: pl.BlockSpec(s, lambda i, j: (0, 0))
    return pl.pallas_call(
        functools.partial(merge_kernel, count=len(lefts), after=len(after), parts=parts, inner=stage[4]),
        grid_spec=pltpu.PrefetchScalarGridSpec(
            num_scalar_prefetch=1,
            grid=(1,),
            in_specs=[full(b.shape) for b in list(lefts) + list(rights)] + [ANY] * len(after),
            out_specs=[full((rows // parts, width))] * parts,
            scratch_shapes=[pltpu.VMEM((rows, width), bf16)],
        ),
        out_shape=[jax.ShapeDtypeStruct((rows // parts, width), bf16)] * parts,
        compiler_params=pltpu.CompilerParams(vmem_limit_bytes=12 * 2**20),
        cost_estimate=cost(2),
        name="merge",
    )(place_of(stage), *lefts, *rights, *after)


def put_together(refs, out, index, inner):
    size = refs[0].shape[0] // inner
    for shift, ref in enumerate(refs):
        for block in range(inner):
            start = pl.multiple_of((block * len(refs) + (index ^ shift)) * size, 16)
            out[pl.ds(start, size), :] = ref[block * size : (block + 1) * size]


def assemble_kernel(index_ref, *refs, inputs, after, inner):
    put_together(refs[:inputs], refs[inputs + after], index_ref[0], inner)


def assemble(blocks, stage, after=(), through=()):
    rows, width = blocks[0].shape
    full = lambda s: pl.BlockSpec(s, lambda i, j: (0, 0))
    shape = (rows * len(blocks), width)
    first = 1 + len(blocks) + len(after)
    after = list(after) + list(through)
    out = pl.pallas_call(
        functools.partial(assemble_kernel, inputs=len(blocks), after=len(after), inner=stage[4]),
        grid_spec=pltpu.PrefetchScalarGridSpec(
            num_scalar_prefetch=1,
            grid=(1,),
            in_specs=[full((rows, width))] * len(blocks) + [ANY] * len(after),
            out_specs=[full(shape)] + [ANY] * len(through),
        ),
        out_shape=[jax.ShapeDtypeStruct(shape, bf16)] + [jax.ShapeDtypeStruct(a.shape, a.dtype) for a in through],
        input_output_aliases={first + i: 1 + i for i in range(len(through))},
        compiler_params=pltpu.CompilerParams(vmem_limit_bytes=12 * 2**20),
        cost_estimate=cost(1),
        name="assemble",
    )(place_of(stage), *blocks, *after)
    return out[0], out[1:]


def place_kernel(*refs, rows):
    outs = refs[-2:]
    row = pl.program_id(0)
    for number in range(rows):

        @pl.when(row == number)
        def _(number=number):
            for which in range(2):
                outs[which][...] = refs[2 * number + which][...].astype(outs[which].dtype)


def place(sources):
    rows = len(sources)
    count, _, span, width = sources[0][0][0].shape
    shape = (count, rows, span, width)
    in_specs = []
    arrays = []
    for row in sources:
        for sent, at in row:
            in_specs.append(pl.BlockSpec((count, 1, span, width), lambda r, at=at: (0, at, 0, 0)))
            arrays.append(sent)
    out_spec = pl.BlockSpec((count, 1, span, width), lambda r: (0, r, 0, 0))
    layer_out, grad = pl.pallas_call(
        functools.partial(place_kernel, rows=rows),
        grid=(rows,),
        in_specs=in_specs,
        out_specs=[out_spec, out_spec],
        out_shape=[jax.ShapeDtypeStruct(shape, bf16), jax.ShapeDtypeStruct(shape, f32)],
        compiler_params=pltpu.CompilerParams(vmem_limit_bytes=VMEM_LIMIT),
        cost_estimate=cost(5),
        name="place",
    )(*arrays)
    return layer_out.reshape(count * rows, span, width), grad.reshape(count * rows, span, width)


def sum_stages(sizes):
    stages = []
    for axis in ("rows", "seq"):
        devices = sizes[axis]
        unit = 1
        while unit < devices:
            size = 2 if unit == 1 and devices.bit_length() % 2 == 0 else 4
            stages.append((axis, devices, unit, size, devices // (unit * size)))
            unit *= size
    return stages


def place_of(stage):
    axis, _, unit, size, _ = stage
    return ((lax.axis_index(axis) // unit) % size).astype(jnp.int32).reshape(1)


def send_parts(parts, stage):
    axis, devices, unit, _, _ = stage
    return exchange(parts, axis, devices, unit)


def cut_for(taken, stage, after=(), through=()):
    return combine(taken, stage[3], stage[4], place_of(stage), after, through)


def add(taken, after=()):
    return combine(taken, 1, 1, jnp.zeros((1,), jnp.int32), after)[0][0]


def unpack_kernel(index_ref, *refs, inputs, after, inner):
    down, up, out, *biases = refs[inputs + after : inputs + after + 10]
    query, key, value, bias_q, bias_v = refs[inputs + after + 10 : -1]
    block = refs[-1]
    put_together(refs[:inputs], block, index_ref[0], inner)
    ff, width = down.shape
    per = ff // width
    down[...] = block[:ff, :width].astype(f32)
    for index in range(per):
        rows = slice(ff + index * width, ff + (index + 1) * width)
        up[:, index * width : (index + 1) * width] = block[rows, :width].astype(f32)
    out[...] = block[2 * ff : 2 * ff + width, :width].astype(f32)
    rows = block[2 * ff + width : 2 * ff + width + 16, :width].astype(f32)
    for index, ref in enumerate(biases[:-1]):
        ref[...] = rows[index]
    biases[-1][...] = jnp.concatenate([rows[len(biases) - 1 + i] for i in range(per)], axis=0)
    per = width // 128
    for number, ref in enumerate((query, key, value)):
        for index in range(per):
            start = (number * per + index) * width
            ref[:, index * 128 : (index + 1) * 128] = block[start : start + width, width:].astype(f32)
    rows = block[3 * per * width : 3 * per * width + 16, width:].astype(f32)
    for number, ref in enumerate((bias_q, bias_v)):
        ref[...] = jnp.concatenate([rows[number * per + i] for i in range(per)], axis=0)


def unpack(blocks, stage, shapes, after=()):
    rows, width = blocks[0].shape
    full = lambda s: pl.BlockSpec(s, lambda i, j: (0,) * len(s))
    return pl.pallas_call(
        functools.partial(unpack_kernel, inputs=len(blocks), after=len(after), inner=stage[4]),
        grid_spec=pltpu.PrefetchScalarGridSpec(
            num_scalar_prefetch=1,
            grid=(1,),
            in_specs=[full((rows, width))] * len(blocks) + [ANY] * len(after),
            out_specs=[full(s) for s in shapes],
            scratch_shapes=[pltpu.VMEM((rows * len(blocks), width), bf16)],
        ),
        out_shape=[jax.ShapeDtypeStruct(s, f32) for s in shapes],
        compiler_params=pltpu.CompilerParams(vmem_limit_bytes=28 * 2**20),
        cost_estimate=cost(4),
        name="unpack",
    )(place_of(stage), *blocks, *after)


def round_up(value, unit):
    return -(-value // unit) * unit


def body(
    tokens, lengths, w_query, b_query, w_key, w_value, b_value, w_out, b_out, gain_attn, shift_attn,
    w_up, b_up, w_down, b_down, gain_ffn, shift_ffn, cotangent, *, sizes,
):
    count = sizes["seq"]
    devices = count * sizes["rows"]
    row_count, span, width = tokens.shape
    ff = w_up.shape[1]
    length = span * count
    rows = row_count // count
    me = lax.axis_index("seq")
    stages = sum_stages(sizes)
    row_stages, seq_stages = [[stage for stage in stages if stage[0] == axis] for axis in ("rows", "seq")]
    first = stages[0]
    index = place_of(first)
    later_rows = round_up(2 * ff + width + 16, 16 * devices)
    first_rows = later_rows

    def split(array):
        return array.reshape(count, rows, 1, span, width)

    def to_owners(parts):
        return lax.all_to_all(parts, "seq", 0, 0, tiled=True)

    parts = [jnp.concatenate([split(tokens)[:, row], split(cotangent)[:, row]], axis=1) for row in range(rows)]
    given = {0: to_owners(parts[0])}

    bounds = lax.dynamic_slice_in_dim(jnp.cumsum(lengths, axis=1), me * rows, rows, 0)
    spots = jnp.arange(length, dtype=jnp.int32)
    segment = jnp.sum((spots[None, None, :] >= bounds[:, :, None]).astype(jnp.int32), axis=1)
    ids = jnp.arange(2 * AUG, dtype=jnp.int32)[None, :, None]
    same = segment[:, None, :] == ids % AUG
    aug = jnp.where(ids < AUG, jnp.where(same, 1.0, 0.0), jnp.where(same | (ids % AUG >= lengths.shape[1]), 0.0, -BIG))
    aug = aug.astype(bf16)

    vectors = [b_query, b_value, b_out, gain_attn, shift_attn, b_down, gain_ffn, shift_ffn]
    vectors = jnp.concatenate([jnp.stack(vectors), b_up.reshape(-1, width)], axis=0)
    (wq_t, wk_t, wv_t, wo_t, wup_t, wdn_t, cols), waiting = prepare(
        (w_query, w_key, w_value, w_out, w_up, w_down), vectors, aug, parts[1:]
    )
    if rows > 1:
        given[1] = to_owners(waiting[0])
    dense_weights = (wo_t, w_out, wup_t, w_up, wdn_t, w_down)
    w_all = jnp.concatenate([w_query, w_key, w_value], axis=1)

    wqkv = (wq_t, wk_t, wv_t)
    last = rows - 1

    def return_pieces(array):
        return lax.all_to_all(array, "seq", 0, 0, tiled=True)

    carried = []
    for row in range(last):
        through = [waiting[row + 1]] if row + 2 < rows else []
        sums, shared, through = whole(
            given[row], row, 2 * last, aug, cols, wqkv, dense_weights + (w_all,), carried, through
        )
        if row + 2 < rows:
            given[row + 2] = to_owners(through[0])
        carried = list(sums) + [shared]
    places = []
    if last:
        moved = return_pieces(shared)
        places = [((moved, 2 * row), (moved, 2 * row + 1)) for row in range(last)]
    shared, saved, later = layer(
        given[last], last, aug, cols, wqkv, dense_weights, (carried[:3] + carried[4:5]) if carried else [],
        later_rows, first[3], first[4], index, [],
    )
    keys, probs, og, delta, gres = saved
    taken = send_parts(later, first)
    ends, early = back(
        shared, keys, probs, og, delta, gres, w_all, (carried[3:4] + carried[5:6]) if carried else [], first_rows,
        first[3], first[4], index, [],
    )
    after = list(early[:1])
    for stage in row_stages[1:]:
        cut, _ = cut_for(taken, stage, after)
        taken = send_parts(cut, stage)
        after = list(cut[:1])
    given_early = send_parts(early, first)
    for stage in row_stages[1:]:
        cut, (ends,) = cut_for(given_early, stage, after, [ends])
        given_early = send_parts(cut, stage)
        after = list(cut[:1])
    ends = return_pieces(ends)
    parts = merge(taken, given_early, seq_stages[0], [moved] if last else [])
    for number, stage in enumerate(seq_stages):
        taken = send_parts(parts, stage)
        if number + 1 < len(seq_stages):
            parts, _ = cut_for(taken, seq_stages[number + 1])
    block = add(taken)
    layer_out, grad_tokens = place(places + [((ends, 0), (ends, 1))])
    for number, stage in enumerate(reversed(stages[1:])):
        taken = send_parts([block] * stage[3], stage)
        block, _ = assemble(taken, stage, [layer_out, grad_tokens] if number == len(stages) - 2 else [])
    shapes = [(ff, width), (width, ff), (width, width)] + [(width,)] * 6 + [(ff,)] + [(width, width)] * 3 + [(width,)] * 2
    (
        grad_down, grad_up, grad_output, grad_gain2, grad_shift2, grad_dnbias, grad_gain1, grad_shift1, grad_obias,
        grad_upbias, grad_query, grad_key, grad_value, grad_qbias, grad_vbias,
    ) = unpack(send_parts([block] * first[3], first), first, shapes)
    return (
        layer_out, grad_tokens, grad_query, grad_qbias, grad_key, grad_value, grad_vbias, grad_output, grad_obias,
        grad_gain1, grad_shift1, grad_up, grad_upbias, grad_down, grad_dnbias, grad_gain2, grad_shift2,
    )


def solution(mesh):
    split = P("rows", "seq", None)
    in_specs = (split, P("rows", None)) + (P(),) * 15 + (split,)
    out_specs = (split, split) + (P(),) * 15
    sizes = dict(mesh.shape)
    return jax.shard_map(
        functools.partial(body, sizes=sizes), mesh=mesh, in_specs=in_specs, out_specs=out_specs, check_vma=False
    )
```

```python
import functools
import math

import jax
import jax.numpy as jnp
from jax import lax
from jax.experimental import pallas as pl
from jax.experimental.pallas import tpu as pltpu
from jax.sharding import PartitionSpec as P

HEADS = 12
HD = 32
GROUPS = 3
PER_GROUP = HEADS // GROUPS
AUG = 16
BIG = 2.0**100
SMALL_SCORE = 60.0
EPSILON = 1e-05
SCALE = HD ** (-0.5)
LOG2E = math.log2(math.e)
Q_FACTOR = SCALE * LOG2E
LN2 = math.log(2.0)
VMEM_LIMIT = 60 * 2**20

f32 = jnp.float32
bf16 = jnp.bfloat16
NN = (((1,), (0,)), ((), ()))
NT = (((1,), (1,)), ((), ()))
TN = (((0,), (0,)), ((), ()))


def dot(left, right, dims=NN):
    return lax.dot_general(left, right, dims, preferred_element_type=f32)


def fold_lanes(values):
    total = values[:, :128]
    for start in range(128, values.shape[1], 128):
        total = total + values[:, start : start + 128]
    return total


def row_sum(partial):
    return jnp.sum(partial.T, axis=0, keepdims=True)


def normalize(hidden):
    scale = 1.0 / hidden.shape[0]
    centre = hidden - jnp.sum(hidden, axis=0, keepdims=True) * scale
    variance = jnp.sum(centre * centre, axis=0, keepdims=True) * scale
    inverse = lax.rsqrt(variance + EPSILON)
    return centre * inverse, inverse


def normalize_back(upstream, scaled, inverse):
    scale = 1.0 / upstream.shape[0]
    mean = jnp.sum(upstream, axis=0, keepdims=True) * scale
    spread = jnp.sum(upstream * scaled, axis=0, keepdims=True) * scale
    return inverse * (upstream - mean - scaled * spread)


def gelu_parts(v):
    cdf = 0.5 + 0.5 * lax.erf(v * 0.5**0.5)
    bell = jnp.exp2((v * v) * (-0.5 * LOG2E))
    return v * cdf, cdf + v * bell * (2.0 * math.pi) ** (-0.5)


def prepare_kernel(*refs, through):
    sources, rows = refs[:6], refs[6]
    targets, columns = refs[8 + through : 14 + through], refs[14 + through]
    for source, target in zip(sources, targets):
        target[...] = source[...].T
    width = rows.shape[1]
    columns[...] = jnp.concatenate([rows[...], jnp.zeros((128 - rows.shape[0], width), f32)], axis=0).T


def prepare(weights, rows, aug, through):
    full = lambda shape: pl.BlockSpec(shape, lambda i: (0, 0))
    shapes = [w.shape[::-1] for w in weights]
    out = pl.pallas_call(
        functools.partial(prepare_kernel, through=len(through)),
        grid=(1,),
        in_specs=[full(w.shape) for w in weights] + [full(rows.shape)] + [ANY] * (1 + len(through)),
        out_specs=[full(s) for s in shapes] + [full((rows.shape[1], 128))] + [ANY] * len(through),
        out_shape=[jax.ShapeDtypeStruct(s, bf16) for s in shapes]
        + [jax.ShapeDtypeStruct((rows.shape[1], 128), f32)]
        + [jax.ShapeDtypeStruct(a.shape, a.dtype) for a in through],
        input_output_aliases={8 + i: 7 + i for i in range(len(through))},
        compiler_params=pltpu.CompilerParams(vmem_limit_bytes=VMEM_LIMIT),
        cost_estimate=cost(5),
        name="prepare",
    )(*weights, rows, aug, *through)
    return out[:7], out[7:]


def cost(micros):
    return pl.CostEstimate(flops=int(micros * 1e5), transcendentals=0, bytes_accessed=int(micros * 1e3))


B_QUERY, B_VALUE, B_OUT, GAIN1, SHIFT1, B_DOWN, GAIN2, SHIFT2, B_UP = range(9)


ANY = pl.BlockSpec(memory_space=pl.ANY)


def head_sums(values):
    return jnp.sum(values.reshape(HEADS, HD, values.shape[1]), axis=1)


def emit(packed, index, outs, inner):
    size = outs[0].shape[0] // inner
    for shift, ref in enumerate(outs):
        for block in range(inner):
            start = pl.multiple_of((block * len(outs) + (index ^ shift)) * size, 16)
            ref[block * size : (block + 1) * size] = packed[pl.ds(start, size), :]


class Taker:
    def __init__(self, refs):
        self.refs = list(refs)

    def __call__(self, number):
        taken = self.refs[:number]
        del self.refs[:number]
        return taken


def column_of(cols, index):
    return cols[:, index : index + 1]


def project_row(piece_ref, cols, wq, wk, wv, saved, small_ref):
    xt = jnp.concatenate([piece_ref[i, 0].T for i in range(piece_ref.shape[0])], axis=1)
    query = (dot(wq[...], xt) + column_of(cols, B_QUERY)) * Q_FACTOR
    key = dot(wk[...], xt)
    saved[0] = query.astype(bf16)
    saved[1] = key.astype(bf16)
    saved[2] = (dot(wv[...], xt) + column_of(cols, B_VALUE)).astype(bf16)
    saved[3] = xt
    bounds = [
        jnp.max(head_sums(query * query), axis=1, keepdims=True),
        jnp.max(head_sums(key * key), axis=1, keepdims=True),
    ]
    small_ref[0] = (jnp.max(bounds[0] * bounds[1]) < SMALL_SCORE**2).astype(jnp.int32)


def head_rows(group, h):
    return pl.ds(pl.multiple_of((group * PER_GROUP + h) * HD, HD), HD)


def attend_heads(group, saved, aug_ref, probs, att_ref, stat_ref, small_ref):
    length = saved.shape[2]
    ones = jnp.ones((AUG, length), bf16)

    def score(h):
        keys = jnp.concatenate([saved[1, head_rows(group, h), :], aug_ref[0, AUG:]], axis=0)
        query = jnp.concatenate([saved[0, head_rows(group, h), :], aug_ref[0, :AUG]], axis=0)
        return dot(keys, query, TN)

    def mix(h):
        values = jnp.concatenate([saved[2, head_rows(group, h), :], ones], axis=0)
        mixed = dot(values, probs(h)[...])
        inverse = 1.0 / mixed[HD : HD + 1]
        att_ref[head_rows(group, h), :] = mixed[:HD] * inverse
        stat_ref[pl.ds(group * PER_GROUP + h, 1), :] = inverse

    def heads(shifted):
        scores = score(0)
        for h in range(PER_GROUP):
            following = score(h + 1) if h + 1 < PER_GROUP else None
            if h >= 1:
                mix(h - 1)
            if shifted:
                scores = scores - jnp.max(scores, axis=0, keepdims=True)
            probs(h)[...] = jnp.exp2(scores).astype(bf16)
            scores = following
        mix(PER_GROUP - 1)

    @pl.when(small_ref[0] == 1)
    def _():
        heads(False)

    @pl.when(small_ref[0] == 0)
    def _():
        heads(True)


def dense_row(piece_ref, cols, saved, att_ref, stat_ref, weights, sums, carried, arriving, write_out, summed, og_ref, delta_ref, gres_ref):
    wo_t, wo, wup_t, wup, wdn_t, wdn = weights
    acc_dn, acc_up, acc_out = sums
    ff = acc_dn.shape[0]
    width = att_ref.shape[0]

    def column(index):
        return column_of(cols, index)

    def add(number, value):
        ref = sums[number]
        if arriving:
            arriving[number].wait()
        ref[...] = ref[...] + value if carried else value
        summed(number)

    att = att_ref[...]
    att_b = att.astype(bf16)
    res1 = saved[3].astype(f32) + dot(wo_t[...], att_b) + column(B_OUT)
    scaled1, inverse1 = normalize(res1)
    normed = scaled1 * column(GAIN1) + column(SHIFT1)
    normed_b = normed.astype(bf16)
    b_up = jnp.concatenate([column(B_UP + i) for i in range(ff // width)], axis=0)
    act, slope = gelu_parts(dot(wup_t[...], normed_b) + b_up)
    act_b = act.astype(bf16)
    res2 = normed + dot(wdn_t[...], act_b) + column(B_DOWN)
    scaled2, inverse2 = normalize(res2)
    write_out((scaled2 * column(GAIN2) + column(SHIFT2)).astype(bf16))
    cot = jnp.concatenate([piece_ref[i, 1].T for i in range(piece_ref.shape[0])], axis=1).astype(f32)
    gres2 = normalize_back(cot * column(GAIN2), scaled2, inverse2)
    down_b = gres2.astype(bf16)
    up_b = (dot(wdn[...], down_b) * slope).astype(bf16)
    add(0, dot(act_b, down_b, NT))
    gnormed = gres2 + dot(wup[...], up_b)
    add(1, dot(normed_b, up_b, NT))
    gres1 = normalize_back(gnormed * column(GAIN1), scaled1, inverse1)
    gres_ref[...] = gres1
    branch_b = gres1.astype(bf16)
    og = dot(wo[...], branch_b)
    add(2, dot(att_b, branch_b, NT))
    for h in range(HEADS):
        part = slice(h * HD, (h + 1) * HD)
        scaled_og = (og[part] * stat_ref[h : h + 1, :]).astype(bf16)
        og_ref[part, :] = scaled_og
        delta_ref[h : h + 1, :] = jnp.sum(scaled_og.astype(f32) * att[part], axis=0, keepdims=True)
    biases = [cot * scaled2, cot, down_b.astype(f32), gnormed * scaled1, gnormed, branch_b.astype(f32)]
    bias_rows = [row_sum(fold_lanes(value)) for value in biases]
    up_sum = fold_lanes(up_b.astype(f32))
    bias_rows += [row_sum(up_sum[i * width : (i + 1) * width]) for i in range(ff // width)]
    bias_rows.append(jnp.zeros((16 - len(bias_rows), width), f32))
    return jnp.concatenate(bias_rows, axis=0)


def back_heads(group, saved, og_ref, delta_ref, probs, grads, held):
    length = og_ref.shape[1]
    width = og_ref.shape[0]
    sign = jnp.where(lax.broadcasted_iota(jnp.int32, (AUG, length), 0) < 3, 1.0, 0.0).astype(bf16)

    def grad_probs(h):
        delta = delta_ref[pl.ds(group * PER_GROUP + h, 1), :]
        first = delta.astype(bf16)
        rest = delta - first.astype(f32)
        second = rest.astype(bf16)
        third = (rest - second.astype(f32)).astype(bf16)
        aug = jnp.concatenate(
            [-first.astype(f32), -second.astype(f32), -third.astype(f32), jnp.zeros((AUG - 3, length), f32)], axis=0
        ).astype(bf16)
        left = jnp.concatenate([saved[2, head_rows(group, h), :], sign], axis=0)
        right = jnp.concatenate([og_ref[head_rows(group, h), :], aug], axis=0)
        return dot(left, right, TN)

    def target(which, h):
        return pl.ds(pl.multiple_of(which * width + (group * PER_GROUP + h) * HD, HD), HD)

    for h in range(PER_GROUP):
        held[h] = (probs(h)[...].astype(f32) * grad_probs(h)).astype(bf16)
        grads[target(2, h), :] = dot(og_ref[head_rows(group, h), :], probs(h)[...], NT).astype(bf16)
    for h in range(PER_GROUP):
        grads[target(0, h), :] = (dot(saved[1, head_rows(group, h), :], held[h]) * SCALE).astype(bf16)
        grads[target(1, h), :] = (dot(saved[0, head_rows(group, h), :], held[h], NT) * LN2).astype(bf16)


def back_biases(total, width):
    rows = [row_sum(fold_lanes(part.astype(f32))) for part in (total[:width], total[2 * width :])]
    return jnp.concatenate(rows + [jnp.zeros((6, width), f32)], axis=0)


def write_pieces(values, ref, at=0):
    span = ref.shape[2]
    for piece in range(ref.shape[0]):
        ref[piece, at] = values[:, piece * span : (piece + 1) * span].T


def copies_of(sources, targets, sem):
    return [pltpu.make_async_copy(a, b, sem.at[i]) for i, (a, b) in enumerate(zip(sources, targets))]


def whole_kernel(*refs, carried, through):
    take = Taker(refs)
    (piece_ref,) = take(1)
    aug_ref, cols, wq, wk, wv = take(5)
    weights_hbm = take(7)
    sums_hbm = take(4 if carried else 0)
    bias_in = take(2 if carried else 0)
    take((1 if carried else 0) + through)
    (out_ref,) = take(1)
    sums_out = take(4)
    bias_out = take(2)
    take(through)
    saved, p_all, att_ref, stat_ref, og_ref, delta_ref, gres_ref, grads, held = take(9)
    weights = take(7)
    sums = take(4)
    small_ref, weight_sem, sum_sem, out_sem = take(4)
    step = pl.program_id(0)
    width = att_ref.shape[0]
    weight_copies = copies_of(weights_hbm, weights, weight_sem)
    sum_copies = copies_of(sums_hbm, sums, sum_sem)
    out_copies = copies_of(sums, sums_out, out_sem)

    @pl.when(step == 0)
    def _():
        for copy in weight_copies + sum_copies:
            copy.start()
        project_row(piece_ref, cols, wq, wk, wv, saved, small_ref)

    @pl.when(step < GROUPS)
    def _():
        attend_heads(step, saved, aug_ref, lambda h: p_all.at[step * PER_GROUP + h], att_ref, stat_ref, small_ref)

    @pl.when(step == GROUPS - 1)
    def _():
        for copy in weight_copies[:6] + sum_copies[:3]:
            copy.wait()
        total = dense_row(
            piece_ref, cols, saved, att_ref, stat_ref, weights[:6], sums[:3], carried, [],
            lambda values: write_pieces(values, out_ref, 0), lambda number: out_copies[number].start(),
            og_ref, delta_ref, gres_ref,
        )
        bias_out[0][...] = total + bias_in[0][...] if carried else total

    @pl.when(step >= GROUPS)
    def _():
        group = step - GROUPS
        back_heads(group, saved, og_ref, delta_ref, lambda h: p_all.at[group * PER_GROUP + h], grads, held)

    @pl.when(step == 2 * GROUPS - 1)
    def _():
        for copy in weight_copies[6:] + sum_copies[3:]:
            copy.wait()
        total = grads[...]
        acc = dot(saved[3], total, NT)
        sums[3][...] = sums[3][...] + acc if carried else acc
        out_copies[3].start()
        bias = back_biases(total, width)
        bias_out[1][...] = bias + bias_in[1][...] if carried else bias
        result = (gres_ref[...] + dot(weights[6][...], total)).astype(bf16)
        write_pieces(result, out_ref, 1)
        for copy in out_copies:
            copy.wait()


def whole(pieces, row, height, aug, cols, wqkv, weights, carried, through):
    count, _, span, width = pieces.shape
    length = span * count
    ff = weights[3].shape[1]
    full = lambda shape: pl.BlockSpec(shape, lambda g: (0,) * len(shape))
    sum_shapes = [(ff, width), (width, ff), (width, width), (width, 3 * width)]
    bias_shapes = [(16, width), (8, width)]
    first = 1 + 5 + 7 + len(carried)
    aliases = {first + i: 7 + i for i in range(len(through))}
    out = pl.pallas_call(
        functools.partial(whole_kernel, carried=bool(carried), through=len(through)),
        grid=(2 * GROUPS,),
        in_specs=[full(pieces.shape)]
        + [pl.BlockSpec((1, 2 * AUG, length), lambda g: (row, 0, 0)), full(cols.shape)]
        + [full(w.shape) for w in wqkv]
        + [ANY] * 7
        + ([ANY] * 4 + [full(s) for s in bias_shapes] + [ANY] if carried else [])
        + [ANY] * len(through),
        out_specs=[pl.BlockSpec((count, 2, span, width), lambda g: (0, row, 0, 0))]
        + [ANY] * 4
        + [full(s) for s in bias_shapes]
        + [ANY] * len(through),
        scratch_shapes=[
            pltpu.VMEM((4, width, length), bf16),
            pltpu.VMEM((HEADS, length, length), bf16),
            pltpu.VMEM((width, length), f32),
            pltpu.VMEM((16, length), f32),
            pltpu.VMEM((width, length), bf16),
            pltpu.VMEM((16, length), f32),
            pltpu.VMEM((width, length), f32),
            pltpu.VMEM((3 * width, length), bf16),
            pltpu.VMEM((PER_GROUP, length, length), bf16),
        ]
        + [pltpu.VMEM(w.shape, bf16) for w in weights]
        + [pltpu.VMEM(s, f32) for s in sum_shapes]
        + [
            pltpu.SMEM((1,), jnp.int32),
            pltpu.SemaphoreType.DMA((7,)),
            pltpu.SemaphoreType.DMA((4,)),
            pltpu.SemaphoreType.DMA((4,)),
        ],
        out_shape=[jax.ShapeDtypeStruct((count, height, span, width), bf16)]
        + [jax.ShapeDtypeStruct(s, f32) for s in sum_shapes + bias_shapes]
        + [jax.ShapeDtypeStruct(a.shape, a.dtype) for a in through],
        input_output_aliases={first - 1: 0, **aliases} if carried else aliases,
        compiler_params=pltpu.CompilerParams(vmem_limit_bytes=VMEM_LIMIT),
        cost_estimate=cost(20),
        name="whole",
    )(pieces, aug, cols, *wqkv, *weights, *carried, *through)
    return out[1:7], out[0], out[7:]


def layer_kernel(index_ref, *refs, carried, after, parts, inner):
    take = Taker(refs)
    (piece_ref,) = take(1)
    aug_ref, cols, wq, wk, wv = take(5)
    weights_hbm = take(6)
    sums_hbm = take(3 if carried else 0)
    bias_in = take(1 if carried else 0)
    take(after)
    (out_ref,) = take(1)
    saved_hbm, p_hbm, og_ref, delta_ref, gres_ref = take(5)
    part_refs = take(parts)
    saved, p_buf, att_ref, stat_ref = take(4)
    weights = take(6)
    sums = take(3)
    packed, small_ref, weight_sem, sum_sem, p_sem, saved_sem, part_sem = take(7)
    group = pl.program_id(0)
    width = att_ref.shape[0]
    weight_copies = copies_of(weights_hbm, weights, weight_sem)
    sum_copies = copies_of(sums_hbm, sums, sum_sem)
    saved_copy = pltpu.make_async_copy(saved, saved_hbm, saved_sem)
    slot = lax.rem(group, 2)

    def p_copy(number):
        start = number * PER_GROUP
        return pltpu.make_async_copy(
            p_buf.at[lax.rem(number, 2)], p_hbm.at[pl.ds(start, PER_GROUP)], p_sem.at[lax.rem(number, 2)]
        )

    @pl.when(group == 0)
    def _():
        for copy in weight_copies + sum_copies:
            copy.start()
        project_row(piece_ref, cols, wq, wk, wv, saved, small_ref)
        saved_copy.start()

    @pl.when(group >= 2)
    def _():
        p_copy(group - 2).wait()

    attend_heads(group, saved, aug_ref, lambda h: p_buf.at[slot, h], att_ref, stat_ref, small_ref)
    p_copy(group).start()

    @pl.when(group == GROUPS - 1)
    def _():
        for copy in weight_copies:
            copy.wait()
        acc_dn, acc_up, acc_out = sums
        ff = acc_dn.shape[0]
        size = part_refs[0].shape[0] // inner
        part_copies = []

        def send(number):
            for shift, ref in enumerate(part_refs):
                start = pl.multiple_of((number * parts + (index_ref[0] ^ shift)) * size, 16)
                copy = pltpu.make_async_copy(
                    packed.at[pl.ds(start, size)], ref.at[pl.ds(number * size, size)], part_sem.at[shift * inner + number]
                )
                copy.start()
                part_copies.append(copy)

        def blocks_until(done):
            return done // (parts * size)

        def pack(number):
            if number == 0:
                packed[:ff] = acc_dn[...].astype(bf16)
                ready = range(blocks_until(ff))
            elif number == 1:
                for index in range(ff // width):
                    packed[ff + index * width : ff + (index + 1) * width] = acc_up[
                        :, index * width : (index + 1) * width
                    ].astype(bf16)
                ready = range(blocks_until(ff), blocks_until(2 * ff))
            else:
                packed[2 * ff : 2 * ff + width] = acc_out[...].astype(bf16)
                ready = []
            for block in ready:
                send(block)

        total = dense_row(
            piece_ref, cols, saved, att_ref, stat_ref, weights, sums, carried, sum_copies,
            lambda values: write_pieces(values, out_ref), pack, og_ref, delta_ref, gres_ref,
        )
        if carried:
            total = total + bias_in[0][...]
        packed[2 * ff + width : 2 * ff + width + 16] = total.astype(bf16)
        rest = packed.shape[0] - 2 * ff - width - 16
        if rest:
            packed[2 * ff + width + 16 :] = jnp.zeros((rest, width), bf16)
        for number in range(blocks_until(2 * ff), inner):
            send(number)
        for copy in part_copies:
            copy.wait()
        saved_copy.wait()
        for number in range(max(GROUPS - 2, 0), GROUPS):
            p_copy(number).wait()


def layer(pieces, row, aug, cols, wqkv, weights, sums, packed_rows, parts, inner, index, after):
    count, _, span, width = pieces.shape
    length = span * count
    ff = weights[3].shape[1]
    full = lambda shape: pl.BlockSpec(shape, lambda g, i: (0,) * len(shape))
    sum_shapes = [(ff, width), (width, ff), (width, width)]
    part = (packed_rows // parts, width)
    out = pl.pallas_call(
        functools.partial(
            layer_kernel, carried=bool(sums), after=len(after), parts=parts, inner=inner
        ),
        grid_spec=pltpu.PrefetchScalarGridSpec(
            num_scalar_prefetch=1,
            grid=(GROUPS,),
            in_specs=[full(pieces.shape)]
            + [pl.BlockSpec((1, 2 * AUG, length), lambda g, i: (row, 0, 0)), full(cols.shape)]
            + [full(w.shape) for w in wqkv]
            + [ANY] * 6
            + ([ANY] * 3 + [full((16, width))] if sums else [])
            + [ANY] * len(after),
            out_specs=[pl.BlockSpec((count, 1, span, width), lambda g, i: (0, 0, 0, 0))]
            + [ANY, ANY, full((width, length)), full((16, length)), full((width, length))]
            + [ANY] * parts,
            scratch_shapes=[
                pltpu.VMEM((4, width, length), bf16),
                pltpu.VMEM((2, PER_GROUP, length, length), bf16),
                pltpu.VMEM((width, length), f32),
                pltpu.VMEM((16, length), f32),
            ]
            + [pltpu.VMEM(w.shape, bf16) for w in weights]
            + [pltpu.VMEM(shape, f32) for shape in sum_shapes]
            + [
                pltpu.VMEM((packed_rows, width), bf16),
                pltpu.SMEM((1,), jnp.int32),
                pltpu.SemaphoreType.DMA((6,)),
                pltpu.SemaphoreType.DMA((3,)),
                pltpu.SemaphoreType.DMA((2,)),
                pltpu.SemaphoreType.DMA,
                pltpu.SemaphoreType.DMA((parts * inner,)),
            ],
        ),
        out_shape=[jax.ShapeDtypeStruct((count, 2, span, width), bf16)]
        + [
            jax.ShapeDtypeStruct((4, width, length), bf16),
            jax.ShapeDtypeStruct((HEADS, length, length), bf16),
            jax.ShapeDtypeStruct((width, length), bf16),
            jax.ShapeDtypeStruct((16, length), f32),
            jax.ShapeDtypeStruct((width, length), f32),
        ]
        + [jax.ShapeDtypeStruct(part, bf16)] * parts,
        compiler_params=pltpu.CompilerParams(vmem_limit_bytes=VMEM_LIMIT),
        cost_estimate=cost(14),
        name="layer",
    )(index, pieces, aug, cols, *wqkv, *weights, *sums, *after)
    return out[0], out[1:6], out[6:]


def back_kernel(index_ref, *refs, carried, after, parts, inner):
    take = Taker(refs)
    saved, og_ref, delta_ref, p_ref, saved_hbm, gres_hbm, w_hbm = take(7)
    sum_hbm = take(1 if carried else 0)
    bias_in = take(1 if carried else 0)
    take(after)
    (out_ref,) = take(1)
    part_refs = take(parts)
    grads, held, xt, gres, w_all = take(5)
    sum_in = take(1 if carried else 0)
    packed, sem = take(2)
    group = pl.program_id(0)
    width = og_ref.shape[0]
    copies = copies_of([saved_hbm.at[3], gres_hbm, w_hbm] + sum_hbm, [xt, gres, w_all] + sum_in, sem)

    @pl.when(group == 0)
    def _():
        for copy in copies:
            copy.start()

    back_heads(group, saved, og_ref, delta_ref, lambda h: p_ref.at[h], grads, held)

    @pl.when(group == GROUPS - 1)
    def _():
        for copy in copies:
            copy.wait()
        total = grads[...]
        acc = dot(xt[...], total, NT)
        bias = back_biases(total, width)
        if carried:
            acc = acc + sum_in[0][...]
            bias = bias + bias_in[0][...]
        per = width // 128
        for index in range(3 * per):
            packed[index * width : (index + 1) * width] = acc[:, index * 128 : (index + 1) * 128].astype(bf16)
        bias_rows = [bias[n : n + 1, i * 128 : (i + 1) * 128] for n in range(2) for i in range(per)]
        tail = packed.shape[0] - 3 * per * width
        bias_rows.append(jnp.zeros((tail - len(bias_rows), 128), f32))
        packed[3 * per * width :] = jnp.concatenate(bias_rows, axis=0).astype(bf16)
        emit(packed, index_ref[0], part_refs, inner)
        write_pieces((gres[...] + dot(w_all[...], total)).astype(bf16), out_ref)


def back(shared, saved, probs, og, delta, gres, w_all, sums, packed_rows, parts, inner, index, after):
    _, width, length = saved.shape
    count, _, span, _ = shared.shape
    first = 1 + 7 + len(sums)
    after = [shared] + list(after)
    full = lambda shape: pl.BlockSpec(shape, lambda g, i: (0,) * len(shape))
    part = (packed_rows // parts, 128)
    out = pl.pallas_call(
        functools.partial(back_kernel, carried=bool(sums), after=len(after), parts=parts, inner=inner),
        grid_spec=pltpu.PrefetchScalarGridSpec(
            num_scalar_prefetch=1,
            grid=(GROUPS,),
            in_specs=[
                full((3, width, length)),
                full((width, length)),
                full((16, length)),
                pl.BlockSpec((PER_GROUP, length, length), lambda g, i: (g, 0, 0)),
            ]
            + [ANY] * 3
            + ([ANY, full((8, width))] if sums else [])
            + [ANY] * len(after),
            out_specs=[pl.BlockSpec((count, 1, span, width), lambda g, i: (0, 1, 0, 0))] + [full(part)] * parts,
            scratch_shapes=[
                pltpu.VMEM((3 * width, length), bf16),
                pltpu.VMEM((PER_GROUP, length, length), bf16),
                pltpu.VMEM((width, length), bf16),
                pltpu.VMEM((width, length), f32),
                pltpu.VMEM(w_all.shape, bf16),
            ]
            + ([pltpu.VMEM((width, 3 * width), f32)] if sums else [])
            + [pltpu.VMEM((packed_rows, 128), bf16), pltpu.SemaphoreType.DMA((4,))],
        ),
        out_shape=[jax.ShapeDtypeStruct((count, 2, span, width), bf16)] + [jax.ShapeDtypeStruct(part, bf16)] * parts,
        input_output_aliases={first: 0},
        compiler_params=pltpu.CompilerParams(vmem_limit_bytes=VMEM_LIMIT),
        cost_estimate=cost(9),
        name="back",
    )(index, saved, og, delta, probs, saved, gres, w_all, *sums, *after)
    return out[0], out[1:]


def exchange(pieces, axis, devices, unit=1):
    moved = [pieces[0]]
    for shift in range(1, len(pieces)):
        moved.append(lax.ppermute(pieces[shift], axis, [(i, i ^ (shift * unit)) for i in range(devices)]))
    return moved


def tree_sum(blocks):
    while len(blocks) > 1:
        blocks = [left + right for left, right in zip(blocks[::2], blocks[1::2])]
    return blocks[0]


def combine_kernel(index_ref, *refs, inputs, after, through, parts, inner):
    total = tree_sum([ref[...].astype(f32) for ref in refs[:inputs]]).astype(bf16)
    refs = refs[inputs + after + through :]
    outs = refs[:parts]
    if parts == 1:
        outs[0][...] = total
    else:
        packed = refs[-1]
        packed[...] = total
        emit(packed, index_ref[0], outs, inner)


def combine(blocks, parts, inner, index, after=(), through=()):
    rows, width = blocks[0].shape
    part = (rows // parts, width)
    first = 1 + len(blocks) + len(after)
    full = lambda s: pl.BlockSpec(s, lambda i, j: (0, 0))
    out = pl.pallas_call(
        functools.partial(
            combine_kernel, inputs=len(blocks), after=len(after), through=len(through), parts=parts, inner=inner
        ),
        grid_spec=pltpu.PrefetchScalarGridSpec(
            num_scalar_prefetch=1,
            grid=(1,),
            in_specs=[full((rows, width))] * len(blocks) + [ANY] * (len(after) + len(through)),
            out_specs=[full(part)] * parts + [ANY] * len(through),
            scratch_shapes=[pltpu.VMEM((rows, width), bf16)] if parts > 1 else [],
        ),
        out_shape=[jax.ShapeDtypeStruct(part, bf16)] * parts
        + [jax.ShapeDtypeStruct(a.shape, a.dtype) for a in through],
        input_output_aliases={first + i: parts + i for i in range(len(through))},
        compiler_params=pltpu.CompilerParams(vmem_limit_bytes=12 * 2**20),
        cost_estimate=cost(1),
        name="combine",
    )(index, *blocks, *after, *through)
    return out[:parts], out[parts:]


def merge_kernel(index_ref, *refs, count, after, parts, inner):
    left = tree_sum([ref[...].astype(f32) for ref in refs[:count]])
    right = tree_sum([ref[...].astype(f32) for ref in refs[count : 2 * count]])
    packed = refs[-1]
    packed[...] = jnp.concatenate([left, right], axis=1).astype(bf16)
    emit(packed, index_ref[0], refs[2 * count + after : -1], inner)


def merge(lefts, rights, stage, after=()):
    rows, left = lefts[0].shape
    width = left + rights[0].shape[1]
    parts = stage[3]
    full = lambda s: pl.BlockSpec(s, lambda i, j: (0, 0))
    return pl.pallas_call(
        functools.partial(merge_kernel, count=len(lefts), after=len(after), parts=parts, inner=stage[4]),
        grid_spec=pltpu.PrefetchScalarGridSpec(
            num_scalar_prefetch=1,
            grid=(1,),
            in_specs=[full(b.shape) for b in list(lefts) + list(rights)] + [ANY] * len(after),
            out_specs=[full((rows // parts, width))] * parts,
            scratch_shapes=[pltpu.VMEM((rows, width), bf16)],
        ),
        out_shape=[jax.ShapeDtypeStruct((rows // parts, width), bf16)] * parts,
        compiler_params=pltpu.CompilerParams(vmem_limit_bytes=12 * 2**20),
        cost_estimate=cost(2),
        name="merge",
    )(place_of(stage), *lefts, *rights, *after)


def put_together(refs, out, index, inner):
    size = refs[0].shape[0] // inner
    for shift, ref in enumerate(refs):
        for block in range(inner):
            start = pl.multiple_of((block * len(refs) + (index ^ shift)) * size, 16)
            out[pl.ds(start, size), :] = ref[block * size : (block + 1) * size]


def assemble_kernel(index_ref, *refs, inputs, after, inner):
    put_together(refs[:inputs], refs[inputs + after], index_ref[0], inner)


def assemble(blocks, stage, after=(), through=()):
    rows, width = blocks[0].shape
    full = lambda s: pl.BlockSpec(s, lambda i, j: (0, 0))
    shape = (rows * len(blocks), width)
    first = 1 + len(blocks) + len(after)
    after = list(after) + list(through)
    out = pl.pallas_call(
        functools.partial(assemble_kernel, inputs=len(blocks), after=len(after), inner=stage[4]),
        grid_spec=pltpu.PrefetchScalarGridSpec(
            num_scalar_prefetch=1,
            grid=(1,),
            in_specs=[full((rows, width))] * len(blocks) + [ANY] * len(after),
            out_specs=[full(shape)] + [ANY] * len(through),
        ),
        out_shape=[jax.ShapeDtypeStruct(shape, bf16)] + [jax.ShapeDtypeStruct(a.shape, a.dtype) for a in through],
        input_output_aliases={first + i: 1 + i for i in range(len(through))},
        compiler_params=pltpu.CompilerParams(vmem_limit_bytes=12 * 2**20),
        cost_estimate=cost(1),
        name="assemble",
    )(place_of(stage), *blocks, *after)
    return out[0], out[1:]


def place_kernel(*refs, rows):
    outs = refs[-2:]
    row = pl.program_id(0)
    for number in range(rows):

        @pl.when(row == number)
        def _(number=number):
            for which in range(2):
                outs[which][...] = refs[2 * number + which][...].astype(outs[which].dtype)


def place(sources):
    rows = len(sources)
    count, _, span, width = sources[0][0][0].shape
    shape = (count, rows, span, width)
    in_specs = []
    arrays = []
    for row in sources:
        for sent, at in row:
            in_specs.append(pl.BlockSpec((count, 1, span, width), lambda r, at=at: (0, at, 0, 0)))
            arrays.append(sent)
    out_spec = pl.BlockSpec((count, 1, span, width), lambda r: (0, r, 0, 0))
    layer_out, grad = pl.pallas_call(
        functools.partial(place_kernel, rows=rows),
        grid=(rows,),
        in_specs=in_specs,
        out_specs=[out_spec, out_spec],
        out_shape=[jax.ShapeDtypeStruct(shape, bf16), jax.ShapeDtypeStruct(shape, f32)],
        compiler_params=pltpu.CompilerParams(vmem_limit_bytes=VMEM_LIMIT),
        cost_estimate=cost(5),
        name="place",
    )(*arrays)
    return layer_out.reshape(count * rows, span, width), grad.reshape(count * rows, span, width)


def sum_stages(sizes):
    stages = []
    for axis in ("rows", "seq"):
        devices = sizes[axis]
        unit = 1
        while unit < devices:
            size = 2 if unit == 1 and devices.bit_length() % 2 == 0 else 4
            stages.append((axis, devices, unit, size, devices // (unit * size)))
            unit *= size
    return stages


def place_of(stage):
    axis, _, unit, size, _ = stage
    return ((lax.axis_index(axis) // unit) % size).astype(jnp.int32).reshape(1)


def send_parts(parts, stage):
    axis, devices, unit, _, _ = stage
    return exchange(parts, axis, devices, unit)


def cut_for(taken, stage, after=(), through=()):
    return combine(taken, stage[3], stage[4], place_of(stage), after, through)


def add(taken, after=()):
    return combine(taken, 1, 1, jnp.zeros((1,), jnp.int32), after)[0][0]


def unpack_kernel(index_ref, *refs, inputs, after, inner):
    down, up, out, *biases = refs[inputs + after : inputs + after + 10]
    query, key, value, bias_q, bias_v = refs[inputs + after + 10 : -1]
    block = refs[-1]
    put_together(refs[:inputs], block, index_ref[0], inner)
    ff, width = down.shape
    per = ff // width
    down[...] = block[:ff, :width].astype(f32)
    for index in range(per):
        rows = slice(ff + index * width, ff + (index + 1) * width)
        up[:, index * width : (index + 1) * width] = block[rows, :width].astype(f32)
    out[...] = block[2 * ff : 2 * ff + width, :width].astype(f32)
    rows = block[2 * ff + width : 2 * ff + width + 16, :width].astype(f32)
    for index, ref in enumerate(biases[:-1]):
        ref[...] = rows[index]
    biases[-1][...] = jnp.concatenate([rows[len(biases) - 1 + i] for i in range(per)], axis=0)
    per = width // 128
    for number, ref in enumerate((query, key, value)):
        for index in range(per):
            start = (number * per + index) * width
            ref[:, index * 128 : (index + 1) * 128] = block[start : start + width, width:].astype(f32)
    rows = block[3 * per * width : 3 * per * width + 16, width:].astype(f32)
    for number, ref in enumerate((bias_q, bias_v)):
        ref[...] = jnp.concatenate([rows[number * per + i] for i in range(per)], axis=0)


def unpack(blocks, stage, shapes, after=()):
    rows, width = blocks[0].shape
    full = lambda s: pl.BlockSpec(s, lambda i, j: (0,) * len(s))
    return pl.pallas_call(
        functools.partial(unpack_kernel, inputs=len(blocks), after=len(after), inner=stage[4]),
        grid_spec=pltpu.PrefetchScalarGridSpec(
            num_scalar_prefetch=1,
            grid=(1,),
            in_specs=[full((rows, width))] * len(blocks) + [ANY] * len(after),
            out_specs=[full(s) for s in shapes],
            scratch_shapes=[pltpu.VMEM((rows * len(blocks), width), bf16)],
        ),
        out_shape=[jax.ShapeDtypeStruct(s, f32) for s in shapes],
        compiler_params=pltpu.CompilerParams(vmem_limit_bytes=28 * 2**20),
        cost_estimate=cost(4),
        name="unpack",
    )(place_of(stage), *blocks, *after)


def round_up(value, unit):
    return -(-value // unit) * unit


def body(
    tokens, lengths, w_query, b_query, w_key, w_value, b_value, w_out, b_out, gain_attn, shift_attn,
    w_up, b_up, w_down, b_down, gain_ffn, shift_ffn, cotangent, *, sizes,
):
    count = sizes["seq"]
    devices = count * sizes["rows"]
    row_count, span, width = tokens.shape
    ff = w_up.shape[1]
    length = span * count
    rows = row_count // count
    me = lax.axis_index("seq")
    stages = sum_stages(sizes)
    row_stages, seq_stages = [[stage for stage in stages if stage[0] == axis] for axis in ("rows", "seq")]
    first = stages[0]
    index = place_of(first)
    later_rows = round_up(2 * ff + width + 16, 16 * devices)
    first_rows = later_rows

    def split(array):
        return array.reshape(count, rows, 1, span, width)

    def to_owners(parts):
        return lax.all_to_all(parts, "seq", 0, 0, tiled=True)

    parts = [jnp.concatenate([split(tokens)[:, row], split(cotangent)[:, row]], axis=1) for row in range(rows)]
    given = {0: to_owners(parts[0])}

    bounds = lax.dynamic_slice_in_dim(jnp.cumsum(lengths, axis=1), me * rows, rows, 0)
    spots = jnp.arange(length, dtype=jnp.int32)
    segment = jnp.sum((spots[None, None, :] >= bounds[:, :, None]).astype(jnp.int32), axis=1)
    ids = jnp.arange(2 * AUG, dtype=jnp.int32)[None, :, None]
    same = segment[:, None, :] == ids % AUG
    aug = jnp.where(ids < AUG, jnp.where(same, 1.0, 0.0), jnp.where(same | (ids % AUG >= lengths.shape[1]), 0.0, -BIG))
    aug = aug.astype(bf16)

    vectors = [b_query, b_value, b_out, gain_attn, shift_attn, b_down, gain_ffn, shift_ffn]
    vectors = jnp.concatenate([jnp.stack(vectors), b_up.reshape(-1, width)], axis=0)
    (wq_t, wk_t, wv_t, wo_t, wup_t, wdn_t, cols), waiting = prepare(
        (w_query, w_key, w_value, w_out, w_up, w_down), vectors, aug, parts[1:]
    )
    if rows > 1:
        given[1] = to_owners(waiting[0])
    dense_weights = (wo_t, w_out, wup_t, w_up, wdn_t, w_down)
    w_all = jnp.concatenate([w_query, w_key, w_value], axis=1)

    wqkv = (wq_t, wk_t, wv_t)
    last = rows - 1

    def return_pieces(array):
        return lax.all_to_all(array, "seq", 0, 0, tiled=True)

    carried = []
    for row in range(last):
        through = [waiting[row + 1]] if row + 2 < rows else []
        sums, shared, through = whole(
            given[row], row, 2 * last, aug, cols, wqkv, dense_weights + (w_all,), carried, through
        )
        if row + 2 < rows:
            given[row + 2] = to_owners(through[0])
        carried = list(sums) + [shared]
    places = []
    if last:
        moved = return_pieces(shared)
        places = [((moved, 2 * row), (moved, 2 * row + 1)) for row in range(last)]
    shared, saved, later = layer(
        given[last], last, aug, cols, wqkv, dense_weights, (carried[:3] + carried[4:5]) if carried else [],
        later_rows, first[3], first[4], index, [],
    )
    keys, probs, og, delta, gres = saved
    taken = send_parts(later, first)
    ends, early = back(
        shared, keys, probs, og, delta, gres, w_all, (carried[3:4] + carried[5:6]) if carried else [], first_rows,
        first[3], first[4], index, [],
    )
    after = list(early[:1])
    for stage in row_stages[1:]:
        cut, _ = cut_for(taken, stage, after)
        taken = send_parts(cut, stage)
        after = list(cut[:1])
    given_early = send_parts(early, first)
    for stage in row_stages[1:]:
        cut, (ends,) = cut_for(given_early, stage, after, [ends])
        given_early = send_parts(cut, stage)
        after = list(cut[:1])
    ends = return_pieces(ends)
    parts = merge(taken, given_early, seq_stages[0], [moved] if last else [])
    for number, stage in enumerate(seq_stages):
        taken = send_parts(parts, stage)
        if number + 1 < len(seq_stages):
            parts, _ = cut_for(taken, seq_stages[number + 1])
    block = add(taken)
    layer_out, grad_tokens = place(places + [((ends, 0), (ends, 1))])
    for number, stage in enumerate(reversed(stages[1:])):
        taken = send_parts([block] * stage[3], stage)
        block, _ = assemble(taken, stage, [layer_out, grad_tokens] if number == len(stages) - 2 else [])
    shapes = [(ff, width), (width, ff), (width, width)] + [(width,)] * 6 + [(ff,)] + [(width, width)] * 3 + [(width,)] * 2
    (
        grad_down, grad_up, grad_output, grad_gain2, grad_shift2, grad_dnbias, grad_gain1, grad_shift1, grad_obias,
        grad_upbias, grad_query, grad_key, grad_value, grad_qbias, grad_vbias,
    ) = unpack(send_parts([block] * first[3], first), first, shapes)
    return (
        layer_out, grad_tokens, grad_query, grad_qbias, grad_key, grad_value, grad_vbias, grad_output, grad_obias,
        grad_gain1, grad_shift1, grad_up, grad_upbias, grad_down, grad_dnbias, grad_gain2, grad_shift2,
    )


def solution(mesh):
    split = P("rows", "seq", None)
    in_specs = (split, P("rows", None)) + (P(),) * 15 + (split,)
    out_specs = (split, split) + (P(),) * 15
    sizes = dict(mesh.shape)
    return jax.shard_map(
        functools.partial(body, sizes=sizes), mesh=mesh, in_specs=in_specs, out_specs=out_specs, check_vma=False
    )
```

```python
import functools
import math

import jax
import jax.numpy as jnp
from jax import lax
from jax.experimental import pallas as pl
from jax.experimental.pallas import tpu as pltpu
from jax.sharding import PartitionSpec as P

HEADS = 12
HD = 32
GROUPS = 3
PER_GROUP = HEADS // GROUPS
AUG = 16
BIG = 2.0**100
SMALL_SCORE = 60.0
EPSILON = 1e-05
SCALE = HD ** (-0.5)
LOG2E = math.log2(math.e)
Q_FACTOR = SCALE * LOG2E
LN2 = math.log(2.0)
VMEM_LIMIT = 60 * 2**20

f32 = jnp.float32
bf16 = jnp.bfloat16
NN = (((1,), (0,)), ((), ()))
NT = (((1,), (1,)), ((), ()))
TN = (((0,), (0,)), ((), ()))


def dot(left, right, dims=NN):
    return lax.dot_general(left, right, dims, preferred_element_type=f32)


def fold_lanes(values):
    total = values[:, :128]
    for start in range(128, values.shape[1], 128):
        total = total + values[:, start : start + 128]
    return total


def row_sum(partial):
    return jnp.sum(partial.T, axis=0, keepdims=True)


def normalize(hidden):
    scale = 1.0 / hidden.shape[0]
    centre = hidden - jnp.sum(hidden, axis=0, keepdims=True) * scale
    variance = jnp.sum(centre * centre, axis=0, keepdims=True) * scale
    inverse = lax.rsqrt(variance + EPSILON)
    return centre * inverse, inverse


def normalize_back(upstream, scaled, inverse):
    scale = 1.0 / upstream.shape[0]
    mean = jnp.sum(upstream, axis=0, keepdims=True) * scale
    spread = jnp.sum(upstream * scaled, axis=0, keepdims=True) * scale
    return inverse * (upstream - mean - scaled * spread)


def gelu_parts(v):
    cdf = 0.5 + 0.5 * lax.erf(v * 0.5**0.5)
    bell = jnp.exp2((v * v) * (-0.5 * LOG2E))
    return v * cdf, cdf + v * bell * (2.0 * math.pi) ** (-0.5)


def prepare_kernel(*refs, through):
    sources, rows = refs[:6], refs[6]
    targets, columns = refs[8 + through : 14 + through], refs[14 + through]
    for source, target in zip(sources, targets):
        target[...] = source[...].T
    width = rows.shape[1]
    columns[...] = jnp.concatenate([rows[...], jnp.zeros((128 - rows.shape[0], width), f32)], axis=0).T


def prepare(weights, rows, aug, through):
    full = lambda shape: pl.BlockSpec(shape, lambda i: (0, 0))
    shapes = [w.shape[::-1] for w in weights]
    out = pl.pallas_call(
        functools.partial(prepare_kernel, through=len(through)),
        grid=(1,),
        in_specs=[full(w.shape) for w in weights] + [full(rows.shape)] + [ANY] * (1 + len(through)),
        out_specs=[full(s) for s in shapes] + [full((rows.shape[1], 128))] + [ANY] * len(through),
        out_shape=[jax.ShapeDtypeStruct(s, bf16) for s in shapes]
        + [jax.ShapeDtypeStruct((rows.shape[1], 128), f32)]
        + [jax.ShapeDtypeStruct(a.shape, a.dtype) for a in through],
        input_output_aliases={8 + i: 7 + i for i in range(len(through))},
        compiler_params=pltpu.CompilerParams(vmem_limit_bytes=VMEM_LIMIT),
        cost_estimate=cost(5),
        name="prepare",
    )(*weights, rows, aug, *through)
    return out[:7], out[7:]


def cost(micros):
    return pl.CostEstimate(flops=int(micros * 1e5), transcendentals=0, bytes_accessed=int(micros * 1e3))


B_QUERY, B_VALUE, B_OUT, GAIN1, SHIFT1, B_DOWN, GAIN2, SHIFT2, B_UP = range(9)


ANY = pl.BlockSpec(memory_space=pl.ANY)


def head_sums(values):
    return jnp.sum(values.reshape(HEADS, HD, values.shape[1]), axis=1)


def emit(packed, index, outs, inner):
    size = outs[0].shape[0] // inner
    for shift, ref in enumerate(outs):
        for block in range(inner):
            start = pl.multiple_of((block * len(outs) + (index ^ shift)) * size, 16)
            ref[block * size : (block + 1) * size] = packed[pl.ds(start, size), :]


class Taker:
    def __init__(self, refs):
        self.refs = list(refs)

    def __call__(self, number):
        taken = self.refs[:number]
        del self.refs[:number]
        return taken


def column_of(cols, index):
    return cols[:, index : index + 1]


def project_row(piece_ref, cols, wq, wk, wv, saved, small_ref):
    xt = jnp.concatenate([piece_ref[i, 0].T for i in range(piece_ref.shape[0])], axis=1)
    query = (dot(wq[...], xt) + column_of(cols, B_QUERY)) * Q_FACTOR
    key = dot(wk[...], xt)
    saved[0] = query.astype(bf16)
    saved[1] = key.astype(bf16)
    saved[2] = (dot(wv[...], xt) + column_of(cols, B_VALUE)).astype(bf16)
    saved[3] = xt
    bounds = [
        jnp.max(head_sums(query * query), axis=1, keepdims=True),
        jnp.max(head_sums(key * key), axis=1, keepdims=True),
    ]
    small_ref[0] = (jnp.max(bounds[0] * bounds[1]) < SMALL_SCORE**2).astype(jnp.int32)


def head_rows(group, h):
    return pl.ds(pl.multiple_of((group * PER_GROUP + h) * HD, HD), HD)


def attend_heads(group, saved, aug_ref, probs, att_ref, stat_ref, small_ref):
    length = saved.shape[2]
    ones = jnp.ones((AUG, length), bf16)

    def score(h):
        keys = jnp.concatenate([saved[1, head_rows(group, h), :], aug_ref[0, AUG:]], axis=0)
        query = jnp.concatenate([saved[0, head_rows(group, h), :], aug_ref[0, :AUG]], axis=0)
        return dot(keys, query, TN)

    def mix(h):
        values = jnp.concatenate([saved[2, head_rows(group, h), :], ones], axis=0)
        mixed = dot(values, probs(h)[...])
        inverse = 1.0 / mixed[HD : HD + 1]
        att_ref[head_rows(group, h), :] = mixed[:HD] * inverse
        stat_ref[pl.ds(group * PER_GROUP + h, 1), :] = inverse

    def heads(shifted):
        scores = score(0)
        for h in range(PER_GROUP):
            following = score(h + 1) if h + 1 < PER_GROUP else None
            if h >= 1:
                mix(h - 1)
            if shifted:
                scores = scores - jnp.max(scores, axis=0, keepdims=True)
            probs(h)[...] = jnp.exp2(scores).astype(bf16)
            scores = following
        mix(PER_GROUP - 1)

    @pl.when(small_ref[0] == 1)
    def _():
        heads(False)

    @pl.when(small_ref[0] == 0)
    def _():
        heads(True)


def dense_row(piece_ref, cols, saved, att_ref, stat_ref, weights, sums, carried, arriving, write_out, summed, og_ref, delta_ref, gres_ref):
    wo_t, wo, wup_t, wup, wdn_t, wdn = weights
    acc_dn, acc_up, acc_out = sums
    ff = acc_dn.shape[0]
    width = att_ref.shape[0]

    def column(index):
        return column_of(cols, index)

    def add(number, value):
        ref = sums[number]
        if arriving:
            arriving[number].wait()
        ref[...] = ref[...] + value if carried else value
        summed(number)

    att = att_ref[...]
    att_b = att.astype(bf16)
    res1 = saved[3].astype(f32) + dot(wo_t[...], att_b) + column(B_OUT)
    scaled1, inverse1 = normalize(res1)
    normed = scaled1 * column(GAIN1) + column(SHIFT1)
    normed_b = normed.astype(bf16)
    b_up = jnp.concatenate([column(B_UP + i) for i in range(ff // width)], axis=0)
    act, slope = gelu_parts(dot(wup_t[...], normed_b) + b_up)
    act_b = act.astype(bf16)
    res2 = normed + dot(wdn_t[...], act_b) + column(B_DOWN)
    scaled2, inverse2 = normalize(res2)
    write_out((scaled2 * column(GAIN2) + column(SHIFT2)).astype(bf16))
    cot = jnp.concatenate([piece_ref[i, 1].T for i in range(piece_ref.shape[0])], axis=1).astype(f32)
    gres2 = normalize_back(cot * column(GAIN2), scaled2, inverse2)
    down_b = gres2.astype(bf16)
    up_b = (dot(wdn[...], down_b) * slope).astype(bf16)
    add(0, dot(act_b, down_b, NT))
    gnormed = gres2 + dot(wup[...], up_b)
    add(1, dot(normed_b, up_b, NT))
    gres1 = normalize_back(gnormed * column(GAIN1), scaled1, inverse1)
    gres_ref[...] = gres1
    branch_b = gres1.astype(bf16)
    og = dot(wo[...], branch_b)
    add(2, dot(att_b, branch_b, NT))
    for h in range(HEADS):
        part = slice(h * HD, (h + 1) * HD)
        scaled_og = (og[part] * stat_ref[h : h + 1, :]).astype(bf16)
        og_ref[part, :] = scaled_og
        delta_ref[h : h + 1, :] = jnp.sum(scaled_og.astype(f32) * att[part], axis=0, keepdims=True)
    biases = [cot * scaled2, cot, down_b.astype(f32), gnormed * scaled1, gnormed, branch_b.astype(f32)]
    bias_rows = [row_sum(fold_lanes(value)) for value in biases]
    up_sum = fold_lanes(up_b.astype(f32))
    bias_rows += [row_sum(up_sum[i * width : (i + 1) * width]) for i in range(ff // width)]
    bias_rows.append(jnp.zeros((16 - len(bias_rows), width), f32))
    return jnp.concatenate(bias_rows, axis=0)


def back_heads(group, saved, og_ref, delta_ref, probs, grads, held):
    length = og_ref.shape[1]
    width = og_ref.shape[0]
    sign = jnp.where(lax.broadcasted_iota(jnp.int32, (AUG, length), 0) < 3, 1.0, 0.0).astype(bf16)

    def grad_probs(h):
        delta = delta_ref[pl.ds(group * PER_GROUP + h, 1), :]
        first = delta.astype(bf16)
        rest = delta - first.astype(f32)
        second = rest.astype(bf16)
        third = (rest - second.astype(f32)).astype(bf16)
        aug = jnp.concatenate(
            [-first.astype(f32), -second.astype(f32), -third.astype(f32), jnp.zeros((AUG - 3, length), f32)], axis=0
        ).astype(bf16)
        left = jnp.concatenate([saved[2, head_rows(group, h), :], sign], axis=0)
        right = jnp.concatenate([og_ref[head_rows(group, h), :], aug], axis=0)
        return dot(left, right, TN)

    def target(which, h):
        return pl.ds(pl.multiple_of(which * width + (group * PER_GROUP + h) * HD, HD), HD)

    for h in range(PER_GROUP):
        held[h] = (probs(h)[...].astype(f32) * grad_probs(h)).astype(bf16)
        grads[target(2, h), :] = dot(og_ref[head_rows(group, h), :], probs(h)[...], NT).astype(bf16)
    for h in range(PER_GROUP):
        grads[target(0, h), :] = (dot(saved[1, head_rows(group, h), :], held[h]) * SCALE).astype(bf16)
        grads[target(1, h), :] = (dot(saved[0, head_rows(group, h), :], held[h], NT) * LN2).astype(bf16)


def back_biases(total, width):
    rows = [row_sum(fold_lanes(part.astype(f32))) for part in (total[:width], total[2 * width :])]
    return jnp.concatenate(rows + [jnp.zeros((6, width), f32)], axis=0)


def write_pieces(values, ref, at=0):
    span = ref.shape[2]
    for piece in range(ref.shape[0]):
        ref[piece, at] = values[:, piece * span : (piece + 1) * span].T


def copies_of(sources, targets, sem):
    return [pltpu.make_async_copy(a, b, sem.at[i]) for i, (a, b) in enumerate(zip(sources, targets))]


def whole_kernel(*refs, carried, through):
    take = Taker(refs)
    (piece_ref,) = take(1)
    aug_ref, cols, wq, wk, wv = take(5)
    weights_hbm = take(7)
    sums_hbm = take(4 if carried else 0)
    bias_in = take(2 if carried else 0)
    take((1 if carried else 0) + through)
    (out_ref,) = take(1)
    sums_out = take(4)
    bias_out = take(2)
    take(through)
    saved, p_all, att_ref, stat_ref, og_ref, delta_ref, gres_ref, grads, held = take(9)
    weights = take(7)
    sums = take(4)
    small_ref, weight_sem, sum_sem, out_sem = take(4)
    step = pl.program_id(0)
    width = att_ref.shape[0]
    weight_copies = copies_of(weights_hbm, weights, weight_sem)
    sum_copies = copies_of(sums_hbm, sums, sum_sem)
    out_copies = copies_of(sums, sums_out, out_sem)

    @pl.when(step == 0)
    def _():
        for copy in weight_copies + sum_copies:
            copy.start()
        project_row(piece_ref, cols, wq, wk, wv, saved, small_ref)

    @pl.when(step < GROUPS)
    def _():
        attend_heads(step, saved, aug_ref, lambda h: p_all.at[step * PER_GROUP + h], att_ref, stat_ref, small_ref)

    @pl.when(step == GROUPS - 1)
    def _():
        for copy in weight_copies[:6] + sum_copies[:3]:
            copy.wait()
        total = dense_row(
            piece_ref, cols, saved, att_ref, stat_ref, weights[:6], sums[:3], carried, [],
            lambda values: write_pieces(values, out_ref, 0), lambda number: out_copies[number].start(),
            og_ref, delta_ref, gres_ref,
        )
        bias_out[0][...] = total + bias_in[0][...] if carried else total

    @pl.when(step >= GROUPS)
    def _():
        group = step - GROUPS
        back_heads(group, saved, og_ref, delta_ref, lambda h: p_all.at[group * PER_GROUP + h], grads, held)

    @pl.when(step == 2 * GROUPS - 1)
    def _():
        for copy in weight_copies[6:] + sum_copies[3:]:
            copy.wait()
        total = grads[...]
        acc = dot(saved[3], total, NT)
        sums[3][...] = sums[3][...] + acc if carried else acc
        out_copies[3].start()
        bias = back_biases(total, width)
        bias_out[1][...] = bias + bias_in[1][...] if carried else bias
        result = (gres_ref[...] + dot(weights[6][...], total)).astype(bf16)
        write_pieces(result, out_ref, 1)
        for copy in out_copies:
            copy.wait()


def whole(pieces, row, height, aug, cols, wqkv, weights, carried, through):
    count, _, span, width = pieces.shape
    length = span * count
    ff = weights[3].shape[1]
    full = lambda shape: pl.BlockSpec(shape, lambda g: (0,) * len(shape))
    sum_shapes = [(ff, width), (width, ff), (width, width), (width, 3 * width)]
    bias_shapes = [(16, width), (8, width)]
    first = 1 + 5 + 7 + len(carried)
    aliases = {first + i: 7 + i for i in range(len(through))}
    out = pl.pallas_call(
        functools.partial(whole_kernel, carried=bool(carried), through=len(through)),
        grid=(2 * GROUPS,),
        in_specs=[full(pieces.shape)]
        + [pl.BlockSpec((1, 2 * AUG, length), lambda g: (row, 0, 0)), full(cols.shape)]
        + [full(w.shape) for w in wqkv]
        + [ANY] * 7
        + ([ANY] * 4 + [full(s) for s in bias_shapes] + [ANY] if carried else [])
        + [ANY] * len(through),
        out_specs=[pl.BlockSpec((count, 2, span, width), lambda g: (0, row, 0, 0))]
        + [ANY] * 4
        + [full(s) for s in bias_shapes]
        + [ANY] * len(through),
        scratch_shapes=[
            pltpu.VMEM((4, width, length), bf16),
            pltpu.VMEM((HEADS, length, length), bf16),
            pltpu.VMEM((width, length), f32),
            pltpu.VMEM((16, length), f32),
            pltpu.VMEM((width, length), bf16),
            pltpu.VMEM((16, length), f32),
            pltpu.VMEM((width, length), f32),
            pltpu.VMEM((3 * width, length), bf16),
            pltpu.VMEM((PER_GROUP, length, length), bf16),
        ]
        + [pltpu.VMEM(w.shape, bf16) for w in weights]
        + [pltpu.VMEM(s, f32) for s in sum_shapes]
        + [
            pltpu.SMEM((1,), jnp.int32),
            pltpu.SemaphoreType.DMA((7,)),
            pltpu.SemaphoreType.DMA((4,)),
            pltpu.SemaphoreType.DMA((4,)),
        ],
        out_shape=[jax.ShapeDtypeStruct((count, height, span, width), bf16)]
        + [jax.ShapeDtypeStruct(s, f32) for s in sum_shapes + bias_shapes]
        + [jax.ShapeDtypeStruct(a.shape, a.dtype) for a in through],
        input_output_aliases={first - 1: 0, **aliases} if carried else aliases,
        compiler_params=pltpu.CompilerParams(vmem_limit_bytes=VMEM_LIMIT),
        cost_estimate=cost(20),
        name="whole",
    )(pieces, aug, cols, *wqkv, *weights, *carried, *through)
    return out[1:7], out[0], out[7:]


def layer_kernel(index_ref, *refs, carried, after, parts, inner):
    take = Taker(refs)
    (piece_ref,) = take(1)
    aug_ref, cols, wq, wk, wv = take(5)
    weights_hbm = take(6)
    sums_hbm = take(3 if carried else 0)
    bias_in = take(1 if carried else 0)
    take(after)
    (out_ref,) = take(1)
    saved_hbm, p_hbm, og_ref, delta_ref, gres_ref = take(5)
    part_refs = take(parts)
    saved, p_buf, att_ref, stat_ref = take(4)
    weights = take(6)
    sums = take(3)
    packed, small_ref, weight_sem, sum_sem, p_sem, saved_sem, part_sem = take(7)
    group = pl.program_id(0)
    width = att_ref.shape[0]
    weight_copies = copies_of(weights_hbm, weights, weight_sem)
    sum_copies = copies_of(sums_hbm, sums, sum_sem)
    saved_copy = pltpu.make_async_copy(saved, saved_hbm, saved_sem)
    slot = lax.rem(group, 2)

    def p_copy(number):
        start = number * PER_GROUP
        return pltpu.make_async_copy(
            p_buf.at[lax.rem(number, 2)], p_hbm.at[pl.ds(start, PER_GROUP)], p_sem.at[lax.rem(number, 2)]
        )

    @pl.when(group == 0)
    def _():
        for copy in weight_copies + sum_copies:
            copy.start()
        project_row(piece_ref, cols, wq, wk, wv, saved, small_ref)
        saved_copy.start()

    @pl.when(group >= 2)
    def _():
        p_copy(group - 2).wait()

    attend_heads(group, saved, aug_ref, lambda h: p_buf.at[slot, h], att_ref, stat_ref, small_ref)
    p_copy(group).start()

    @pl.when(group == GROUPS - 1)
    def _():
        for copy in weight_copies:
            copy.wait()
        acc_dn, acc_up, acc_out = sums
        ff = acc_dn.shape[0]
        size = part_refs[0].shape[0] // inner
        part_copies = []

        def send(number):
            for shift, ref in enumerate(part_refs):
                start = pl.multiple_of((number * parts + (index_ref[0] ^ shift)) * size, 16)
                copy = pltpu.make_async_copy(
                    packed.at[pl.ds(start, size)], ref.at[pl.ds(number * size, size)], part_sem.at[shift * inner + number]
                )
                copy.start()
                part_copies.append(copy)

        def blocks_until(done):
            return done // (parts * size)

        def pack(number):
            if number == 0:
                packed[:ff] = acc_dn[...].astype(bf16)
                ready = range(blocks_until(ff))
            elif number == 1:
                for index in range(ff // width):
                    packed[ff + index * width : ff + (index + 1) * width] = acc_up[
                        :, index * width : (index + 1) * width
                    ].astype(bf16)
                ready = range(blocks_until(ff), blocks_until(2 * ff))
            else:
                packed[2 * ff : 2 * ff + width] = acc_out[...].astype(bf16)
                ready = []
            for block in ready:
                send(block)

        total = dense_row(
            piece_ref, cols, saved, att_ref, stat_ref, weights, sums, carried, sum_copies,
            lambda values: write_pieces(values, out_ref), pack, og_ref, delta_ref, gres_ref,
        )
        if carried:
            total = total + bias_in[0][...]
        packed[2 * ff + width : 2 * ff + width + 16] = total.astype(bf16)
        rest = packed.shape[0] - 2 * ff - width - 16
        if rest:
            packed[2 * ff + width + 16 :] = jnp.zeros((rest, width), bf16)
        for number in range(blocks_until(2 * ff), inner):
            send(number)
        for copy in part_copies:
            copy.wait()
        saved_copy.wait()
        for number in range(max(GROUPS - 2, 0), GROUPS):
            p_copy(number).wait()


def layer(pieces, row, aug, cols, wqkv, weights, sums, packed_rows, parts, inner, index, after):
    count, _, span, width = pieces.shape
    length = span * count
    ff = weights[3].shape[1]
    full = lambda shape: pl.BlockSpec(shape, lambda g, i: (0,) * len(shape))
    sum_shapes = [(ff, width), (width, ff), (width, width)]
    part = (packed_rows // parts, width)
    out = pl.pallas_call(
        functools.partial(
            layer_kernel, carried=bool(sums), after=len(after), parts=parts, inner=inner
        ),
        grid_spec=pltpu.PrefetchScalarGridSpec(
            num_scalar_prefetch=1,
            grid=(GROUPS,),
            in_specs=[full(pieces.shape)]
            + [pl.BlockSpec((1, 2 * AUG, length), lambda g, i: (row, 0, 0)), full(cols.shape)]
            + [full(w.shape) for w in wqkv]
            + [ANY] * 6
            + ([ANY] * 3 + [full((16, width))] if sums else [])
            + [ANY] * len(after),
            out_specs=[pl.BlockSpec((count, 1, span, width), lambda g, i: (0, 0, 0, 0))]
            + [ANY, ANY, full((width, length)), full((16, length)), full((width, length))]
            + [ANY] * parts,
            scratch_shapes=[
                pltpu.VMEM((4, width, length), bf16),
                pltpu.VMEM((2, PER_GROUP, length, length), bf16),
                pltpu.VMEM((width, length), f32),
                pltpu.VMEM((16, length), f32),
            ]
            + [pltpu.VMEM(w.shape, bf16) for w in weights]
            + [pltpu.VMEM(shape, f32) for shape in sum_shapes]
            + [
                pltpu.VMEM((packed_rows, width), bf16),
                pltpu.SMEM((1,), jnp.int32),
                pltpu.SemaphoreType.DMA((6,)),
                pltpu.SemaphoreType.DMA((3,)),
                pltpu.SemaphoreType.DMA((2,)),
                pltpu.SemaphoreType.DMA,
                pltpu.SemaphoreType.DMA((parts * inner,)),
            ],
        ),
        out_shape=[jax.ShapeDtypeStruct((count, 2, span, width), bf16)]
        + [
            jax.ShapeDtypeStruct((4, width, length), bf16),
            jax.ShapeDtypeStruct((HEADS, length, length), bf16),
            jax.ShapeDtypeStruct((width, length), bf16),
            jax.ShapeDtypeStruct((16, length), f32),
            jax.ShapeDtypeStruct((width, length), f32),
        ]
        + [jax.ShapeDtypeStruct(part, bf16)] * parts,
        compiler_params=pltpu.CompilerParams(vmem_limit_bytes=VMEM_LIMIT),
        cost_estimate=cost(14),
        name="layer",
    )(index, pieces, aug, cols, *wqkv, *weights, *sums, *after)
    return out[0], out[1:6], out[6:]


def back_kernel(index_ref, *refs, carried, after, parts, inner):
    take = Taker(refs)
    saved, og_ref, delta_ref, p_ref, saved_hbm, gres_hbm, w_hbm = take(7)
    sum_hbm = take(1 if carried else 0)
    bias_in = take(1 if carried else 0)
    take(after)
    (out_ref,) = take(1)
    part_refs = take(parts)
    grads, held, xt, gres, w_all = take(5)
    sum_in = take(1 if carried else 0)
    packed, sem = take(2)
    group = pl.program_id(0)
    width = og_ref.shape[0]
    copies = copies_of([saved_hbm.at[3], gres_hbm, w_hbm] + sum_hbm, [xt, gres, w_all] + sum_in, sem)

    @pl.when(group == 0)
    def _():
        for copy in copies:
            copy.start()

    back_heads(group, saved, og_ref, delta_ref, lambda h: p_ref.at[h], grads, held)

    @pl.when(group == GROUPS - 1)
    def _():
        for copy in copies:
            copy.wait()
        total = grads[...]
        acc = dot(xt[...], total, NT)
        bias = back_biases(total, width)
        if carried:
            acc = acc + sum_in[0][...]
            bias = bias + bias_in[0][...]
        per = width // 128
        for index in range(3 * per):
            packed[index * width : (index + 1) * width] = acc[:, index * 128 : (index + 1) * 128].astype(bf16)
        bias_rows = [bias[n : n + 1, i * 128 : (i + 1) * 128] for n in range(2) for i in range(per)]
        tail = packed.shape[0] - 3 * per * width
        bias_rows.append(jnp.zeros((tail - len(bias_rows), 128), f32))
        packed[3 * per * width :] = jnp.concatenate(bias_rows, axis=0).astype(bf16)
        emit(packed, index_ref[0], part_refs, inner)
        write_pieces((gres[...] + dot(w_all[...], total)).astype(bf16), out_ref)


def back(shared, saved, probs, og, delta, gres, w_all, sums, packed_rows, parts, inner, index, after):
    _, width, length = saved.shape
    count, _, span, _ = shared.shape
    first = 1 + 7 + len(sums)
    after = [shared] + list(after)
    full = lambda shape: pl.BlockSpec(shape, lambda g, i: (0,) * len(shape))
    part = (packed_rows // parts, 128)
    out = pl.pallas_call(
        functools.partial(back_kernel, carried=bool(sums), after=len(after), parts=parts, inner=inner),
        grid_spec=pltpu.PrefetchScalarGridSpec(
            num_scalar_prefetch=1,
            grid=(GROUPS,),
            in_specs=[
                full((3, width, length)),
                full((width, length)),
                full((16, length)),
                pl.BlockSpec((PER_GROUP, length, length), lambda g, i: (g, 0, 0)),
            ]
            + [ANY] * 3
            + ([ANY, full((8, width))] if sums else [])
            + [ANY] * len(after),
            out_specs=[pl.BlockSpec((count, 1, span, width), lambda g, i: (0, 1, 0, 0))] + [full(part)] * parts,
            scratch_shapes=[
                pltpu.VMEM((3 * width, length), bf16),
                pltpu.VMEM((PER_GROUP, length, length), bf16),
                pltpu.VMEM((width, length), bf16),
                pltpu.VMEM((width, length), f32),
                pltpu.VMEM(w_all.shape, bf16),
            ]
            + ([pltpu.VMEM((width, 3 * width), f32)] if sums else [])
            + [pltpu.VMEM((packed_rows, 128), bf16), pltpu.SemaphoreType.DMA((4,))],
        ),
        out_shape=[jax.ShapeDtypeStruct((count, 2, span, width), bf16)] + [jax.ShapeDtypeStruct(part, bf16)] * parts,
        input_output_aliases={first: 0},
        compiler_params=pltpu.CompilerParams(vmem_limit_bytes=VMEM_LIMIT),
        cost_estimate=cost(9),
        name="back",
    )(index, saved, og, delta, probs, saved, gres, w_all, *sums, *after)
    return out[0], out[1:]


def exchange(pieces, axis, devices, unit=1):
    moved = [pieces[0]]
    for shift in range(1, len(pieces)):
        moved.append(lax.ppermute(pieces[shift], axis, [(i, i ^ (shift * unit)) for i in range(devices)]))
    return moved


def tree_sum(blocks):
    while len(blocks) > 1:
        blocks = [left + right for left, right in zip(blocks[::2], blocks[1::2])]
    return blocks[0]


def combine_kernel(index_ref, *refs, inputs, after, through, parts, inner):
    total = tree_sum([ref[...].astype(f32) for ref in refs[:inputs]]).astype(bf16)
    refs = refs[inputs + after + through :]
    outs = refs[:parts]
    if parts == 1:
        outs[0][...] = total
    else:
        packed = refs[-1]
        packed[...] = total
        emit(packed, index_ref[0], outs, inner)


def combine(blocks, parts, inner, index, after=(), through=()):
    rows, width = blocks[0].shape
    part = (rows // parts, width)
    first = 1 + len(blocks) + len(after)
    full = lambda s: pl.BlockSpec(s, lambda i, j: (0, 0))
    out = pl.pallas_call(
        functools.partial(
            combine_kernel, inputs=len(blocks), after=len(after), through=len(through), parts=parts, inner=inner
        ),
        grid_spec=pltpu.PrefetchScalarGridSpec(
            num_scalar_prefetch=1,
            grid=(1,),
            in_specs=[full((rows, width))] * len(blocks) + [ANY] * (len(after) + len(through)),
            out_specs=[full(part)] * parts + [ANY] * len(through),
            scratch_shapes=[pltpu.VMEM((rows, width), bf16)] if parts > 1 else [],
        ),
        out_shape=[jax.ShapeDtypeStruct(part, bf16)] * parts
        + [jax.ShapeDtypeStruct(a.shape, a.dtype) for a in through],
        input_output_aliases={first + i: parts + i for i in range(len(through))},
        compiler_params=pltpu.CompilerParams(vmem_limit_bytes=12 * 2**20),
        cost_estimate=cost(1),
        name="combine",
    )(index, *blocks, *after, *through)
    return out[:parts], out[parts:]


def merge_kernel(index_ref, *refs, count, after, parts, inner):
    left = tree_sum([ref[...].astype(f32) for ref in refs[:count]])
    right = tree_sum([ref[...].astype(f32) for ref in refs[count : 2 * count]])
    packed = refs[-1]
    packed[...] = jnp.concatenate([left, right], axis=1).astype(bf16)
    emit(packed, index_ref[0], refs[2 * count + after : -1], inner)


def merge(lefts, rights, stage, after=()):
    rows, left = lefts[0].shape
    width = left + rights[0].shape[1]
    parts = stage[3]
    full = lambda s: pl.BlockSpec(s, lambda i, j: (0, 0))
    return pl.pallas_call(
        functools.partial(merge_kernel, count=len(lefts), after=len(after), parts=parts, inner=stage[4]),
        grid_spec=pltpu.PrefetchScalarGridSpec(
            num_scalar_prefetch=1,
            grid=(1,),
            in_specs=[full(b.shape) for b in list(lefts) + list(rights)] + [ANY] * len(after),
            out_specs=[full((rows // parts, width))] * parts,
            scratch_shapes=[pltpu.VMEM((rows, width), bf16)],
        ),
        out_shape=[jax.ShapeDtypeStruct((rows // parts, width), bf16)] * parts,
        compiler_params=pltpu.CompilerParams(vmem_limit_bytes=12 * 2**20),
        cost_estimate=cost(2),
        name="merge",
    )(place_of(stage), *lefts, *rights, *after)


def put_together(refs, out, index, inner):
    size = refs[0].shape[0] // inner
    for shift, ref in enumerate(refs):
        for block in range(inner):
            start = pl.multiple_of((block * len(refs) + (index ^ shift)) * size, 16)
            out[pl.ds(start, size), :] = ref[block * size : (block + 1) * size]


def assemble_kernel(index_ref, *refs, inputs, after, inner):
    put_together(refs[:inputs], refs[inputs + after], index_ref[0], inner)


def assemble(blocks, stage, after=(), through=()):
    rows, width = blocks[0].shape
    full = lambda s: pl.BlockSpec(s, lambda i, j: (0, 0))
    shape = (rows * len(blocks), width)
    first = 1 + len(blocks) + len(after)
    after = list(after) + list(through)
    out = pl.pallas_call(
        functools.partial(assemble_kernel, inputs=len(blocks), after=len(after), inner=stage[4]),
        grid_spec=pltpu.PrefetchScalarGridSpec(
            num_scalar_prefetch=1,
            grid=(1,),
            in_specs=[full((rows, width))] * len(blocks) + [ANY] * len(after),
            out_specs=[full(shape)] + [ANY] * len(through),
        ),
        out_shape=[jax.ShapeDtypeStruct(shape, bf16)] + [jax.ShapeDtypeStruct(a.shape, a.dtype) for a in through],
        input_output_aliases={first + i: 1 + i for i in range(len(through))},
        compiler_params=pltpu.CompilerParams(vmem_limit_bytes=12 * 2**20),
        cost_estimate=cost(1),
        name="assemble",
    )(place_of(stage), *blocks, *after)
    return out[0], out[1:]


def place_kernel(*refs, rows):
    outs = refs[-3:-1]
    refs[-1][...] = jnp.zeros(refs[-1].shape, f32)
    row = pl.program_id(0)
    for number in range(rows):

        @pl.when(row == number)
        def _(number=number):
            for which in range(2):
                outs[which][...] = refs[2 * number + which][...].astype(outs[which].dtype)


def place(sources):
    rows = len(sources)
    count, _, span, width = sources[0][0][0].shape
    shape = (count, rows, span, width)
    in_specs = []
    arrays = []
    for row in sources:
        for sent, at in row:
            in_specs.append(pl.BlockSpec((count, 1, span, width), lambda r, at=at: (0, at, 0, 0)))
            arrays.append(sent)
    out_spec = pl.BlockSpec((count, 1, span, width), lambda r: (0, r, 0, 0))
    layer_out, grad, token = pl.pallas_call(
        functools.partial(place_kernel, rows=rows),
        grid=(rows,),
        in_specs=in_specs,
        out_specs=[out_spec, out_spec, pl.BlockSpec((8, 128), lambda r: (0, 0))],
        out_shape=[jax.ShapeDtypeStruct(shape, bf16), jax.ShapeDtypeStruct(shape, f32), jax.ShapeDtypeStruct((8, 128), f32)],
        compiler_params=pltpu.CompilerParams(vmem_limit_bytes=VMEM_LIMIT),
        cost_estimate=cost(5),
        name="place",
    )(*arrays)
    return layer_out.reshape(count * rows, span, width), grad.reshape(count * rows, span, width), token


def sum_stages(sizes):
    stages = []
    for axis in ("rows", "seq"):
        devices = sizes[axis]
        unit = 1
        while unit < devices:
            size = 2 if unit == 1 and devices.bit_length() % 2 == 0 else 4
            stages.append((axis, devices, unit, size, devices // (unit * size)))
            unit *= size
    return stages


def place_of(stage):
    axis, _, unit, size, _ = stage
    return ((lax.axis_index(axis) // unit) % size).astype(jnp.int32).reshape(1)


def send_parts(parts, stage):
    axis, devices, unit, _, _ = stage
    return exchange(parts, axis, devices, unit)


def cut_for(taken, stage, after=(), through=()):
    return combine(taken, stage[3], stage[4], place_of(stage), after, through)


def add(taken, after=()):
    return combine(taken, 1, 1, jnp.zeros((1,), jnp.int32), after)[0][0]


def unpack_kernel(index_ref, *refs, inputs, after, inner):
    down, up, out, *biases = refs[inputs + after : inputs + after + 10]
    query, key, value, bias_q, bias_v = refs[inputs + after + 10 : -1]
    block = refs[-1]
    put_together(refs[:inputs], block, index_ref[0], inner)
    ff, width = down.shape
    per = ff // width
    down[...] = block[:ff, :width].astype(f32)
    for index in range(per):
        rows = slice(ff + index * width, ff + (index + 1) * width)
        up[:, index * width : (index + 1) * width] = block[rows, :width].astype(f32)
    out[...] = block[2 * ff : 2 * ff + width, :width].astype(f32)
    rows = block[2 * ff + width : 2 * ff + width + 16, :width].astype(f32)
    for index, ref in enumerate(biases[:-1]):
        ref[...] = rows[index]
    biases[-1][...] = jnp.concatenate([rows[len(biases) - 1 + i] for i in range(per)], axis=0)
    per = width // 128
    for number, ref in enumerate((query, key, value)):
        for index in range(per):
            start = (number * per + index) * width
            ref[:, index * 128 : (index + 1) * 128] = block[start : start + width, width:].astype(f32)
    rows = block[3 * per * width : 3 * per * width + 16, width:].astype(f32)
    for number, ref in enumerate((bias_q, bias_v)):
        ref[...] = jnp.concatenate([rows[number * per + i] for i in range(per)], axis=0)


def unpack(blocks, stage, shapes, after=()):
    rows, width = blocks[0].shape
    full = lambda s: pl.BlockSpec(s, lambda i, j: (0,) * len(s))
    return pl.pallas_call(
        functools.partial(unpack_kernel, inputs=len(blocks), after=len(after), inner=stage[4]),
        grid_spec=pltpu.PrefetchScalarGridSpec(
            num_scalar_prefetch=1,
            grid=(1,),
            in_specs=[full((rows, width))] * len(blocks) + [ANY] * len(after),
            out_specs=[full(s) for s in shapes],
            scratch_shapes=[pltpu.VMEM((rows * len(blocks), width), bf16)],
        ),
        out_shape=[jax.ShapeDtypeStruct(s, f32) for s in shapes],
        compiler_params=pltpu.CompilerParams(vmem_limit_bytes=28 * 2**20),
        cost_estimate=cost(4),
        name="unpack",
    )(place_of(stage), *blocks, *after)


def round_up(value, unit):
    return -(-value // unit) * unit


def body(
    tokens, lengths, w_query, b_query, w_key, w_value, b_value, w_out, b_out, gain_attn, shift_attn,
    w_up, b_up, w_down, b_down, gain_ffn, shift_ffn, cotangent, *, sizes,
):
    count = sizes["seq"]
    devices = count * sizes["rows"]
    row_count, span, width = tokens.shape
    ff = w_up.shape[1]
    length = span * count
    rows = row_count // count
    me = lax.axis_index("seq")
    stages = sum_stages(sizes)
    row_stages, seq_stages = [[stage for stage in stages if stage[0] == axis] for axis in ("rows", "seq")]
    first = stages[0]
    index = place_of(first)
    later_rows = round_up(2 * ff + width + 16, 16 * devices)
    first_rows = later_rows

    def split(array):
        return array.reshape(count, rows, 1, span, width)

    def to_owners(parts):
        return lax.all_to_all(parts, "seq", 0, 0, tiled=True)

    parts = [jnp.concatenate([split(tokens)[:, row], split(cotangent)[:, row]], axis=1) for row in range(rows)]
    given = {0: to_owners(parts[0])}

    bounds = lax.dynamic_slice_in_dim(jnp.cumsum(lengths, axis=1), me * rows, rows, 0)
    spots = jnp.arange(length, dtype=jnp.int32)
    segment = jnp.sum((spots[None, None, :] >= bounds[:, :, None]).astype(jnp.int32), axis=1)
    ids = jnp.arange(2 * AUG, dtype=jnp.int32)[None, :, None]
    same = segment[:, None, :] == ids % AUG
    aug = jnp.where(ids < AUG, jnp.where(same, 1.0, 0.0), jnp.where(same | (ids % AUG >= lengths.shape[1]), 0.0, -BIG))
    aug = aug.astype(bf16)

    vectors = [b_query, b_value, b_out, gain_attn, shift_attn, b_down, gain_ffn, shift_ffn]
    vectors = jnp.concatenate([jnp.stack(vectors), b_up.reshape(-1, width)], axis=0)
    (wq_t, wk_t, wv_t, wo_t, wup_t, wdn_t, cols), waiting = prepare(
        (w_query, w_key, w_value, w_out, w_up, w_down), vectors, aug, parts[1:]
    )
    if rows > 1:
        given[1] = to_owners(waiting[0])
    dense_weights = (wo_t, w_out, wup_t, w_up, wdn_t, w_down)
    w_all = jnp.concatenate([w_query, w_key, w_value], axis=1)

    wqkv = (wq_t, wk_t, wv_t)
    last = rows - 1

    def return_pieces(array):
        return lax.all_to_all(array, "seq", 0, 0, tiled=True)

    carried = []
    for row in range(last):
        through = [waiting[row + 1]] if row + 2 < rows else []
        sums, shared, through = whole(
            given[row], row, 2 * last, aug, cols, wqkv, dense_weights + (w_all,), carried, through
        )
        if row + 2 < rows:
            given[row + 2] = to_owners(through[0])
        carried = list(sums) + [shared]
    places = []
    if last:
        moved = return_pieces(shared)
        places = [((moved, 2 * row), (moved, 2 * row + 1)) for row in range(last)]
    shared, saved, later = layer(
        given[last], last, aug, cols, wqkv, dense_weights, (carried[:3] + carried[4:5]) if carried else [],
        later_rows, first[3], first[4], index, [],
    )
    keys, probs, og, delta, gres = saved
    taken = send_parts(later, first)
    ends, early = back(
        shared, keys, probs, og, delta, gres, w_all, (carried[3:4] + carried[5:6]) if carried else [], first_rows,
        first[3], first[4], index, [],
    )
    after = list(early[:1])
    for stage in row_stages[1:]:
        cut, _ = cut_for(taken, stage, after)
        taken = send_parts(cut, stage)
        after = list(cut[:1])
    given_early = send_parts(early, first)
    for stage in row_stages[1:]:
        cut, (ends,) = cut_for(given_early, stage, after, [ends])
        given_early = send_parts(cut, stage)
        after = list(cut[:1])
    ends = return_pieces(ends)
    parts = merge(taken, given_early, seq_stages[0], [moved] if last else [])
    for number, stage in enumerate(seq_stages):
        taken = send_parts(parts, stage)
        if number + 1 < len(seq_stages):
            parts, _ = cut_for(taken, seq_stages[number + 1])
    block = add(taken)
    layer_out, grad_tokens, token = place(places + [((ends, 0), (ends, 1))])
    for number, stage in enumerate(reversed(stages[1:])):
        taken = send_parts([block] * stage[3], stage)
        block, _ = assemble(taken, stage, [token] if number == len(stages) - 2 else [])
    shapes = [(ff, width), (width, ff), (width, width)] + [(width,)] * 6 + [(ff,)] + [(width, width)] * 3 + [(width,)] * 2
    (
        grad_down, grad_up, grad_output, grad_gain2, grad_shift2, grad_dnbias, grad_gain1, grad_shift1, grad_obias,
        grad_upbias, grad_query, grad_key, grad_value, grad_qbias, grad_vbias,
    ) = unpack(send_parts([block] * first[3], first), first, shapes)
    return (
        layer_out, grad_tokens, grad_query, grad_qbias, grad_key, grad_value, grad_vbias, grad_output, grad_obias,
        grad_gain1, grad_shift1, grad_up, grad_upbias, grad_down, grad_dnbias, grad_gain2, grad_shift2,
    )


def solution(mesh):
    split = P("rows", "seq", None)
    in_specs = (split, P("rows", None)) + (P(),) * 15 + (split,)
    out_specs = (split, split) + (P(),) * 15
    sizes = dict(mesh.shape)
    return jax.shard_map(
        functools.partial(body, sizes=sizes), mesh=mesh, in_specs=in_specs, out_specs=out_specs, check_vma=False
    )
```

```python
import functools
import math

import jax
import jax.numpy as jnp
from jax import lax
from jax.experimental import pallas as pl
from jax.experimental.pallas import tpu as pltpu
from jax.sharding import PartitionSpec as P

HEADS = 12
HD = 32
GROUPS = 3
PER_GROUP = HEADS // GROUPS
AUG = 16
BIG = 2.0**100
SMALL_SCORE = 60.0
EPSILON = 1e-05
SCALE = HD ** (-0.5)
LOG2E = math.log2(math.e)
Q_FACTOR = SCALE * LOG2E
LN2 = math.log(2.0)
VMEM_LIMIT = 60 * 2**20

f32 = jnp.float32
bf16 = jnp.bfloat16
NN = (((1,), (0,)), ((), ()))
NT = (((1,), (1,)), ((), ()))
TN = (((0,), (0,)), ((), ()))


def dot(left, right, dims=NN):
    return lax.dot_general(left, right, dims, preferred_element_type=f32)


def fold_lanes(values):
    total = values[:, :128]
    for start in range(128, values.shape[1], 128):
        total = total + values[:, start : start + 128]
    return total


def row_sum(partial):
    return jnp.sum(partial.T, axis=0, keepdims=True)


def normalize(hidden):
    scale = 1.0 / hidden.shape[0]
    centre = hidden - jnp.sum(hidden, axis=0, keepdims=True) * scale
    variance = jnp.sum(centre * centre, axis=0, keepdims=True) * scale
    inverse = lax.rsqrt(variance + EPSILON)
    return centre * inverse, inverse


def normalize_back(upstream, scaled, inverse):
    scale = 1.0 / upstream.shape[0]
    mean = jnp.sum(upstream, axis=0, keepdims=True) * scale
    spread = jnp.sum(upstream * scaled, axis=0, keepdims=True) * scale
    return inverse * (upstream - mean - scaled * spread)


def gelu_parts(v):
    cdf = 0.5 + 0.5 * lax.erf(v * 0.5**0.5)
    bell = jnp.exp2((v * v) * (-0.5 * LOG2E))
    return v * cdf, cdf + v * bell * (2.0 * math.pi) ** (-0.5)


def prepare_kernel(*refs, through):
    sources, rows = refs[:6], refs[6]
    targets, columns = refs[8 + through : 14 + through], refs[14 + through]
    for source, target in zip(sources, targets):
        target[...] = source[...].T
    width = rows.shape[1]
    columns[...] = jnp.concatenate([rows[...], jnp.zeros((128 - rows.shape[0], width), f32)], axis=0).T


def prepare(weights, rows, aug, through):
    full = lambda shape: pl.BlockSpec(shape, lambda i: (0, 0))
    shapes = [w.shape[::-1] for w in weights]
    out = pl.pallas_call(
        functools.partial(prepare_kernel, through=len(through)),
        grid=(1,),
        in_specs=[full(w.shape) for w in weights] + [full(rows.shape)] + [ANY] * (1 + len(through)),
        out_specs=[full(s) for s in shapes] + [full((rows.shape[1], 128))] + [ANY] * len(through),
        out_shape=[jax.ShapeDtypeStruct(s, bf16) for s in shapes]
        + [jax.ShapeDtypeStruct((rows.shape[1], 128), f32)]
        + [jax.ShapeDtypeStruct(a.shape, a.dtype) for a in through],
        input_output_aliases={8 + i: 7 + i for i in range(len(through))},
        compiler_params=pltpu.CompilerParams(vmem_limit_bytes=VMEM_LIMIT),
        cost_estimate=cost(5),
        name="prepare",
    )(*weights, rows, aug, *through)
    return out[:7], out[7:]


def cost(micros):
    return pl.CostEstimate(flops=int(micros * 1e5), transcendentals=0, bytes_accessed=int(micros * 1e3))


B_QUERY, B_VALUE, B_OUT, GAIN1, SHIFT1, B_DOWN, GAIN2, SHIFT2, B_UP = range(9)


ANY = pl.BlockSpec(memory_space=pl.ANY)


def head_sums(values):
    return jnp.sum(values.reshape(HEADS, HD, values.shape[1]), axis=1)


def emit(packed, index, outs, inner):
    size = outs[0].shape[0] // inner
    for shift, ref in enumerate(outs):
        for block in range(inner):
            start = pl.multiple_of((block * len(outs) + (index ^ shift)) * size, 16)
            ref[block * size : (block + 1) * size] = packed[pl.ds(start, size), :]


class Taker:
    def __init__(self, refs):
        self.refs = list(refs)

    def __call__(self, number):
        taken = self.refs[:number]
        del self.refs[:number]
        return taken


def column_of(cols, index):
    return cols[:, index : index + 1]


def project_row(piece_ref, cols, wq, wk, wv, saved, small_ref):
    xt = jnp.concatenate([piece_ref[i, 0].T for i in range(piece_ref.shape[0])], axis=1)
    query = (dot(wq[...], xt) + column_of(cols, B_QUERY)) * Q_FACTOR
    key = dot(wk[...], xt)
    saved[0] = query.astype(bf16)
    saved[1] = key.astype(bf16)
    saved[2] = (dot(wv[...], xt) + column_of(cols, B_VALUE)).astype(bf16)
    saved[3] = xt
    bounds = [
        jnp.max(head_sums(query * query), axis=1, keepdims=True),
        jnp.max(head_sums(key * key), axis=1, keepdims=True),
    ]
    small_ref[0] = (jnp.max(bounds[0] * bounds[1]) < SMALL_SCORE**2).astype(jnp.int32)


def head_rows(group, h):
    return pl.ds(pl.multiple_of((group * PER_GROUP + h) * HD, HD), HD)


def attend_heads(group, saved, aug_ref, probs, att_ref, stat_ref, small_ref):
    length = saved.shape[2]
    ones = jnp.ones((AUG, length), bf16)

    def score(h):
        keys = jnp.concatenate([saved[1, head_rows(group, h), :], aug_ref[0, AUG:]], axis=0)
        query = jnp.concatenate([saved[0, head_rows(group, h), :], aug_ref[0, :AUG]], axis=0)
        return dot(keys, query, TN)

    def mix(h):
        values = jnp.concatenate([saved[2, head_rows(group, h), :], ones], axis=0)
        mixed = dot(values, probs(h)[...])
        inverse = 1.0 / mixed[HD : HD + 1]
        att_ref[head_rows(group, h), :] = mixed[:HD] * inverse
        stat_ref[pl.ds(group * PER_GROUP + h, 1), :] = inverse

    def heads(shifted):
        scores = score(0)
        for h in range(PER_GROUP):
            following = score(h + 1) if h + 1 < PER_GROUP else None
            if h >= 1:
                mix(h - 1)
            if shifted:
                scores = scores - jnp.max(scores, axis=0, keepdims=True)
            probs(h)[...] = jnp.exp2(scores).astype(bf16)
            scores = following
        mix(PER_GROUP - 1)

    @pl.when(small_ref[0] == 1)
    def _():
        heads(False)

    @pl.when(small_ref[0] == 0)
    def _():
        heads(True)


def dense_row(piece_ref, cols, saved, att_ref, stat_ref, weights, sums, carried, arriving, write_out, summed, og_ref, delta_ref, gres_ref):
    wo_t, wo, wup_t, wup, wdn_t, wdn = weights
    acc_dn, acc_up, acc_out = sums
    ff = acc_dn.shape[0]
    width = att_ref.shape[0]

    def column(index):
        return column_of(cols, index)

    def add(number, value):
        ref = sums[number]
        if arriving:
            arriving[number].wait()
        ref[...] = ref[...] + value if carried else value
        summed(number)

    att = att_ref[...]
    att_b = att.astype(bf16)
    res1 = saved[3].astype(f32) + dot(wo_t[...], att_b) + column(B_OUT)
    scaled1, inverse1 = normalize(res1)
    normed = scaled1 * column(GAIN1) + column(SHIFT1)
    normed_b = normed.astype(bf16)
    b_up = jnp.concatenate([column(B_UP + i) for i in range(ff // width)], axis=0)
    act, slope = gelu_parts(dot(wup_t[...], normed_b) + b_up)
    act_b = act.astype(bf16)
    res2 = normed + dot(wdn_t[...], act_b) + column(B_DOWN)
    scaled2, inverse2 = normalize(res2)
    write_out((scaled2 * column(GAIN2) + column(SHIFT2)).astype(bf16))
    cot = jnp.concatenate([piece_ref[i, 1].T for i in range(piece_ref.shape[0])], axis=1).astype(f32)
    gres2 = normalize_back(cot * column(GAIN2), scaled2, inverse2)
    down_b = gres2.astype(bf16)
    up_b = (dot(wdn[...], down_b) * slope).astype(bf16)
    add(0, dot(act_b, down_b, NT))
    gnormed = gres2 + dot(wup[...], up_b)
    add(1, dot(normed_b, up_b, NT))
    gres1 = normalize_back(gnormed * column(GAIN1), scaled1, inverse1)
    gres_ref[...] = gres1
    branch_b = gres1.astype(bf16)
    og = dot(wo[...], branch_b)
    add(2, dot(att_b, branch_b, NT))
    for h in range(HEADS):
        part = slice(h * HD, (h + 1) * HD)
        scaled_og = (og[part] * stat_ref[h : h + 1, :]).astype(bf16)
        og_ref[part, :] = scaled_og
        delta_ref[h : h + 1, :] = jnp.sum(scaled_og.astype(f32) * att[part], axis=0, keepdims=True)
    biases = [cot * scaled2, cot, down_b.astype(f32), gnormed * scaled1, gnormed, branch_b.astype(f32)]
    bias_rows = [row_sum(fold_lanes(value)) for value in biases]
    up_sum = fold_lanes(up_b.astype(f32))
    bias_rows += [row_sum(up_sum[i * width : (i + 1) * width]) for i in range(ff // width)]
    bias_rows.append(jnp.zeros((16 - len(bias_rows), width), f32))
    return jnp.concatenate(bias_rows, axis=0)


def back_heads(group, saved, og_ref, delta_ref, probs, grads, held):
    length = og_ref.shape[1]
    width = og_ref.shape[0]
    sign = jnp.where(lax.broadcasted_iota(jnp.int32, (AUG, length), 0) < 3, 1.0, 0.0).astype(bf16)

    def grad_probs(h):
        delta = delta_ref[pl.ds(group * PER_GROUP + h, 1), :]
        first = delta.astype(bf16)
        rest = delta - first.astype(f32)
        second = rest.astype(bf16)
        third = (rest - second.astype(f32)).astype(bf16)
        aug = jnp.concatenate(
            [-first.astype(f32), -second.astype(f32), -third.astype(f32), jnp.zeros((AUG - 3, length), f32)], axis=0
        ).astype(bf16)
        left = jnp.concatenate([saved[2, head_rows(group, h), :], sign], axis=0)
        right = jnp.concatenate([og_ref[head_rows(group, h), :], aug], axis=0)
        return dot(left, right, TN)

    def target(which, h):
        return pl.ds(pl.multiple_of(which * width + (group * PER_GROUP + h) * HD, HD), HD)

    for h in range(PER_GROUP):
        held[h] = (probs(h)[...].astype(f32) * grad_probs(h)).astype(bf16)
        grads[target(2, h), :] = dot(og_ref[head_rows(group, h), :], probs(h)[...], NT).astype(bf16)
    for h in range(PER_GROUP):
        grads[target(0, h), :] = (dot(saved[1, head_rows(group, h), :], held[h]) * SCALE).astype(bf16)
        grads[target(1, h), :] = (dot(saved[0, head_rows(group, h), :], held[h], NT) * LN2).astype(bf16)


def back_biases(total, width):
    rows = [row_sum(fold_lanes(part.astype(f32))) for part in (total[:width], total[2 * width :])]
    return jnp.concatenate(rows + [jnp.zeros((6, width), f32)], axis=0)


def write_pieces(values, ref, at=0):
    span = ref.shape[2]
    for piece in range(ref.shape[0]):
        ref[piece, at] = values[:, piece * span : (piece + 1) * span].T


def copies_of(sources, targets, sem):
    return [pltpu.make_async_copy(a, b, sem.at[i]) for i, (a, b) in enumerate(zip(sources, targets))]


def whole_kernel(*refs, carried, through):
    take = Taker(refs)
    (piece_ref,) = take(1)
    aug_ref, cols, wq, wk, wv = take(5)
    weights_hbm = take(7)
    sums_hbm = take(4 if carried else 0)
    bias_in = take(2 if carried else 0)
    take((1 if carried else 0) + through)
    (out_ref,) = take(1)
    sums_out = take(4)
    bias_out = take(2)
    take(through)
    saved, p_all, att_ref, stat_ref, og_ref, delta_ref, gres_ref, grads, held = take(9)
    weights = take(7)
    sums = take(4)
    small_ref, weight_sem, sum_sem, out_sem = take(4)
    step = pl.program_id(0)
    width = att_ref.shape[0]
    weight_copies = copies_of(weights_hbm, weights, weight_sem)
    sum_copies = copies_of(sums_hbm, sums, sum_sem)
    out_copies = copies_of(sums, sums_out, out_sem)

    @pl.when(step == 0)
    def _():
        for copy in weight_copies + sum_copies:
            copy.start()
        project_row(piece_ref, cols, wq, wk, wv, saved, small_ref)

    @pl.when(step < GROUPS)
    def _():
        attend_heads(step, saved, aug_ref, lambda h: p_all.at[step * PER_GROUP + h], att_ref, stat_ref, small_ref)

    @pl.when(step == GROUPS - 1)
    def _():
        for copy in weight_copies[:6] + sum_copies[:3]:
            copy.wait()
        total = dense_row(
            piece_ref, cols, saved, att_ref, stat_ref, weights[:6], sums[:3], carried, [],
            lambda values: write_pieces(values, out_ref, 0), lambda number: out_copies[number].start(),
            og_ref, delta_ref, gres_ref,
        )
        bias_out[0][...] = total + bias_in[0][...] if carried else total

    @pl.when(step >= GROUPS)
    def _():
        group = step - GROUPS
        back_heads(group, saved, og_ref, delta_ref, lambda h: p_all.at[group * PER_GROUP + h], grads, held)

    @pl.when(step == 2 * GROUPS - 1)
    def _():
        for copy in weight_copies[6:] + sum_copies[3:]:
            copy.wait()
        total = grads[...]
        acc = dot(saved[3], total, NT)
        sums[3][...] = sums[3][...] + acc if carried else acc
        out_copies[3].start()
        bias = back_biases(total, width)
        bias_out[1][...] = bias + bias_in[1][...] if carried else bias
        result = (gres_ref[...] + dot(weights[6][...], total)).astype(bf16)
        write_pieces(result, out_ref, 1)
        for copy in out_copies:
            copy.wait()


def whole(pieces, row, height, aug, cols, wqkv, weights, carried, through):
    count, _, span, width = pieces.shape
    length = span * count
    ff = weights[3].shape[1]
    full = lambda shape: pl.BlockSpec(shape, lambda g: (0,) * len(shape))
    sum_shapes = [(ff, width), (width, ff), (width, width), (width, 3 * width)]
    bias_shapes = [(16, width), (8, width)]
    first = 1 + 5 + 7 + len(carried)
    aliases = {first + i: 7 + i for i in range(len(through))}
    out = pl.pallas_call(
        functools.partial(whole_kernel, carried=bool(carried), through=len(through)),
        grid=(2 * GROUPS,),
        in_specs=[full(pieces.shape)]
        + [pl.BlockSpec((1, 2 * AUG, length), lambda g: (row, 0, 0)), full(cols.shape)]
        + [full(w.shape) for w in wqkv]
        + [ANY] * 7
        + ([ANY] * 4 + [full(s) for s in bias_shapes] + [ANY] if carried else [])
        + [ANY] * len(through),
        out_specs=[pl.BlockSpec((count, 2, span, width), lambda g: (0, row, 0, 0))]
        + [ANY] * 4
        + [full(s) for s in bias_shapes]
        + [ANY] * len(through),
        scratch_shapes=[
            pltpu.VMEM((4, width, length), bf16),
            pltpu.VMEM((HEADS, length, length), bf16),
            pltpu.VMEM((width, length), f32),
            pltpu.VMEM((16, length), f32),
            pltpu.VMEM((width, length), bf16),
            pltpu.VMEM((16, length), f32),
            pltpu.VMEM((width, length), f32),
            pltpu.VMEM((3 * width, length), bf16),
            pltpu.VMEM((PER_GROUP, length, length), bf16),
        ]
        + [pltpu.VMEM(w.shape, bf16) for w in weights]
        + [pltpu.VMEM(s, f32) for s in sum_shapes]
        + [
            pltpu.SMEM((1,), jnp.int32),
            pltpu.SemaphoreType.DMA((7,)),
            pltpu.SemaphoreType.DMA((4,)),
            pltpu.SemaphoreType.DMA((4,)),
        ],
        out_shape=[jax.ShapeDtypeStruct((count, height, span, width), bf16)]
        + [jax.ShapeDtypeStruct(s, f32) for s in sum_shapes + bias_shapes]
        + [jax.ShapeDtypeStruct(a.shape, a.dtype) for a in through],
        input_output_aliases={first - 1: 0, **aliases} if carried else aliases,
        compiler_params=pltpu.CompilerParams(vmem_limit_bytes=VMEM_LIMIT),
        cost_estimate=cost(20),
        name="whole",
    )(pieces, aug, cols, *wqkv, *weights, *carried, *through)
    return out[1:7], out[0], out[7:]


def layer_kernel(index_ref, *refs, carried, after, parts, inner):
    take = Taker(refs)
    (piece_ref,) = take(1)
    aug_ref, cols, wq, wk, wv = take(5)
    weights_hbm = take(6)
    sums_hbm = take(3 if carried else 0)
    bias_in = take(1 if carried else 0)
    take(after)
    (out_ref,) = take(1)
    saved_hbm, p_hbm, og_ref, delta_ref, gres_ref = take(5)
    part_refs = take(parts)
    saved, p_buf, att_ref, stat_ref = take(4)
    weights = take(6)
    sums = take(3)
    packed, small_ref, weight_sem, sum_sem, p_sem, saved_sem, part_sem = take(7)
    group = pl.program_id(0)
    width = att_ref.shape[0]
    weight_copies = copies_of(weights_hbm, weights, weight_sem)
    sum_copies = copies_of(sums_hbm, sums, sum_sem)
    saved_copy = pltpu.make_async_copy(saved, saved_hbm, saved_sem)
    slot = lax.rem(group, 2)

    def p_copy(number):
        start = number * PER_GROUP
        return pltpu.make_async_copy(
            p_buf.at[lax.rem(number, 2)], p_hbm.at[pl.ds(start, PER_GROUP)], p_sem.at[lax.rem(number, 2)]
        )

    @pl.when(group == 0)
    def _():
        for copy in weight_copies + sum_copies:
            copy.start()
        project_row(piece_ref, cols, wq, wk, wv, saved, small_ref)
        saved_copy.start()

    @pl.when(group >= 2)
    def _():
        p_copy(group - 2).wait()

    attend_heads(group, saved, aug_ref, lambda h: p_buf.at[slot, h], att_ref, stat_ref, small_ref)
    p_copy(group).start()

    @pl.when(group == GROUPS - 1)
    def _():
        for copy in weight_copies:
            copy.wait()
        acc_dn, acc_up, acc_out = sums
        ff = acc_dn.shape[0]
        size = part_refs[0].shape[0] // inner
        part_copies = []

        def send(number):
            for shift, ref in enumerate(part_refs):
                start = pl.multiple_of((number * parts + (index_ref[0] ^ shift)) * size, 16)
                copy = pltpu.make_async_copy(
                    packed.at[pl.ds(start, size)], ref.at[pl.ds(number * size, size)], part_sem.at[shift * inner + number]
                )
                copy.start()
                part_copies.append(copy)

        def blocks_until(done):
            return done // (parts * size)

        def pack(number):
            if number == 0:
                packed[:ff] = acc_dn[...].astype(bf16)
                ready = range(blocks_until(ff))
            elif number == 1:
                for index in range(ff // width):
                    packed[ff + index * width : ff + (index + 1) * width] = acc_up[
                        :, index * width : (index + 1) * width
                    ].astype(bf16)
                ready = range(blocks_until(ff), blocks_until(2 * ff))
            else:
                packed[2 * ff : 2 * ff + width] = acc_out[...].astype(bf16)
                ready = []
            for block in ready:
                send(block)

        total = dense_row(
            piece_ref, cols, saved, att_ref, stat_ref, weights, sums, carried, sum_copies,
            lambda values: write_pieces(values, out_ref), pack, og_ref, delta_ref, gres_ref,
        )
        if carried:
            total = total + bias_in[0][...]
        packed[2 * ff + width : 2 * ff + width + 16] = total.astype(bf16)
        rest = packed.shape[0] - 2 * ff - width - 16
        if rest:
            packed[2 * ff + width + 16 :] = jnp.zeros((rest, width), bf16)
        for number in range(blocks_until(2 * ff), inner):
            send(number)
        for copy in part_copies:
            copy.wait()
        saved_copy.wait()
        for number in range(max(GROUPS - 2, 0), GROUPS):
            p_copy(number).wait()


def layer(pieces, row, aug, cols, wqkv, weights, sums, packed_rows, parts, inner, index, after):
    count, _, span, width = pieces.shape
    length = span * count
    ff = weights[3].shape[1]
    full = lambda shape: pl.BlockSpec(shape, lambda g, i: (0,) * len(shape))
    sum_shapes = [(ff, width), (width, ff), (width, width)]
    part = (packed_rows // parts, width)
    out = pl.pallas_call(
        functools.partial(
            layer_kernel, carried=bool(sums), after=len(after), parts=parts, inner=inner
        ),
        grid_spec=pltpu.PrefetchScalarGridSpec(
            num_scalar_prefetch=1,
            grid=(GROUPS,),
            in_specs=[full(pieces.shape)]
            + [pl.BlockSpec((1, 2 * AUG, length), lambda g, i: (row, 0, 0)), full(cols.shape)]
            + [full(w.shape) for w in wqkv]
            + [ANY] * 6
            + ([ANY] * 3 + [full((16, width))] if sums else [])
            + [ANY] * len(after),
            out_specs=[pl.BlockSpec((count, 1, span, width), lambda g, i: (0, 0, 0, 0))]
            + [ANY, ANY, full((width, length)), full((16, length)), full((width, length))]
            + [ANY] * parts,
            scratch_shapes=[
                pltpu.VMEM((4, width, length), bf16),
                pltpu.VMEM((2, PER_GROUP, length, length), bf16),
                pltpu.VMEM((width, length), f32),
                pltpu.VMEM((16, length), f32),
            ]
            + [pltpu.VMEM(w.shape, bf16) for w in weights]
            + [pltpu.VMEM(shape, f32) for shape in sum_shapes]
            + [
                pltpu.VMEM((packed_rows, width), bf16),
                pltpu.SMEM((1,), jnp.int32),
                pltpu.SemaphoreType.DMA((6,)),
                pltpu.SemaphoreType.DMA((3,)),
                pltpu.SemaphoreType.DMA((2,)),
                pltpu.SemaphoreType.DMA,
                pltpu.SemaphoreType.DMA((parts * inner,)),
            ],
        ),
        out_shape=[jax.ShapeDtypeStruct((count, 2, span, width), bf16)]
        + [
            jax.ShapeDtypeStruct((4, width, length), bf16),
            jax.ShapeDtypeStruct((HEADS, length, length), bf16),
            jax.ShapeDtypeStruct((width, length), bf16),
            jax.ShapeDtypeStruct((16, length), f32),
            jax.ShapeDtypeStruct((width, length), f32),
        ]
        + [jax.ShapeDtypeStruct(part, bf16)] * parts,
        compiler_params=pltpu.CompilerParams(vmem_limit_bytes=VMEM_LIMIT),
        cost_estimate=cost(14),
        name="layer",
    )(index, pieces, aug, cols, *wqkv, *weights, *sums, *after)
    return out[0], out[1:6], out[6:]


def back_kernel(index_ref, *refs, carried, after, parts, inner):
    take = Taker(refs)
    saved, og_ref, delta_ref, p_ref, saved_hbm, gres_hbm, w_hbm = take(7)
    sum_hbm = take(1 if carried else 0)
    bias_in = take(1 if carried else 0)
    take(after)
    (out_ref,) = take(1)
    part_refs = take(parts)
    grads, held, xt, gres, w_all = take(5)
    sum_in = take(1 if carried else 0)
    packed, sem = take(2)
    group = pl.program_id(0)
    width = og_ref.shape[0]
    copies = copies_of([saved_hbm.at[3], gres_hbm, w_hbm] + sum_hbm, [xt, gres, w_all] + sum_in, sem)

    @pl.when(group == 0)
    def _():
        for copy in copies:
            copy.start()

    back_heads(group, saved, og_ref, delta_ref, lambda h: p_ref.at[h], grads, held)

    @pl.when(group == GROUPS - 1)
    def _():
        for copy in copies:
            copy.wait()
        total = grads[...]
        acc = dot(xt[...], total, NT)
        bias = back_biases(total, width)
        if carried:
            acc = acc + sum_in[0][...]
            bias = bias + bias_in[0][...]
        per = width // 128
        for index in range(3 * per):
            packed[index * width : (index + 1) * width] = acc[:, index * 128 : (index + 1) * 128].astype(bf16)
        bias_rows = [bias[n : n + 1, i * 128 : (i + 1) * 128] for n in range(2) for i in range(per)]
        tail = packed.shape[0] - 3 * per * width
        bias_rows.append(jnp.zeros((tail - len(bias_rows), 128), f32))
        packed[3 * per * width :] = jnp.concatenate(bias_rows, axis=0).astype(bf16)
        emit(packed, index_ref[0], part_refs, inner)
        write_pieces((gres[...] + dot(w_all[...], total)).astype(bf16), out_ref)


def back(shared, saved, probs, og, delta, gres, w_all, sums, packed_rows, parts, inner, index, after):
    _, width, length = saved.shape
    count, _, span, _ = shared.shape
    first = 1 + 7 + len(sums)
    after = [shared] + list(after)
    full = lambda shape: pl.BlockSpec(shape, lambda g, i: (0,) * len(shape))
    part = (packed_rows // parts, 128)
    out = pl.pallas_call(
        functools.partial(back_kernel, carried=bool(sums), after=len(after), parts=parts, inner=inner),
        grid_spec=pltpu.PrefetchScalarGridSpec(
            num_scalar_prefetch=1,
            grid=(GROUPS,),
            in_specs=[
                full((3, width, length)),
                full((width, length)),
                full((16, length)),
                pl.BlockSpec((PER_GROUP, length, length), lambda g, i: (g, 0, 0)),
            ]
            + [ANY] * 3
            + ([ANY, full((8, width))] if sums else [])
            + [ANY] * len(after),
            out_specs=[pl.BlockSpec((count, 1, span, width), lambda g, i: (0, 1, 0, 0))] + [full(part)] * parts,
            scratch_shapes=[
                pltpu.VMEM((3 * width, length), bf16),
                pltpu.VMEM((PER_GROUP, length, length), bf16),
                pltpu.VMEM((width, length), bf16),
                pltpu.VMEM((width, length), f32),
                pltpu.VMEM(w_all.shape, bf16),
            ]
            + ([pltpu.VMEM((width, 3 * width), f32)] if sums else [])
            + [pltpu.VMEM((packed_rows, 128), bf16), pltpu.SemaphoreType.DMA((4,))],
        ),
        out_shape=[jax.ShapeDtypeStruct((count, 2, span, width), bf16)] + [jax.ShapeDtypeStruct(part, bf16)] * parts,
        input_output_aliases={first: 0},
        compiler_params=pltpu.CompilerParams(vmem_limit_bytes=VMEM_LIMIT),
        cost_estimate=cost(9),
        name="back",
    )(index, saved, og, delta, probs, saved, gres, w_all, *sums, *after)
    return out[0], out[1:]


def exchange(pieces, axis, devices, unit=1):
    moved = [pieces[0]]
    for shift in range(1, len(pieces)):
        moved.append(lax.ppermute(pieces[shift], axis, [(i, i ^ (shift * unit)) for i in range(devices)]))
    return moved


def tree_sum(blocks):
    while len(blocks) > 1:
        blocks = [left + right for left, right in zip(blocks[::2], blocks[1::2])]
    return blocks[0]


def combine_kernel(index_ref, *refs, inputs, after, through, parts, inner):
    total = tree_sum([ref[...].astype(f32) for ref in refs[:inputs]]).astype(bf16)
    refs = refs[inputs + after + through :]
    outs = refs[:parts]
    if parts == 1:
        outs[0][...] = total
    else:
        packed = refs[-1]
        packed[...] = total
        emit(packed, index_ref[0], outs, inner)


def combine(blocks, parts, inner, index, after=(), through=()):
    rows, width = blocks[0].shape
    part = (rows // parts, width)
    first = 1 + len(blocks) + len(after)
    full = lambda s: pl.BlockSpec(s, lambda i, j: (0, 0))
    out = pl.pallas_call(
        functools.partial(
            combine_kernel, inputs=len(blocks), after=len(after), through=len(through), parts=parts, inner=inner
        ),
        grid_spec=pltpu.PrefetchScalarGridSpec(
            num_scalar_prefetch=1,
            grid=(1,),
            in_specs=[full((rows, width))] * len(blocks) + [ANY] * (len(after) + len(through)),
            out_specs=[full(part)] * parts + [ANY] * len(through),
            scratch_shapes=[pltpu.VMEM((rows, width), bf16)] if parts > 1 else [],
        ),
        out_shape=[jax.ShapeDtypeStruct(part, bf16)] * parts
        + [jax.ShapeDtypeStruct(a.shape, a.dtype) for a in through],
        input_output_aliases={first + i: parts + i for i in range(len(through))},
        compiler_params=pltpu.CompilerParams(vmem_limit_bytes=20 * 2**20),
        cost_estimate=cost(1),
        name="combine",
    )(index, *blocks, *after, *through)
    return out[:parts], out[parts:]


def merge_kernel(index_ref, *refs, count, after, parts, inner):
    left = tree_sum([ref[...].astype(f32) for ref in refs[:count]])
    right = tree_sum([ref[...].astype(f32) for ref in refs[count : 2 * count]])
    packed = refs[-1]
    packed[...] = jnp.concatenate([left, right], axis=1).astype(bf16)
    emit(packed, index_ref[0], refs[2 * count + after : -1], inner)


def merge(lefts, rights, stage, after=()):
    rows, left = lefts[0].shape
    width = left + rights[0].shape[1]
    parts = stage[3]
    full = lambda s: pl.BlockSpec(s, lambda i, j: (0, 0))
    return pl.pallas_call(
        functools.partial(merge_kernel, count=len(lefts), after=len(after), parts=parts, inner=stage[4]),
        grid_spec=pltpu.PrefetchScalarGridSpec(
            num_scalar_prefetch=1,
            grid=(1,),
            in_specs=[full(b.shape) for b in list(lefts) + list(rights)] + [ANY] * len(after),
            out_specs=[full((rows // parts, width))] * parts,
            scratch_shapes=[pltpu.VMEM((rows, width), bf16)],
        ),
        out_shape=[jax.ShapeDtypeStruct((rows // parts, width), bf16)] * parts,
        compiler_params=pltpu.CompilerParams(vmem_limit_bytes=12 * 2**20),
        cost_estimate=cost(2),
        name="merge",
    )(place_of(stage), *lefts, *rights, *after)


def put_together(refs, out, index, inner):
    size = refs[0].shape[0] // inner
    for shift, ref in enumerate(refs):
        for block in range(inner):
            start = pl.multiple_of((block * len(refs) + (index ^ shift)) * size, 16)
            out[pl.ds(start, size), :] = ref[block * size : (block + 1) * size]


def assemble_kernel(index_ref, *refs, inputs, after, inner):
    put_together(refs[:inputs], refs[inputs + after], index_ref[0], inner)


def assemble(blocks, stage, after=(), through=()):
    rows, width = blocks[0].shape
    full = lambda s: pl.BlockSpec(s, lambda i, j: (0, 0))
    shape = (rows * len(blocks), width)
    first = 1 + len(blocks) + len(after)
    after = list(after) + list(through)
    out = pl.pallas_call(
        functools.partial(assemble_kernel, inputs=len(blocks), after=len(after), inner=stage[4]),
        grid_spec=pltpu.PrefetchScalarGridSpec(
            num_scalar_prefetch=1,
            grid=(1,),
            in_specs=[full((rows, width))] * len(blocks) + [ANY] * len(after),
            out_specs=[full(shape)] + [ANY] * len(through),
        ),
        out_shape=[jax.ShapeDtypeStruct(shape, bf16)] + [jax.ShapeDtypeStruct(a.shape, a.dtype) for a in through],
        input_output_aliases={first + i: 1 + i for i in range(len(through))},
        compiler_params=pltpu.CompilerParams(vmem_limit_bytes=12 * 2**20),
        cost_estimate=cost(1),
        name="assemble",
    )(place_of(stage), *blocks, *after)
    return out[0], out[1:]


def place_kernel(*refs, rows):
    outs = refs[-3:-1]
    refs[-1][...] = jnp.zeros(refs[-1].shape, f32)
    row = pl.program_id(0)
    for number in range(rows):

        @pl.when(row == number)
        def _(number=number):
            for which in range(2):
                outs[which][...] = refs[2 * number + which][...].astype(outs[which].dtype)


def place(sources):
    rows = len(sources)
    count, _, span, width = sources[0][0][0].shape
    shape = (count, rows, span, width)
    in_specs = []
    arrays = []
    for row in sources:
        for sent, at in row:
            in_specs.append(pl.BlockSpec((count, 1, span, width), lambda r, at=at: (0, at, 0, 0)))
            arrays.append(sent)
    out_spec = pl.BlockSpec((count, 1, span, width), lambda r: (0, r, 0, 0))
    layer_out, grad, token = pl.pallas_call(
        functools.partial(place_kernel, rows=rows),
        grid=(rows,),
        in_specs=in_specs,
        out_specs=[out_spec, out_spec, pl.BlockSpec((8, 128), lambda r: (0, 0))],
        out_shape=[jax.ShapeDtypeStruct(shape, bf16), jax.ShapeDtypeStruct(shape, f32), jax.ShapeDtypeStruct((8, 128), f32)],
        compiler_params=pltpu.CompilerParams(vmem_limit_bytes=VMEM_LIMIT),
        cost_estimate=cost(5),
        name="place",
    )(*arrays)
    return layer_out.reshape(count * rows, span, width), grad.reshape(count * rows, span, width), token


def sum_stages(sizes):
    stages = []
    for axis in ("rows", "seq"):
        devices = sizes[axis]
        unit = 1
        while unit < devices:
            size = 2 if unit == 1 and devices.bit_length() % 2 == 0 else 4
            stages.append((axis, devices, unit, size, devices // (unit * size)))
            unit *= size
    return stages


def place_of(stage):
    axis, _, unit, size, _ = stage
    return ((lax.axis_index(axis) // unit) % size).astype(jnp.int32).reshape(1)


def send_parts(parts, stage):
    axis, devices, unit, _, _ = stage
    return exchange(parts, axis, devices, unit)


def cut_for(taken, stage, after=(), through=()):
    return combine(taken, stage[3], stage[4], place_of(stage), after, through)


def add(taken, after=()):
    return combine(taken, 1, 1, jnp.zeros((1,), jnp.int32), after)[0][0]


def unpack_kernel(index_ref, *refs, inputs, after, inner):
    down, up, out, *biases = refs[inputs + after : inputs + after + 10]
    query, key, value, bias_q, bias_v = refs[inputs + after + 10 : -1]
    block = refs[-1]
    put_together(refs[:inputs], block, index_ref[0], inner)
    ff, width = down.shape
    per = ff // width
    down[...] = block[:ff, :width].astype(f32)
    for index in range(per):
        rows = slice(ff + index * width, ff + (index + 1) * width)
        up[:, index * width : (index + 1) * width] = block[rows, :width].astype(f32)
    out[...] = block[2 * ff : 2 * ff + width, :width].astype(f32)
    rows = block[2 * ff + width : 2 * ff + width + 16, :width].astype(f32)
    for index, ref in enumerate(biases[:-1]):
        ref[...] = rows[index]
    biases[-1][...] = jnp.concatenate([rows[len(biases) - 1 + i] for i in range(per)], axis=0)
    per = width // 128
    for number, ref in enumerate((query, key, value)):
        for index in range(per):
            start = (number * per + index) * width
            ref[:, index * 128 : (index + 1) * 128] = block[start : start + width, width:].astype(f32)
    rows = block[3 * per * width : 3 * per * width + 16, width:].astype(f32)
    for number, ref in enumerate((bias_q, bias_v)):
        ref[...] = jnp.concatenate([rows[number * per + i] for i in range(per)], axis=0)


def unpack(blocks, stage, shapes, after=()):
    rows, width = blocks[0].shape
    full = lambda s: pl.BlockSpec(s, lambda i, j: (0,) * len(s))
    return pl.pallas_call(
        functools.partial(unpack_kernel, inputs=len(blocks), after=len(after), inner=stage[4]),
        grid_spec=pltpu.PrefetchScalarGridSpec(
            num_scalar_prefetch=1,
            grid=(1,),
            in_specs=[full((rows, width))] * len(blocks) + [ANY] * len(after),
            out_specs=[full(s) for s in shapes],
            scratch_shapes=[pltpu.VMEM((rows * len(blocks), width), bf16)],
        ),
        out_shape=[jax.ShapeDtypeStruct(s, f32) for s in shapes],
        compiler_params=pltpu.CompilerParams(vmem_limit_bytes=28 * 2**20),
        cost_estimate=cost(4),
        name="unpack",
    )(place_of(stage), *blocks, *after)


def round_up(value, unit):
    return -(-value // unit) * unit


def body(
    tokens, lengths, w_query, b_query, w_key, w_value, b_value, w_out, b_out, gain_attn, shift_attn,
    w_up, b_up, w_down, b_down, gain_ffn, shift_ffn, cotangent, *, sizes,
):
    count = sizes["seq"]
    devices = count * sizes["rows"]
    row_count, span, width = tokens.shape
    ff = w_up.shape[1]
    length = span * count
    rows = row_count // count
    me = lax.axis_index("seq")
    stages = sum_stages(sizes)
    row_stages, seq_stages = [[stage for stage in stages if stage[0] == axis] for axis in ("rows", "seq")]
    first = stages[0]
    index = place_of(first)
    later_rows = round_up(2 * ff + width + 16, 16 * devices)
    first_rows = later_rows

    def split(array):
        return array.reshape(count, rows, 1, span, width)

    def to_owners(parts):
        return lax.all_to_all(parts, "seq", 0, 0, tiled=True)

    parts = [jnp.concatenate([split(tokens)[:, row], split(cotangent)[:, row]], axis=1) for row in range(rows)]
    given = {0: to_owners(parts[0])}

    bounds = lax.dynamic_slice_in_dim(jnp.cumsum(lengths, axis=1), me * rows, rows, 0)
    spots = jnp.arange(length, dtype=jnp.int32)
    segment = jnp.sum((spots[None, None, :] >= bounds[:, :, None]).astype(jnp.int32), axis=1)
    ids = jnp.arange(2 * AUG, dtype=jnp.int32)[None, :, None]
    same = segment[:, None, :] == ids % AUG
    aug = jnp.where(ids < AUG, jnp.where(same, 1.0, 0.0), jnp.where(same | (ids % AUG >= lengths.shape[1]), 0.0, -BIG))
    aug = aug.astype(bf16)

    vectors = [b_query, b_value, b_out, gain_attn, shift_attn, b_down, gain_ffn, shift_ffn]
    vectors = jnp.concatenate([jnp.stack(vectors), b_up.reshape(-1, width)], axis=0)
    (wq_t, wk_t, wv_t, wo_t, wup_t, wdn_t, cols), waiting = prepare(
        (w_query, w_key, w_value, w_out, w_up, w_down), vectors, aug, parts[1:]
    )
    if rows > 1:
        given[1] = to_owners(waiting[0])
    dense_weights = (wo_t, w_out, wup_t, w_up, wdn_t, w_down)
    w_all = jnp.concatenate([w_query, w_key, w_value], axis=1)

    wqkv = (wq_t, wk_t, wv_t)
    last = rows - 1

    def return_pieces(array):
        return lax.all_to_all(array, "seq", 0, 0, tiled=True)

    carried = []
    for row in range(last):
        through = [waiting[row + 1]] if row + 2 < rows else []
        sums, shared, through = whole(
            given[row], row, 2 * last, aug, cols, wqkv, dense_weights + (w_all,), carried, through
        )
        if row + 2 < rows:
            given[row + 2] = to_owners(through[0])
        carried = list(sums) + [shared]
    places = []
    if last:
        moved = return_pieces(shared)
        places = [((moved, 2 * row), (moved, 2 * row + 1)) for row in range(last)]
    shared, saved, later = layer(
        given[last], last, aug, cols, wqkv, dense_weights, (carried[:3] + carried[4:5]) if carried else [],
        later_rows, first[3], first[4], index, [],
    )
    keys, probs, og, delta, gres = saved
    taken = send_parts(later, first)
    ends, early = back(
        shared, keys, probs, og, delta, gres, w_all, (carried[3:4] + carried[5:6]) if carried else [], first_rows,
        first[3], first[4], index, [],
    )
    after = list(early[:1])
    for stage in row_stages[1:]:
        cut, _ = cut_for(taken, stage, after)
        taken = send_parts(cut, stage)
        after = list(cut[:1])
    given_early = send_parts(early, first)
    for stage in row_stages[1:]:
        cut, (ends,) = cut_for(given_early, stage, after, [ends])
        given_early = send_parts(cut, stage)
        after = list(cut[:1])
    ends = return_pieces(ends)
    parts = merge(taken, given_early, seq_stages[0], [moved] if last else [])
    for number, stage in enumerate(seq_stages):
        taken = send_parts(parts, stage)
        if number + 1 < len(seq_stages):
            parts, _ = cut_for(taken, seq_stages[number + 1])
    block = add(taken)
    layer_out, grad_tokens, token = place(places + [((ends, 0), (ends, 1))])
    for number, stage in enumerate(reversed(stages[1:])):
        taken = send_parts([block] * stage[3], stage)
        block, _ = assemble(taken, stage, [token] if number == len(stages) - 2 else [])
    shapes = [(ff, width), (width, ff), (width, width)] + [(width,)] * 6 + [(ff,)] + [(width, width)] * 3 + [(width,)] * 2
    (
        grad_down, grad_up, grad_output, grad_gain2, grad_shift2, grad_dnbias, grad_gain1, grad_shift1, grad_obias,
        grad_upbias, grad_query, grad_key, grad_value, grad_qbias, grad_vbias,
    ) = unpack(send_parts([block] * first[3], first), first, shapes)
    return (
        layer_out, grad_tokens, grad_query, grad_qbias, grad_key, grad_value, grad_vbias, grad_output, grad_obias,
        grad_gain1, grad_shift1, grad_up, grad_upbias, grad_down, grad_dnbias, grad_gain2, grad_shift2,
    )


def solution(mesh):
    split = P("rows", "seq", None)
    in_specs = (split, P("rows", None)) + (P(),) * 15 + (split,)
    out_specs = (split, split) + (P(),) * 15
    sizes = dict(mesh.shape)
    return jax.shard_map(
        functools.partial(body, sizes=sizes), mesh=mesh, in_specs=in_specs, out_specs=out_specs, check_vma=False
    )
```
